32 devices in a mesh: fsdp: 2 (over y), ctx: 4 (over z), tp: 4 (over x, core).
Axes of the slice: x: 2, y: 2, z: 4, core: 2. Of those that a mesh axis runs over, the one named last changes fastest.
Arguments:
- tokens: bfloat16 [4096, 1024], P(('fsdp', 'ctx')), may hold values from -6 to 6
- cotangent: bfloat16 [4096, 1024], P(('fsdp', 'ctx')), may hold values from -6 to 6
- block_place: int32 [2, 16], P('fsdp'), may hold values from 0 to 15, each once within a row
- segment_ids: int32 [2, 2048], P('fsdp'), may hold values from -1 to 3, as said below
- qkv_weight: bfloat16 [2, 1024, 3, 1024], P(None, ('fsdp', 'ctx'), None, 'tp'), may hold values from -0.1875 to 0.1875
- out_weight: bfloat16 [2, 1024, 1024], P(None, ('fsdp', 'ctx'), 'tp'), may hold values from -0.5 to 0.5
- up_weight: bfloat16 [2, 1024, 4096], P(None, ('fsdp', 'ctx'), 'tp'), may hold values from -0.1875 to 0.1875
- down_weight: bfloat16 [2, 1024, 4096], P(None, ('fsdp', 'ctx'), 'tp'), may hold values from -0.09375 to 0.09375
- query_value_bias: bfloat16 [2, 2, 1024], P(None, None, 'tp'), may hold values from -3 to 3
- up_bias: bfloat16 [2, 4096], P(None, 'tp'), may hold values from -3 to 3
- norm_gains: bfloat16 [2, 1024, 2], P(None, ('fsdp', 'ctx')), may hold values from 0.099609375 to 1.8984375
- row_biases: bfloat16 [2, 1024, 4], P(None, ('fsdp', 'ctx')), may hold values from -3 to 3
Outputs:
- block_output: bfloat16 [4096, 1024], P(('fsdp', 'ctx'))
- grad_tokens: float32 [4096, 1024], P(('fsdp', 'ctx'))
- grad_qkv_weight: float32 [2, 1024, 3, 1024], P(None, ('fsdp', 'ctx'), None, 'tp')
- grad_out_weight: float32 [2, 1024, 1024], P(None, ('fsdp', 'ctx'), 'tp')
- grad_up_weight: float32 [2, 1024, 4096], P(None, ('fsdp', 'ctx'), 'tp')
- grad_down_weight: float32 [2, 1024, 4096], P(None, ('fsdp', 'ctx'), 'tp')
- grad_query_value_bias: float32 [2, 2, 1024], P(None, None, 'tp')
- grad_up_bias: float32 [2, 4096], P(None, 'tp')
- grad_norm_gains: float32 [2, 1024, 2], P(None, ('fsdp', 'ctx'))
- grad_row_biases: float32 [2, 1024, 4], P(None, ('fsdp', 'ctx'))
The draws below stay inside these ranges and needn't reach their ends.
Inputs may be any that keep to these rules, and one draw needn't show every extreme that they name: `block_place`: each row is a permutation of 0 to 15. `segment_ids`: in stream order each sequence is a run of one id that begins at the start of a block and lies within one aligned group of 8 blocks; the rows after a sequence up to the end of its last block carry -1; ids of different sequences of one batch differ; every batch has a sequence of 1024 rows and three sequences in all.
All inputs are finite; a program needn't handle non-finite values.
Results may differ from the reference program's by a relative error of at most 0.013.
Values may be sent and summed in bfloat16 or wider, within the bound.
No kernel may reach another device: no remote copies, remote signals or barrier semaphores. Data moves between devices by JAX's collectives and lax.ppermute only.
A program may use at most 192 MiB of HBM per device.

```python
from functools import partial
import jax
import jax.numpy as jnp
from jax import lax

D = 1024
HEADS = 16
HD = 64
FF = 4096
BLK = 128
LAYERS = 2
NB = 16
RUN_BLOCKS = 8
BATCHES = 2
TOKENS = 4096


def draw_segment_ids(key, part):
    run_count = NB // RUN_BLOCKS
    key_first, key_len_a, key_len_b = jax.random.split(key, 3)
    run_number = jnp.arange(run_count, dtype=jnp.int32)
    first_blocks = jax.random.randint(key_first, (BATCHES, run_count), 1, RUN_BLOCKS + 1)
    first_blocks = jnp.where(run_number[None, :] == 0, RUN_BLOCKS, first_blocks)
    first_blocks = jnp.where(run_number[None, :] == run_count - 1, jnp.minimum(first_blocks, RUN_BLOCKS - 1), first_blocks)
    first_length = (first_blocks - 1) * BLK + jax.random.randint(key_len_a, (BATCHES, run_count), 1, BLK + 1)
    first_length = jnp.where(run_number[None, :] == 0, RUN_BLOCKS * BLK, first_length)
    second_blocks = RUN_BLOCKS - first_blocks
    second_top = jnp.where(run_number == run_count - 1, BLK, BLK + 1)
    second_extra = jax.random.randint(key_len_b, (BATCHES, run_count), 1, second_top[None, :])
    second_length = jnp.where(second_blocks > 0, (second_blocks - 1) * BLK + second_extra, 0)
    position = jnp.arange(RUN_BLOCKS * BLK, dtype=jnp.int32)[None, None, :]
    second_start = (first_blocks * BLK)[:, :, None]
    in_first = position < first_length[:, :, None]
    in_second = (position >= second_start) & (position < second_start + second_length[:, :, None])
    ids = jnp.where(in_first, 2 * run_number[None, :, None], jnp.where(in_second, 2 * run_number[None, :, None] + 1, -1))
    return ids.reshape(BATCHES, NB * BLK).astype(jnp.int32)


def shard_levels(rng, shape, pieces, smallest, largest):
    gain = 1.0
    for dim, shards_of in pieces:
        heights = jax.random.uniform(jax.random.fold_in(jax.random.fold_in(rng, 6), dim), (shards_of,), jnp.float32, smallest / len(pieces), largest / len(pieces))
        gain = gain * jnp.repeat(jnp.exp(heights), shape[dim] // shards_of).reshape((-1,) + (1,) * (len(shape) - 1 - dim))
    return gain


def noise(rng, extent, scale, most, cuts=(), kind=jnp.bfloat16):
    entries = jax.random.normal(rng, extent, jnp.float32) * scale
    if len(cuts) > 0:
        entries = shard_levels(rng, extent, cuts, -0.22, 0.18) * entries
    return jnp.clip(entries, min=-most, max=most).astype(kind)


def setup_inputs(seed: int = 0) -> dict:
    keys = jax.random.split(jax.random.key(seed), 13)
    tokens = noise(keys[0], (TOKENS, D), 1.0, 6.0, ((0, 8),))
    cotangent = noise(keys[1], (TOKENS, D), 1.0, 6.0, ((0, 8),))
    block_place = jax.vmap(lambda own: jax.random.permutation(own, NB))(jax.random.split(keys[2], BATCHES)).reshape((BATCHES, NB)).astype(jnp.int32)
    segment_ids = draw_segment_ids(jax.random.fold_in(keys[12], 71), 0)
    qkv_weight = noise(keys[4], (LAYERS, D, 3, D), D ** -0.5, 0.1875, ((1, 8), (3, 4)))
    out_weight = noise(keys[5], (LAYERS, D, D), (D // 8) ** -0.5, 0.5, ((1, 8), (2, 4)))
    up_weight = noise(keys[6], (LAYERS, D, FF), D ** -0.5, 0.1875, ((1, 8), (2, 4)))
    down_weight = noise(keys[7], (LAYERS, D, FF), FF ** -0.5, 0.09375, ((1, 8), (2, 4)))
    query_value_bias = noise(keys[8], (LAYERS, 2, D), 0.5, 3.0, ((2, 4),))
    up_bias = noise(keys[9], (LAYERS, FF), 0.5, 3.0, ((1, 4),))
    norm_gains = jnp.clip(1.0 + 0.18 * jax.random.normal(keys[10], (LAYERS, D, 2), jnp.float32), 0.099609375, 1.8984375).astype(jnp.bfloat16)
    row_biases = noise(keys[11], (LAYERS, D, 4), 0.5, 3.0, ((1, 8),))
    return {"tokens": tokens, "cotangent": cotangent, "block_place": block_place, "segment_ids": segment_ids, "qkv_weight": qkv_weight, "out_weight": out_weight, "up_weight": up_weight, "down_weight": down_weight, "query_value_bias": query_value_bias, "up_bias": up_bias, "norm_gains": norm_gains, "row_biases": row_biases}


@jax.custom_vjp
def low(v):
    return lax.optimization_barrier(v.astype(jnp.bfloat16)).astype(jnp.float32)

@jax.custom_vjp
def low_back(v):
    return v

def low_keep(v):
    return (low(v), None)

def low_pass(kept, grad):
    return (grad,)

def back_keep(v):
    return (v, None)

def back_low(kept, grad):
    return (low(grad),)
low.defvjp(low_keep, low_pass)
low_back.defvjp(back_keep, back_low)
highest = lax.Precision.HIGHEST

def matmul(left, right):
    return jnp.dot(left, right, precision=highest, preferred_element_type=jnp.float32)

def layer_norm(values, gain_vec, shift_vec):
    average = lax.optimization_barrier(jnp.mean(values, axis=-1, keepdims=True))
    centred = values - average
    variance = lax.optimization_barrier(jnp.mean(centred * centred, axis=-1, keepdims=True))
    return centred * lax.rsqrt(variance + 1e-05) * gain_vec + shift_vec

def attend_run(slopes, members):
    queries, key_heads, value_heads, segments = members
    score_scale = queries.shape[-1] ** (-0.5)
    positions = jnp.arange(queries.shape[0], dtype=jnp.int32)
    scores = jnp.einsum('qhd,khd->hqk', queries, key_heads, precision=highest, preferred_element_type=jnp.float32) * score_scale
    distance = positions[:, None] - positions[None, :]
    allowed = (segments[:, None] == segments[None, :]) & (segments[:, None] >= 0) & (distance >= 0) | (distance == 0)
    scores = scores - slopes[:, None, None] * distance.astype(jnp.float32)[None]
    scores = low_back(jnp.where(allowed[None], scores, -1000000000.0))
    softmax_out = low(jax.nn.softmax(scores, axis=-1))
    return jnp.einsum('hqk,khd->qhd', softmax_out, value_heads, precision=highest, preferred_element_type=jnp.float32)

def forward(stream_rows, params, seg_runs):
    qkv_weight, out_weight, up_weight, down_weight, query_value_bias, up_bias, norm_gains, row_biases = params
    slopes = jnp.exp2(-8.0 * (jnp.arange(HEADS, dtype=jnp.float32) + 1.0) / HEADS)
    run_count = seg_runs.shape[0]
    residual = stream_rows
    for layer_number in range(LAYERS):
        normed = low(layer_norm(residual, norm_gains[layer_number, :, 0], row_biases[layer_number, :, 0]))
        queries = low(low_back(matmul(normed, qkv_weight[layer_number, :, 0]) + query_value_bias[layer_number, 0]))
        key_heads = low(low_back(matmul(normed, qkv_weight[layer_number, :, 1])))
        value_heads = low(low_back(matmul(normed, qkv_weight[layer_number, :, 2]) + query_value_bias[layer_number, 1]))
        attended = lax.map(jax.checkpoint(partial(attend_run, slopes)), (queries.reshape(run_count, -1, HEADS, HD), key_heads.reshape(run_count, -1, HEADS, HD), value_heads.reshape(run_count, -1, HEADS, HD), seg_runs))
        heads_low = low(low_back(attended.reshape(residual.shape)))
        branch = low_back(matmul(heads_low, out_weight[layer_number].T) + row_biases[layer_number, :, 1])
        middle = residual + branch
        second_normed = low(layer_norm(middle, norm_gains[layer_number, :, 1], row_biases[layer_number, :, 2]))
        hidden = low_back(matmul(second_normed, up_weight[layer_number]) + up_bias[layer_number])
        activated = low(jax.nn.gelu(hidden, approximate=True))
        second_branch = low_back(matmul(activated, down_weight[layer_number].T) + row_biases[layer_number, :, 3])
        residual = middle + second_branch
    return residual

def reorder(source, order):
    blocks = source.reshape(BATCHES, NB, BLK, source.shape[-1])
    picked = jnp.take_along_axis(blocks, order[:, :, None, None], axis=1)
    return picked.reshape(source.shape)

def reference(tokens, cotangent, block_place, segment_ids, qkv_weight, out_weight, up_weight, down_weight, query_value_bias, up_bias, norm_gains, row_biases):
    inverse = jnp.argsort(block_place, axis=1).astype(jnp.int32)
    stream_rows = reorder(tokens.astype(jnp.float32), inverse)
    stream_grad = reorder(cotangent.astype(jnp.float32), inverse)
    params = tuple((member.astype(jnp.float32) for member in (qkv_weight, out_weight, up_weight, down_weight, query_value_bias, up_bias, norm_gains, row_biases)))
    seg_runs = segment_ids.reshape(-1, RUN_BLOCKS * BLK)

    def whole(rows_in, weights):
        return forward(rows_in, weights, seg_runs)
    output, pullback = jax.vjp(whole, stream_rows, params)
    grad_stream, grad_params = pullback(stream_grad)
    block_output = reorder(output, block_place).astype(jnp.bfloat16)
    grad_tokens = reorder(grad_stream, block_place)
    return (block_output, grad_tokens, grad_params[0], grad_params[1], grad_params[2], grad_params[3], grad_params[4], grad_params[5], grad_params[6], grad_params[7])
```

```python
from functools import partial

import jax
import jax.numpy as jnp
from jax import lax
from jax.experimental import pallas as pl
from jax.experimental.pallas import tpu as pltpu
from jax.sharding import PartitionSpec as P

HEADS = 16
HD = 64
BLK = 128
RUN_BLOCKS = 8
LAYERS = 2
NORM_ROWS = 8
NORM_EPS = 1e-05
MASKED = -1000000000.0
QB = 256
GELU_A = 0.7978845608028654
GELU_B = 0.044715
BF = jnp.bfloat16
F32 = jnp.float32
NN = ((1,), (0,))
NT = ((1,), (1,))
VMEM_LIMIT = 40 * 1024 * 1024


def dot(left, right, dims=NN):
    return lax.dot_general(left, right, (dims, ((), ())), preferred_element_type=F32)


def shaped(shape, dtype):
    return jax.ShapeDtypeStruct(shape, dtype)


def whole():
    return pl.BlockSpec(memory_space=pltpu.VMEM)


def fixed(shape):
    return pl.BlockSpec(shape, lambda *ids: (0,) * len(shape))


def params(flops, bytes_accessed, transcendentals=0):
    return dict(
        compiler_params=pltpu.CompilerParams(vmem_limit_bytes=VMEM_LIMIT),
        cost_estimate=pl.CostEstimate(
            flops=int(flops), bytes_accessed=int(bytes_accessed), transcendentals=int(transcendentals)
        ),
    )


def rows_of(w_ref, depth):
    return jnp.concatenate([w_ref[z, :depth, :] for z in range(w_ref.shape[0])], axis=0)


def norm_stats(values):
    average = jnp.mean(values, axis=-1, keepdims=True)
    centred = values - average
    variance = jnp.mean(centred * centred, axis=-1, keepdims=True)
    scale = lax.rsqrt(variance + NORM_EPS)
    return centred * scale, scale


def gelu_parts(u):
    inner = GELU_A * (u + GELU_B * u * u * u)
    t = jnp.tanh(inner)
    return t


def norm_kernel(row, x_ref, table_ref, h_ref):
    n, _ = norm_stats(x_ref[...].astype(F32))
    h_ref[...] = (n * table_ref[row : row + 1, :] + table_ref[row + 2 : row + 3, :]).astype(BF)


def first_norm(x, table, row):
    rows, width = x.shape
    step = min(rows, 256)
    return pl.pallas_call(
        partial(norm_kernel, row),
        grid=(rows // step,),
        in_specs=[pl.BlockSpec((step, width), lambda i: (i, 0)), fixed(table.shape)],
        out_specs=pl.BlockSpec((step, width), lambda i: (i, 0)),
        out_shape=shaped((rows, width), BF),
        **params(rows * width * 10, rows * width * 4),
    )(x, table)


def add_norm_kernel(bias_row, gain_row, shift_row, x_ref, a_ref, b_ref, table_ref, y_ref, h_ref):
    branch = a_ref[...].astype(F32) + b_ref[...].astype(F32) + table_ref[bias_row : bias_row + 1, :]
    y = x_ref[...].astype(F32) + branch
    y_ref[...] = y
    n, _ = norm_stats(y)
    h_ref[...] = (
        n * table_ref[gain_row : gain_row + 1, :] + table_ref[shift_row : shift_row + 1, :]
    ).astype(BF)


def add_norm(x, a, b, table, bias_row, gain_row, shift_row):
    rows, width = x.shape
    step = min(rows, 128)
    spec = pl.BlockSpec((step, width), lambda i: (i, 0))
    return pl.pallas_call(
        partial(add_norm_kernel, bias_row, gain_row, shift_row),
        grid=(rows // step,),
        in_specs=[spec, spec, spec, fixed(table.shape)],
        out_specs=[spec, spec],
        out_shape=[shaped((rows, width), F32), shaped((rows, width), BF)],
        **params(rows * width * 12, rows * width * 14),
    )(x, a, b, table)


def qkv_kernel(nf, depth, *refs):
    h_refs, bias_ref, w_refs, out_ref = refs[:2], refs[2], refs[3 : 3 + nf], refs[3 + nf]
    weights = [rows_of(w, depth) for w in w_refs]
    span = weights[0].shape[0]
    heads = out_ref.shape[0]
    half = h_refs[0].shape[0]
    for number, h_ref in enumerate(h_refs):
        total = bias_ref[0]
        for y in range(nf):
            total = total + dot(h_ref[:, y * span : (y + 1) * span], weights[y])
        turned = total.astype(BF).T
        for j in range(heads):
            out_ref[j, :, number * half : (number + 1) * half] = turned[j * HD : (j + 1) * HD, :]


def qkv_project(h_own, h_oth, bias, packs, depth):
    half, width = h_own.shape
    nc, pad_depth, cols = packs[0].shape
    nf = len(packs)
    local = cols // 3
    heads = local // HD
    return pl.pallas_call(
        partial(qkv_kernel, nf, depth),
        grid=(3,),
        in_specs=[fixed((half, width))] * 2
        + [pl.BlockSpec((1, 1, local), lambda i: (i, 0, 0))]
        + [pl.BlockSpec((nc, pad_depth, local), lambda i: (0, 0, i))] * nf,
        out_specs=pl.BlockSpec((heads, HD, 2 * half), lambda i: (0, i, 0)),
        out_shape=shaped((heads, 3 * HD, 2 * half), BF),
        **params(2 * 2 * half * width * cols, width * cols * 2 + 2 * half * (width + cols) * 2),
    )(h_own, h_oth, bias, *packs)


def out_kernel(nf, depth, col, start, o_ref, *refs):
    w_refs, out_ref = refs[:nf], refs[nf]
    half = out_ref.shape[0]
    heads = o_ref.shape[0]
    o = jnp.concatenate([o_ref[j, :, start : start + half] for j in range(heads)], axis=0).T
    span = w_refs[0].shape[0] * depth
    for y in range(nf):
        out_ref[:, y * span : (y + 1) * span] = dot(o, rows_of(w_refs[y], depth), NT).astype(out_ref.dtype)


def out_project(o_rows, packs, depth, col, start, dtype):
    heads, _, rows = o_rows.shape
    half = rows // 2
    local = heads * HD
    nc = packs[0].shape[0]
    nf = len(packs)
    width = nf * nc * depth
    return pl.pallas_call(
        partial(out_kernel, nf, depth, col, start),
        grid=(1,),
        in_specs=[fixed(o_rows.shape)]
        + [pl.BlockSpec((nc, depth, local), lambda i: (0, 0, col // local))] * nf,
        out_specs=fixed((half, width)),
        out_shape=shaped((half, width), dtype),
        **params(2 * half * width * local, width * local * 2 + half * width * 4),
    )(o_rows, *packs)


def mlp_kernel(nf, depth, *refs):
    h_refs, bias_ref = refs[:2], refs[2]
    up_refs, down_refs = refs[3 : 3 + nf], refs[3 + nf : 3 + 2 * nf]
    u_ref, oth_ref, own_ref, acc_ref = refs[3 + 2 * nf :]
    step = pl.program_id(0)
    half = h_refs[0].shape[0]
    ups = [rows_of(w, depth) for w in up_refs]
    downs = [rows_of(w, depth) for w in down_refs]
    span = ups[0].shape[0]
    for number in range(2):
        rows = slice(number * half, (number + 1) * half)
        u = bias_ref[...]
        for y in range(nf):
            u = u + dot(h_refs[number][:, y * span : (y + 1) * span], ups[y])
        u_ref[rows, :] = u
        act = (0.5 * u * (1.0 + gelu_parts(u))).astype(BF)
        for y in range(nf):
            piece = dot(act, downs[y], NT)
            cols = slice(y * span, (y + 1) * span)

            @pl.when(step == 0)
            def _():
                acc_ref[rows, cols] = piece

            @pl.when(step > 0)
            def _():
                acc_ref[rows, cols] += piece

    @pl.when(step == pl.num_programs(0) - 1)
    def _():
        own_ref[...] = acc_ref[:half, :]
        oth_ref[...] = acc_ref[half:, :].astype(BF)


def mlp_forward(h_own, h_oth, bias, ups, up_col, downs, down_col, depth, hidden):
    half, width = h_own.shape
    nc = ups[0].shape[0]
    nf = len(ups)
    tile = min(hidden, 256)

    def weight_spec(w, col):
        return pl.BlockSpec((nc, w.shape[1], tile), lambda i: (0, 0, col // tile + i))

    return pl.pallas_call(
        partial(mlp_kernel, nf, depth),
        grid=(hidden // tile,),
        in_specs=[fixed((half, width))] * 2
        + [pl.BlockSpec((1, tile), lambda i: (0, i))]
        + [weight_spec(w, up_col) for w in ups]
        + [weight_spec(w, down_col) for w in downs],
        out_specs=[
            pl.BlockSpec((2 * half, tile), lambda i: (0, i)),
            fixed((half, width)),
            fixed((half, width)),
        ],
        out_shape=[
            shaped((2 * half, hidden), F32),
            shaped((half, width), BF),
            shaped((half, width), F32),
        ],
        scratch_shapes=[pltpu.VMEM((2 * half, width), F32)],
        **params(8 * half * width * hidden, 4 * width * hidden + 8 * half * hidden, 2 * half * hidden),
    )(h_own, h_oth, bias, *ups, *downs)


def mlp_back_kernel(nf, depth, *refs):
    g_refs, u_ref = refs[:2], refs[2]
    up_refs, down_refs = refs[3 : 3 + nf], refs[3 + nf : 3 + 2 * nf]
    act_ref, gu_ref, sum_ref, oth_ref, own_ref, acc_ref = refs[3 + 2 * nf :]
    step = pl.program_id(0)
    half = g_refs[0].shape[0]
    ups = [rows_of(w, depth) for w in up_refs]
    downs = [rows_of(w, depth) for w in down_refs]
    span = ups[0].shape[0]
    column = 0.0
    for number in range(2):
        rows = slice(number * half, (number + 1) * half)
        grad = 0.0
        for y in range(nf):
            grad = grad + dot(g_refs[number][:, y * span : (y + 1) * span], downs[y])
        u = u_ref[rows, :]
        t = gelu_parts(u)
        act_ref[rows, :] = (0.5 * u * (1.0 + t)).astype(BF)
        slope = 0.5 * (1.0 + t) + 0.5 * u * (1.0 - t * t) * (GELU_A * (1.0 + 3.0 * GELU_B * u * u))
        gu = (grad * slope).astype(BF)
        gu_ref[rows, :] = gu
        column = column + jnp.sum(gu.astype(F32), axis=0, keepdims=True)
        for y in range(nf):
            piece = dot(gu, ups[y], NT)
            cols = slice(y * span, (y + 1) * span)

            @pl.when(step == 0)
            def _():
                acc_ref[rows, cols] = piece

            @pl.when(step > 0)
            def _():
                acc_ref[rows, cols] += piece

    sum_ref[...] = column

    @pl.when(step == pl.num_programs(0) - 1)
    def _():
        own_ref[...] = acc_ref[:half, :]
        oth_ref[...] = acc_ref[half:, :].astype(BF)


def mlp_backward(g_own, g_oth, u, ups, up_col, downs, down_col, depth):
    half, width = g_own.shape
    hidden = u.shape[1]
    nc = ups[0].shape[0]
    nf = len(ups)
    tile = min(hidden, 256)

    def weight_spec(w, col):
        return pl.BlockSpec((nc, w.shape[1], tile), lambda i: (0, 0, col // tile + i))

    rows_spec = pl.BlockSpec((2 * half, tile), lambda i: (0, i))
    return pl.pallas_call(
        partial(mlp_back_kernel, nf, depth),
        grid=(hidden // tile,),
        in_specs=[fixed((half, width))] * 2
        + [rows_spec]
        + [weight_spec(w, up_col) for w in ups]
        + [weight_spec(w, down_col) for w in downs],
        out_specs=[
            rows_spec,
            rows_spec,
            pl.BlockSpec((1, tile), lambda i: (0, i)),
            fixed((half, width)),
            fixed((half, width)),
        ],
        out_shape=[
            shaped((2 * half, hidden), BF),
            shaped((2 * half, hidden), BF),
            shaped((1, hidden), F32),
            shaped((half, width), BF),
            shaped((half, width), F32),
        ],
        scratch_shapes=[pltpu.VMEM((2 * half, width), F32)],
        **params(8 * half * width * hidden, 4 * width * hidden + 16 * half * hidden, 2 * half * hidden),
    )(g_own, g_oth, u, *ups, *downs)


def weight_grad_kernel(nf, *refs):
    l_own, l_oth, r_ref = refs[:3]
    out_refs, turned_ref = refs[3 : 3 + nf], refs[3 + nf]
    half = l_own.shape[0]

    @pl.when(pl.program_id(0) == 0)
    def _():
        turned_ref[:, :half] = l_own[...].T
        turned_ref[:, half:] = l_oth[...].T

    right = r_ref[...]
    span = out_refs[0].shape[0]
    for y in range(nf):
        out_refs[y][...] = dot(turned_ref[y * span : (y + 1) * span, :], right).astype(BF)


def weight_grad(l_own, l_oth, right, nf):
    half, width = l_own.shape
    cols = right.shape[1]
    tile = min(cols, 256)
    return pl.pallas_call(
        partial(weight_grad_kernel, nf),
        grid=(cols // tile,),
        in_specs=[fixed((half, width))] * 2 + [pl.BlockSpec((2 * half, tile), lambda i: (0, i))],
        out_specs=[pl.BlockSpec((width // nf, tile), lambda i: (0, i))] * nf,
        out_shape=[shaped((width // nf, cols), BF)] * nf,
        scratch_shapes=[pltpu.VMEM((width, 2 * half), BF)],
        **params(4 * half * width * cols, 2 * width * cols + 4 * half * (width + cols)),
    )(l_own, l_oth, right)


def out_grad_kernel(nf, *refs):
    l_own, l_oth, o_ref = refs[:3]
    out_refs = refs[3:]
    half = l_own.shape[0]
    heads = o_ref.shape[0]
    turned = jnp.concatenate([o_ref[j] for j in range(heads)], axis=0)
    span = out_refs[0].shape[0]
    for y in range(nf):
        cols = slice(y * span, (y + 1) * span)
        total = dot(turned[:, :half], l_own[:, cols]) + dot(turned[:, half:], l_oth[:, cols])
        out_refs[y][...] = total.astype(BF).T


def out_grad(l_own, l_oth, o_rows, nf):
    half, width = l_own.shape
    local = o_rows.shape[0] * HD
    return pl.pallas_call(
        partial(out_grad_kernel, nf),
        in_specs=[whole()] * 3,
        out_specs=[whole()] * nf,
        out_shape=[shaped((width // nf, local), BF)] * nf,
        **params(4 * half * width * local, 2 * width * local + 4 * half * (width + local)),
    )(l_own, l_oth, o_rows)


def norm_back_kernel(gain_row, gx_ref, a_ref, b_ref, y_ref, table_ref, gy_ref, low_ref, sums_ref):
    step = pl.program_id(0)
    grad = a_ref[...].astype(F32) + b_ref[...].astype(F32)
    n, scale = norm_stats(y_ref[...].astype(F32))
    e = grad * table_ref[gain_row : gain_row + 1, :]
    mean_e = jnp.mean(e, axis=-1, keepdims=True)
    mean_en = jnp.mean(e * n, axis=-1, keepdims=True)
    gy = gx_ref[...].astype(F32) + scale * (e - mean_e - n * mean_en)
    gy_ref[...] = gy
    low = gy.astype(BF)
    low_ref[...] = low
    sums = [
        jnp.sum(grad * n, axis=0, keepdims=True),
        jnp.sum(grad, axis=0, keepdims=True),
        jnp.sum(low.astype(F32), axis=0, keepdims=True),
        jnp.sum(gx_ref[...].astype(BF).astype(F32), axis=0, keepdims=True),
    ]
    packed = jnp.concatenate(sums + [jnp.zeros((4, sums[0].shape[1]), F32)], axis=0)

    @pl.when(step == 0)
    def _():
        sums_ref[...] = packed

    @pl.when(step > 0)
    def _():
        sums_ref[...] += packed


def norm_backward(gx, a, b, y, table, gain_row):
    rows, width = gx.shape
    step = min(rows, 128)
    spec = pl.BlockSpec((step, width), lambda i: (i, 0))
    return pl.pallas_call(
        partial(norm_back_kernel, gain_row),
        grid=(rows // step,),
        in_specs=[spec] * 4 + [fixed(table.shape)],
        out_specs=[spec, spec, fixed((8, width))],
        out_shape=[shaped((rows, width), F32), shaped((rows, width), BF), shaped((8, width), F32)],
        **params(rows * width * 25, rows * width * 18),
    )(gx, a, b, y, table)


def out_back_kernel(nf, depth, *refs):
    g_refs, w_refs, out_ref = refs[:2], refs[2 : 2 + nf], refs[2 + nf]
    half = g_refs[0].shape[0]
    heads = out_ref.shape[0]
    weights = [rows_of(w, depth) for w in w_refs]
    span = weights[0].shape[0]
    for number, g_ref in enumerate(g_refs):
        total = 0.0
        for y in range(nf):
            total = total + dot(g_ref[:, y * span : (y + 1) * span], weights[y])
        turned = total.astype(BF).T
        for j in range(heads):
            out_ref[j, :, number * half : (number + 1) * half] = turned[j * HD : (j + 1) * HD, :]


def out_backward(g_own, g_oth, packs, col, depth, local):
    half, width = g_own.shape
    nc = packs[0].shape[0]
    nf = len(packs)
    return pl.pallas_call(
        partial(out_back_kernel, nf, depth),
        grid=(1,),
        in_specs=[fixed((half, width))] * 2
        + [pl.BlockSpec((nc, depth, local), lambda i: (0, 0, col // local))] * nf,
        out_specs=fixed((local // HD, HD, 2 * half)),
        out_shape=shaped((local // HD, HD, 2 * half), BF),
        **params(4 * half * width * local, 2 * width * local + 4 * half * (width + local)),
    )(g_own, g_oth, *packs)


def qkv_back_kernel(nf, depth, *refs):
    g_ref, w_refs = refs[0], refs[1 : 1 + nf]
    rows_ref, sum_ref, oth_ref, own_ref = refs[1 + nf :]
    heads = g_ref.shape[0]
    half = own_ref.shape[0]
    weights = [rows_of(w, depth) for w in w_refs]
    span = weights[0].shape[0]
    local = heads * HD
    planes = [
        jnp.concatenate([g_ref[j, i * HD : (i + 1) * HD, :] for j in range(heads)], axis=0).T
        for i in range(3)
    ]
    grads = jnp.concatenate(planes, axis=1)
    rows_ref[...] = grads
    for y in range(nf):
        cols = slice(y * span, (y + 1) * span)
        oth_ref[:, cols] = dot(grads[half:, :], weights[y], NT).astype(BF)
        own_ref[:, cols] = dot(grads[:half, :], weights[y], NT)
    sum_ref[...] = jnp.sum(grads.astype(F32), axis=0, keepdims=True)


def qkv_backward(g, packs, depth):
    heads, _, rows = g.shape
    half = rows // 2
    cols = 3 * heads * HD
    nc, pad_depth = packs[0].shape[:2]
    nf = len(packs)
    width = nf * nc * depth
    return pl.pallas_call(
        partial(qkv_back_kernel, nf, depth),
        grid=(1,),
        in_specs=[fixed(g.shape)] + [fixed((nc, pad_depth, cols))] * nf,
        out_specs=[fixed((rows, cols)), fixed((1, cols)), fixed((half, width)), fixed((half, width))],
        out_shape=[
            shaped((rows, cols), BF),
            shaped((1, cols), F32),
            shaped((half, width), BF),
            shaped((half, width), F32),
        ],
        **params(2 * rows * width * cols, 2 * width * cols + 4 * rows * cols + 3 * rows * width),
    )(g, *packs)


def gather_blocks(source_ref, src_ref, dest_ref, per_device):
    for s in range(dest_ref.shape[1] // BLK):
        src = src_ref[s]
        z = src // per_device
        start = pl.multiple_of((src - z * per_device) * BLK, BLK)
        dest_ref[:, s * BLK : (s + 1) * BLK] = source_ref[z, :, pl.ds(start, BLK)]


def scatter_blocks(dest_ref, src_ref, source, per_device, low, first):
    depth, columns = source.shape
    for s in range(columns // BLK):
        src = src_ref[first + s]
        z = src // per_device
        start = pl.multiple_of((src - z * per_device) * BLK, BLK)
        dest_ref[z, low : low + depth, pl.ds(start, BLK)] = source[:, s * BLK : (s + 1) * BLK]


def segment_columns(seg_ref, column_ref):
    for s in range(seg_ref.shape[1] // BLK):
        row = seg_ref[:, s * BLK : (s + 1) * BLK]
        row = jnp.where(row < 0, -2, row).astype(F32)
        column_ref[s * BLK : (s + 1) * BLK, :] = jnp.broadcast_to(row, (BLK, BLK)).T


def score_tile(keys, queries, column_ref, seg_ref, slope, base, first, last):
    depth = keys.shape[0]
    width = last - first
    scores = dot(keys, queries)
    key_row = lax.broadcasted_iota(jnp.int32, (depth, width), 0)
    query_row = lax.broadcasted_iota(jnp.int32, (depth, width), 1) + (first - base)
    distance = query_row - key_row
    scores = scores - slope * distance.astype(F32)
    columns = column_ref[base : base + depth, :]
    key_seg = jnp.concatenate([columns] * (width // BLK), axis=1)
    query_seg = seg_ref[:, first:last].astype(F32)
    allowed = ((key_seg == query_seg) & (distance >= 0)) | (distance == 0)
    return scores, allowed


def attend_kernel(per_device, src_ref, slope_ref, seg_ref, qkv_ref, o_ref, lse_ref, stream_ref, column_ref):
    gather_blocks(qkv_ref, src_ref, stream_ref, per_device)
    segment_columns(seg_ref, column_ref)
    slope = slope_ref[0]
    run = RUN_BLOCKS * BLK
    for base in range(0, stream_ref.shape[1], run):
        keys = stream_ref[HD : 2 * HD, base : base + run].T
        for first in range(base, base + run, QB):
            last = first + QB
            depth = last - base
            queries = stream_ref[:HD, first:last] * jnp.asarray(HD**-0.5, BF)
            scores, allowed = score_tile(
                keys[:depth], queries, column_ref, seg_ref, slope, base, first, last
            )
            scores = jnp.where(allowed, scores, MASKED)
            top = jnp.max(scores, axis=0, keepdims=True)
            weights = jnp.exp(scores - top)
            total = jnp.sum(weights, axis=0, keepdims=True)
            lse_ref[:, first:last] = top + jnp.log(total)
            values = stream_ref[2 * HD :, base : base + depth]
            out = (dot(values, weights.astype(BF)) / total).astype(BF)
            scatter_blocks(o_ref, src_ref, out, per_device, 0, first // BLK)


def attend(qkv, source, slope, segments):
    nc, depth, rows = qkv.shape
    length = nc * rows
    smem = pl.BlockSpec(memory_space=pltpu.SMEM)
    return pl.pallas_call(
        partial(attend_kernel, rows // BLK),
        in_specs=[smem, smem, whole(), whole()],
        out_specs=[whole(), whole()],
        out_shape=[shaped((nc, HD, rows), BF), shaped((1, length), F32)],
        scratch_shapes=[pltpu.VMEM((3 * HD, length), BF), pltpu.VMEM((length, BLK), F32)],
        **params(length * RUN_BLOCKS * BLK * HD * 3, length * HD * 8, length * RUN_BLOCKS * BLK // 2),
    )(source, slope, segments, qkv)


def attend_back_kernel(
    per_device, src_ref, slope_ref, seg_ref, qkv_ref, g_ref, lse_ref, out_ref, stream_ref, grad_ref, column_ref, k_acc, v_acc
):
    gather_blocks(qkv_ref, src_ref, stream_ref, per_device)
    gather_blocks(g_ref, src_ref, grad_ref, per_device)
    segment_columns(seg_ref, column_ref)
    slope = slope_ref[0]
    run = RUN_BLOCKS * BLK
    scale = HD**-0.5
    for base in range(0, stream_ref.shape[1], run):
        rows = slice(base, base + run)
        keys_turned = stream_ref[HD : 2 * HD, rows]
        keys = keys_turned.T
        values = stream_ref[2 * HD :, rows].T
        queries_rows = stream_ref[:HD, rows].T
        grads_rows = grad_ref[:, rows].T
        for first in range(base + run - QB, base - 1, -QB):
            last = first + QB
            depth = last - base
            inner = slice(first - base, last - base)
            queries = stream_ref[:HD, first:last] * jnp.asarray(scale, BF)
            scores, allowed = score_tile(
                keys[:depth], queries, column_ref, seg_ref, slope, base, first, last
            )
            weights = jnp.where(allowed, jnp.exp(scores - lse_ref[:, first:last]), 0.0)
            back = dot(values[:depth], grad_ref[:, first:last])
            delta = jnp.sum(weights * back, axis=0, keepdims=True)
            low = (weights * (back - delta)).astype(BF)
            v_piece = dot(weights.astype(BF), grads_rows[inner])
            k_piece = dot(low, queries_rows[inner])
            if depth == run:
                v_acc[...] = v_piece
                k_acc[...] = k_piece
            else:
                v_acc[:depth, :] += v_piece
                k_acc[:depth, :] += k_piece
            q_grad = (dot(keys_turned[:, :depth], low) * scale).astype(BF)
            scatter_blocks(out_ref, src_ref, q_grad, per_device, 0, first // BLK)
        scatter_blocks(out_ref, src_ref, (k_acc[...] * scale).T.astype(BF), per_device, HD, base // BLK)
        scatter_blocks(out_ref, src_ref, v_acc[...].T.astype(BF), per_device, 2 * HD, base // BLK)


def attend_backward(qkv, grads, lse, source, slope, segments):
    nc, depth, rows = qkv.shape
    length = nc * rows
    run = RUN_BLOCKS * BLK
    smem = pl.BlockSpec(memory_space=pltpu.SMEM)
    return pl.pallas_call(
        partial(attend_back_kernel, rows // BLK),
        in_specs=[smem, smem, whole(), whole(), whole(), whole()],
        out_specs=whole(),
        out_shape=shaped((nc, depth, rows), BF),
        scratch_shapes=[
            pltpu.VMEM((3 * HD, length), BF),
            pltpu.VMEM((HD, length), BF),
            pltpu.VMEM((length, BLK), F32),
            pltpu.VMEM((run, HD), F32),
            pltpu.VMEM((run, HD), F32),
        ],
        **params(length * run * HD * 7, length * HD * 16, length * run // 2),
    )(source, slope, segments, qkv, grads, lse)


def on_device(
    nf,
    nc,
    nt,
    tokens,
    cotangent,
    block_place,
    segment_ids,
    qkv_weight,
    out_weight,
    up_weight,
    down_weight,
    query_value_bias,
    up_bias,
    norm_gains,
    row_biases,
):
    rows, width = tokens.shape
    half = rows // 2
    depth = qkv_weight.shape[1]
    local = qkv_weight.shape[3]
    heads = local // HD
    hidden = up_weight.shape[2]
    span = nc * depth
    y_index = lax.axis_index("fsdp")
    z_index = lax.axis_index("ctx")
    t_index = lax.axis_index("tp")
    side = t_index % 2

    def swap(value, axis, size, bit):
        return lax.ppermute(value, axis, [(i, i ^ bit) for i in range(size)])

    def sibling(value):
        return swap(value, "tp", nt, 1)

    def across(value):
        return lax.all_to_all(value, "ctx", 0, 0)

    def gather(shard):
        mine = across(jnp.broadcast_to(shard[None], (nc,) + shard.shape))
        return [mine] + [swap(mine, "fsdp", nf, bit) for bit in range(1, nf)]

    def reduce_rows(parts):
        total = parts[0].astype(F32)
        for bit in range(1, nf):
            total = total + swap(parts[bit], "fsdp", nf, bit).astype(F32)
        pieces = across(total.astype(parts[0].dtype).reshape((nc, -1) + total.shape[1:]))
        return jnp.sum(pieces.astype(F32), axis=0)

    def tensor_sum(other, own):
        term = (own + sibling(other).astype(F32)).astype(BF)
        bit = 2
        while bit * 2 < nt:
            term = (term.astype(F32) + swap(term, "tp", nt, bit).astype(F32)).astype(BF)
            bit *= 2
        return term, swap(term, "tp", nt, bit)

    def columns_relative(value):
        return jnp.concatenate(
            [
                lax.dynamic_slice_in_dim(value, (y_index ^ bit) * span, span, axis=1)
                for bit in range(nf)
            ],
            axis=1,
        )

    def take_half(value, which):
        return lax.dynamic_slice_in_dim(value, which * half, half)

    def columns_canonical(own, oth):
        rows_all = jnp.where(
            side == 0, jnp.concatenate([own, oth], axis=0), jnp.concatenate([oth, own], axis=0)
        )
        return columns_relative(rows_all)

    per_device = rows // BLK
    count = nc * per_device
    place = block_place[0]
    stored = jnp.arange(count, dtype=jnp.int32)
    relative = (stored // per_device) * per_device + (stored % per_device + side * (per_device // 2)) % per_device
    source = jnp.sum(
        jnp.where(place[None, :] == jnp.arange(count, dtype=jnp.int32)[:, None], relative[None, :], 0), axis=1
    ).astype(jnp.int32)
    head = (t_index * heads + z_index).astype(F32)
    slope = jnp.exp2(-8.0 * (head + 1.0) / HEADS).reshape(1)
    segments = segment_ids

    def qkv_shard(layer):
        return jnp.concatenate([qkv_weight[layer, :, i, :] for i in range(3)], axis=1)

    table_rows = []
    for layer in range(LAYERS):
        table_rows += [norm_gains[layer].T, row_biases[layer].T, jnp.zeros((2, depth), BF)]
    table_shard = jnp.concatenate(table_rows, axis=0)
    extra = table_shard.shape[0]
    table_padded = jnp.pad(table_shard, ((0, 0), (0, 3 * local - depth)))
    first_packs = gather(jnp.concatenate([qkv_shard(0), table_padded], axis=0))
    table = jnp.concatenate(
        [
            jnp.transpose(part[:, depth:, :depth], (1, 0, 2)).reshape(extra, span)
            for part in first_packs
        ],
        axis=1,
    ).astype(F32)
    out_up = [gather(jnp.concatenate([out_weight[0], up_weight[0]], axis=1)), None]
    down = [gather(down_weight[0]), None]
    qkv_out_1 = gather(jnp.concatenate([out_weight[1], qkv_shard(1)], axis=1))
    up_down_1 = gather(jnp.concatenate([up_weight[1], down_weight[1]], axis=1))

    biases = [
        jnp.stack([query_value_bias[l, 0], jnp.zeros((local,), BF), query_value_bias[l, 1]])
        .astype(F32)
        .reshape(3, 1, local)
        for l in range(LAYERS)
    ]
    up_biases = [up_bias[l].astype(F32).reshape(1, hidden) for l in range(LAYERS)]

    qkv_1 = [part[:, :, local:] for part in qkv_out_1]
    qkv_packs = [first_packs, qkv_1]
    out_packs = [(out_up[0], 0), (qkv_out_1, 0)]
    up_packs = [([p[:, :, local:] for p in out_up[0]], 0), (up_down_1, 0)]
    down_packs = [(down[0], 0), (up_down_1, hidden)]

    x_all = columns_relative(tokens)
    x_half = take_half(x_all, side)
    h_own = first_norm(x_half, table, 0)
    h_oth = first_norm(take_half(x_all, 1 - side), table, 0)
    records = []
    for l in range(LAYERS):
        row = l * NORM_ROWS
        qkv = across(qkv_project(h_own, h_oth, biases[l], qkv_packs[l], depth))
        o_stream, lse = attend(qkv, source, slope, segments)
        o_rows = across(o_stream)
        packs, col = out_packs[l]
        other = out_project(o_rows, packs, depth, col, half, BF)
        own = out_project(o_rows, packs, depth, col, 0, F32)
        a, b = tensor_sum(other, own)
        y_half, h2_own = add_norm(x_half, a, b, table, row + 3, row + 1, row + 4)
        h2_oth = sibling(h2_own)
        u, other, own = mlp_forward(
            h2_own, h2_oth, up_biases[l], *up_packs[l], *down_packs[l], depth, hidden
        )
        a, b = tensor_sum(other, own)
        following = row + NORM_ROWS if l + 1 < LAYERS else row
        records.append((x_half, h_own, h_oth, qkv, lse, o_rows, y_half, h2_own, h2_oth, u))
        x_half, h_own = add_norm(y_half, a, b, table, row + 5, following, following + 2)
        if l + 1 < LAYERS:
            h_oth = sibling(h_own)
    final_low = x_half.astype(BF)
    block_output = columns_canonical(final_low, sibling(final_low))

    g_all = columns_relative(cotangent)
    gz_own, gz_oth = take_half(g_all, side), take_half(g_all, 1 - side)
    gx_half = gz_own.astype(F32)
    grads = [None] * LAYERS
    sums = [None] * LAYERS
    for l in reversed(range(LAYERS)):
        row = l * NORM_ROWS
        x_half, h_own, h_oth, qkv, lse, o_rows, y_half, h2_own, h2_oth, u = records[l]
        act, gu, up_sum, other, own = mlp_backward(
            gz_own, gz_oth, u, *up_packs[l], *down_packs[l], depth
        )
        a, b = tensor_sum(other, own)
        grad_down = reduce_rows(weight_grad(gz_own, gz_oth, act, nf))
        grad_up = reduce_rows(weight_grad(h2_own, h2_oth, gu, nf))
        gy_half, ga_own, sums_two = norm_backward(gx_half, a, b, y_half, table, row + 1)
        ga_oth = sibling(ga_own)
        packs, col = out_packs[l]
        g_stream = across(out_backward(ga_own, ga_oth, packs, col, depth, local))
        grad_out = reduce_rows(out_grad(ga_own, ga_oth, o_rows, nf))
        g_rows = across(attend_backward(qkv, g_stream, lse, source, slope, segments))
        g_proj, qkv_sum, other, own = qkv_backward(g_rows, qkv_packs[l], depth)
        a, b = tensor_sum(other, own)
        grad_qkv = reduce_rows(weight_grad(h_own, h_oth, g_proj, nf))
        gx_half, gz_own, sums_one = norm_backward(gy_half, a, b, x_half, table, row)
        if l > 0:
            gz_oth = sibling(gz_own)
        grads[l] = (grad_qkv, grad_out, grad_up, grad_down)
        sums[l] = (sums_one, sums_two, qkv_sum, up_sum)

    grad_tokens = columns_canonical(gx_half, sibling(gx_half))

    norm_parts = []
    for l in range(LAYERS):
        one, two = sums[l][0], sums[l][1]
        norm_parts += [one[0], two[0], one[1], two[2], two[1], two[3]]
    norm_all = jnp.stack(norm_parts)
    bias_all = jnp.concatenate(
        [sums[l][2][0, :local] for l in range(LAYERS)]
        + [sums[l][2][0, 2 * local :] for l in range(LAYERS)]
        + [sums[l][3][0] for l in range(LAYERS)]
    )
    count_norm = norm_all.shape[0]
    by_part = norm_all.reshape(count_norm, nf, nc, depth).transpose(1, 2, 3, 0).reshape(nf, -1)
    norm_total = by_part[0]
    bias_total = bias_all
    for bit in range(1, nf):
        came = swap(jnp.concatenate([by_part[bit], bias_all]), "fsdp", nf, bit)
        norm_total = norm_total + came[: norm_total.size]
        bias_total = bias_total + came[norm_total.size :]
    sent = jnp.concatenate(
        [
            norm_total.reshape(nc, depth * count_norm),
            jnp.broadcast_to(bias_total[None], (nc, bias_total.size)),
        ],
        axis=1,
    )
    came = jnp.sum(across(sent), axis=0)
    norm_mine = came[: depth * count_norm]
    norm_mine = (norm_mine + sibling(norm_mine)).reshape(depth, LAYERS, count_norm // LAYERS)
    norm_mine = norm_mine.transpose(1, 0, 2)
    bias_sum = came[depth * count_norm :]
    queries, values = bias_sum[: LAYERS * local], bias_sum[LAYERS * local : 2 * LAYERS * local]
    grad_bias = jnp.stack([queries.reshape(LAYERS, local), values.reshape(LAYERS, local)], axis=1)
    grad_up_bias = bias_sum[2 * LAYERS * local :].reshape(LAYERS, hidden)

    grad_qkv = jnp.stack(
        [jnp.stack([grads[l][0][:, i * local : (i + 1) * local] for i in range(3)], axis=1) for l in range(LAYERS)]
    )
    return (
        block_output,
        grad_tokens,
        grad_qkv,
        jnp.stack([grads[l][1] for l in range(LAYERS)]),
        jnp.stack([grads[l][2] for l in range(LAYERS)]),
        jnp.stack([grads[l][3] for l in range(LAYERS)]),
        grad_bias,
        grad_up_bias,
        norm_mine[:, :, :2],
        norm_mine[:, :, 2:],
    )


def solution(mesh):
    placed = (
        P(("fsdp", "ctx"), None),
        P(("fsdp", "ctx"), None),
        P("fsdp", None),
        P("fsdp", None),
        P(None, ("fsdp", "ctx"), None, "tp"),
        P(None, ("fsdp", "ctx"), "tp"),
        P(None, ("fsdp", "ctx"), "tp"),
        P(None, ("fsdp", "ctx"), "tp"),
        P(None, None, "tp"),
        P(None, "tp"),
        P(None, ("fsdp", "ctx"), None),
        P(None, ("fsdp", "ctx"), None),
    )
    return jax.shard_map(
        partial(on_device, mesh.shape["fsdp"], mesh.shape["ctx"], mesh.shape["tp"]),
        mesh=mesh,
        in_specs=placed,
        out_specs=(
            P(("fsdp", "ctx"), None),
            P(("fsdp", "ctx"), None),
            P(None, ("fsdp", "ctx"), None, "tp"),
            P(None, ("fsdp", "ctx"), "tp"),
            P(None, ("fsdp", "ctx"), "tp"),
            P(None, ("fsdp", "ctx"), "tp"),
            P(None, None, "tp"),
            P(None, "tp"),
            P(None, ("fsdp", "ctx"), None),
            P(None, ("fsdp", "ctx"), None),
        ),
        check_vma=False,
    )
```

```python
from functools import partial

import jax
import jax.numpy as jnp
from jax import lax
from jax.experimental import pallas as pl
from jax.experimental.pallas import tpu as pltpu
from jax.sharding import PartitionSpec as P

HEADS = 16
HD = 64
BLK = 128
RUN_BLOCKS = 8
LAYERS = 2
NORM_ROWS = 8
NORM_EPS = 1e-05
MASKED = -1000000000.0
QB = 256
GELU_A = 0.7978845608028654
GELU_B = 0.044715
BF = jnp.bfloat16
F32 = jnp.float32
NN = ((1,), (0,))
NT = ((1,), (1,))
VMEM_LIMIT = 40 * 1024 * 1024


def dot(left, right, dims=NN):
    return lax.dot_general(left, right, (dims, ((), ())), preferred_element_type=F32)


def shaped(shape, dtype):
    return jax.ShapeDtypeStruct(shape, dtype)


def whole():
    return pl.BlockSpec(memory_space=pltpu.VMEM)


def params(flops, bytes_accessed, transcendentals=0):
    return dict(
        compiler_params=pltpu.CompilerParams(vmem_limit_bytes=VMEM_LIMIT),
        cost_estimate=pl.CostEstimate(
            flops=int(flops), bytes_accessed=int(bytes_accessed), transcendentals=int(transcendentals)
        ),
    )


def rows_of(refs, col, cols, depth, extra=0):
    pieces = []
    for ref in refs:
        for start in range(0, ref.shape[0], depth + extra):
            pieces.append(ref[start : start + depth, col : col + cols])
    return jnp.concatenate(pieces, axis=0)


def call(kernel, out_shape, args, flops, scratch=(), transcendentals=0, smem=0):
    outs = out_shape if isinstance(out_shape, (list, tuple)) else [out_shape]
    moved = sum(a.size * a.dtype.itemsize for a in args) + sum(
        o.size * jnp.dtype(o.dtype).itemsize for o in outs
    )
    specs = [pl.BlockSpec(memory_space=pltpu.SMEM)] * smem + [whole()] * (len(args) - smem)
    return pl.pallas_call(
        kernel,
        in_specs=specs,
        out_specs=[whole()] * len(outs) if outs is out_shape else whole(),
        out_shape=out_shape,
        scratch_shapes=list(scratch),
        **params(flops, moved, transcendentals),
    )(*args)


def norm_stats(values):
    average = jnp.mean(values, axis=-1, keepdims=True)
    centred = values - average
    variance = jnp.mean(centred * centred, axis=-1, keepdims=True)
    scale = lax.rsqrt(variance + NORM_EPS)
    return centred * scale, scale


def gelu_parts(u):
    inner = GELU_A * (u + GELU_B * u * u * u)
    t = jnp.tanh(inner)
    return t


def add_norm_kernel(bias_row, gain_row, shift_row, x_ref, a_ref, b_ref, table_ref, y_ref, h_ref):
    branch = a_ref[...].astype(F32) + b_ref[...].astype(F32) + table_ref[bias_row : bias_row + 1, :]
    y = x_ref[...].astype(F32) + branch
    y_ref[...] = y
    n, _ = norm_stats(y)
    h_ref[...] = (
        n * table_ref[gain_row : gain_row + 1, :] + table_ref[shift_row : shift_row + 1, :]
    ).astype(BF)


def add_norm(x, a, b, table, bias_row, gain_row, shift_row):
    rows, width = x.shape
    return call(
        partial(add_norm_kernel, bias_row, gain_row, shift_row),
        [shaped((rows, width), F32), shaped((rows, width), BF)],
        [x, a, b, table],
        rows * width * 12,
    )


def heads_out(out_ref, total, number, row):
    half = total.shape[0]
    turned = total.astype(BF).T
    for j in range(out_ref.shape[0]):
        out_ref[j, row : row + HD, number * half : (number + 1) * half] = turned[j * HD : (j + 1) * HD, :]


def qkv_rows(h_refs, bias_ref, w_refs, out_ref, col, depth, extra):
    local = out_ref.shape[0] * HD
    h = jnp.concatenate([h_ref[...] for h_ref in h_refs], axis=0)
    for i in range(3):
        weights = rows_of(w_refs, col + i * local, local, depth, extra)
        heads_out(out_ref, dot(h, weights) + bias_ref[i : i + 1, :], 0, i * HD)


def qkv_kernel(col, depth, h_own, h_oth, bias_ref, *refs):
    qkv_rows([h_own, h_oth], bias_ref, refs[:-1], refs[-1], col, depth, 0)


def qkv_project(h_own, h_oth, bias, pack, col, depth):
    half, width = h_own.shape
    local = bias.shape[1]
    return call(
        partial(qkv_kernel, col, depth),
        shaped((local // HD, 3 * HD, 2 * half), BF),
        [h_own, h_oth, bias, *pack],
        12 * half * width * local,
    )


def first_qkv_kernel(row, depth, extra, n_own, n_oth, table_ref, bias_ref, *refs):
    w_refs, (h_own, h_oth, out_ref) = refs[:-3], refs[-3:]
    for n_ref, h_ref in ((n_own, h_own), (n_oth, h_oth)):
        h_ref[...] = (n_ref[...] * table_ref[row : row + 1, :] + table_ref[row + 2 : row + 3, :]).astype(BF)
    qkv_rows([h_own, h_oth], bias_ref, w_refs, out_ref, 0, depth, extra)


def first_qkv(n_own, n_oth, table, row, bias, pack, depth, extra):
    half, width = n_own.shape
    local = bias.shape[1]
    return call(
        partial(first_qkv_kernel, row, depth, extra),
        [
            shaped((half, width), BF),
            shaped((half, width), BF),
            shaped((local // HD, 3 * HD, 2 * half), BF),
        ],
        [n_own, n_oth, table, bias, *pack],
        12 * half * width * local,
    )


def out_kernel(col, depth, start, o_ref, *refs):
    w_refs, out_ref = refs[:-1], refs[-1]
    half = out_ref.shape[0]
    heads = o_ref.shape[0]
    o = jnp.concatenate([o_ref[j, :, start : start + half] for j in range(heads)], axis=0).T
    weights = rows_of(w_refs, col, heads * HD, depth)
    out_ref[...] = dot(o, weights, NT).astype(out_ref.dtype)


def out_project(o_rows, pack, col, depth, width, start, dtype):
    heads, _, rows = o_rows.shape
    half = rows // 2
    return call(
        partial(out_kernel, col, depth, start),
        shaped((half, width), dtype),
        [o_rows, *pack],
        2 * half * width * heads * HD,
    )


def mlp_kernel(counts, up_col, down_col, depth, h_own, h_oth, bias_ref, *refs):
    ups, downs = refs[: counts[0]], refs[counts[0] : counts[0] + counts[1]]
    u_ref, oth_ref, own_ref = refs[counts[0] + counts[1] :]
    half = h_own.shape[0]
    hidden = u_ref.shape[1]
    h = jnp.concatenate([h_own[...], h_oth[...]], axis=0)
    u = dot(h, rows_of(ups, up_col, hidden, depth)) + bias_ref[...]
    u_ref[...] = u
    act = (0.5 * u * (1.0 + gelu_parts(u))).astype(BF)
    total = dot(act, rows_of(downs, down_col, hidden, depth), NT)
    own_ref[...] = total[:half, :]
    oth_ref[...] = total[half:, :].astype(BF)


def mlp_forward(h_own, h_oth, bias, up, down, depth):
    half, width = h_own.shape
    hidden = bias.shape[1]
    return call(
        partial(mlp_kernel, (len(up[0]), len(down[0])), up[1], down[1], depth),
        [
            shaped((2 * half, hidden), F32),
            shaped((half, width), BF),
            shaped((half, width), F32),
        ],
        [h_own, h_oth, bias, *up[0], *down[0]],
        8 * half * width * hidden,
        transcendentals=2 * half * hidden,
    )


def mlp_back_kernel(counts, up_col, down_col, depth, g_own, g_oth, u_ref, *refs):
    ups, downs = refs[: counts[0]], refs[counts[0] : counts[0] + counts[1]]
    act_ref, gu_ref, sum_ref, oth_ref, own_ref = refs[counts[0] + counts[1] :]
    half = g_own.shape[0]
    hidden = u_ref.shape[1]
    g = jnp.concatenate([g_own[...], g_oth[...]], axis=0)
    grad = dot(g, rows_of(downs, down_col, hidden, depth))
    u = u_ref[...]
    t = gelu_parts(u)
    act_ref[...] = (0.5 * u * (1.0 + t)).astype(BF)
    slope = 0.5 * (1.0 + t) + 0.5 * u * (1.0 - t * t) * (GELU_A * (1.0 + 3.0 * GELU_B * u * u))
    gu = (grad * slope).astype(BF)
    gu_ref[...] = gu
    sum_ref[...] = jnp.sum(gu.astype(F32), axis=0, keepdims=True)
    total = dot(gu, rows_of(ups, up_col, hidden, depth), NT)
    own_ref[...] = total[:half, :]
    oth_ref[...] = total[half:, :].astype(BF)


def mlp_backward(g_own, g_oth, u, up, down, depth):
    half, width = g_own.shape
    hidden = u.shape[1]
    return call(
        partial(mlp_back_kernel, (len(up[0]), len(down[0])), up[1], down[1], depth),
        [
            shaped((2 * half, hidden), BF),
            shaped((2 * half, hidden), BF),
            shaped((1, hidden), F32),
            shaped((half, width), BF),
            shaped((half, width), F32),
        ],
        [g_own, g_oth, u, *up[0], *down[0]],
        8 * half * width * hidden,
        transcendentals=2 * half * hidden,
    )


def grads_out(out_refs, total, col):
    span = out_refs[0].shape[0]
    for y, out_ref in enumerate(out_refs):
        out_ref[:, col : col + total.shape[1]] = total[y * span : (y + 1) * span].astype(BF)


def mlp_grad_kernel(g_own, g_oth, h_own, h_oth, act_ref, gu_ref, *out_refs):
    hidden = act_ref.shape[1]
    h = jnp.concatenate([h_own[...], h_oth[...]], axis=0).T
    grads_out(out_refs, dot(h, gu_ref[...]), 0)
    g = jnp.concatenate([g_own[...], g_oth[...]], axis=0).T
    grads_out(out_refs, dot(g, act_ref[...]), hidden)


def mlp_grad(g_own, g_oth, h_own, h_oth, act, gu, nf):
    half, width = g_own.shape
    hidden = act.shape[1]
    return call(
        mlp_grad_kernel,
        [shaped((width // nf, 2 * hidden), BF)] * nf,
        [g_own, g_oth, h_own, h_oth, act, gu],
        8 * half * width * hidden,
    )


def out_q_grad_kernel(g_own, g_oth, o_ref, h_own, h_oth, p_ref, *out_refs):
    heads = o_ref.shape[0]
    local = heads * HD
    g = jnp.concatenate([g_own[...], g_oth[...]], axis=0).T
    o = jnp.concatenate([o_ref[j] for j in range(heads)], axis=0)
    grads_out(out_refs, dot(g, o, NT), 0)
    h = jnp.concatenate([h_own[...], h_oth[...]], axis=0).T
    grads_out(out_refs, dot(h, p_ref[:, :local]), local)


def out_q_grad(g_own, g_oth, o_rows, h_own, h_oth, g_proj, nf):
    half, width = g_own.shape
    local = o_rows.shape[0] * HD
    return call(
        out_q_grad_kernel,
        [shaped((width // nf, 2 * local), BF)] * nf,
        [g_own, g_oth, o_rows, h_own, h_oth, g_proj],
        8 * half * width * local,
    )


def kv_grad_kernel(h_own, h_oth, p_ref, *out_refs):
    local = p_ref.shape[1] // 3
    h = jnp.concatenate([h_own[...], h_oth[...]], axis=0).T
    grads_out(out_refs, dot(h, p_ref[:, local:]), 0)


def kv_grad(h_own, h_oth, g_proj, nf):
    half, width = h_own.shape
    local = g_proj.shape[1] // 3
    return call(
        kv_grad_kernel,
        [shaped((width // nf, 2 * local), BF)] * nf,
        [h_own, h_oth, g_proj],
        8 * half * width * local,
    )


def part_sum_kernel(depth, own_ref, *refs):
    count = (len(refs) - own_ref.shape[0] // depth)
    came, outs = refs[:count], refs[count:]
    for number, out_ref in enumerate(outs):
        rows = slice(number * depth, (number + 1) * depth)
        total = own_ref[rows, :].astype(F32)
        for ref in came:
            total = total + ref[rows, :].astype(F32)
        out_ref[...] = total.astype(out_ref.dtype)


def part_sum(own, came, depth):
    rows, cols = own.shape
    pieces = rows // depth
    return call(
        partial(part_sum_kernel, depth),
        [shaped((depth, cols), F32 if k == 0 else BF) for k in range(pieces)],
        [own, *came],
        rows * cols * 2,
    )


def final_kernel(plans, *refs):
    outs = refs[-len(plans) :]
    for out_ref, plan in zip(outs, plans):
        for index, first, count, col in plan:
            cols = out_ref.shape[-1]
            total = refs[first][:, col : col + cols].astype(F32)
            for k in range(1, count):
                total = total + refs[first + k][:, col : col + cols].astype(F32)
            out_ref[index] = total


def final_sums(plans, shapes, pieces):
    return call(partial(final_kernel, plans), shapes, pieces, sum(p.size for p in pieces))


def norm_back_kernel(gain_row, gx_ref, a_ref, b_ref, y_ref, table_ref, gy_ref, low_ref, sums_ref):
    grad = a_ref[...].astype(F32) + b_ref[...].astype(F32)
    n, scale = norm_stats(y_ref[...].astype(F32))
    e = grad * table_ref[gain_row : gain_row + 1, :]
    mean_e = jnp.mean(e, axis=-1, keepdims=True)
    mean_en = jnp.mean(e * n, axis=-1, keepdims=True)
    gx = gx_ref[...].astype(F32)
    gy = gx + scale * (e - mean_e - n * mean_en)
    gy_ref[...] = gy
    low = gy.astype(BF)
    low_ref[...] = low
    sums_ref[0:1, :] = jnp.sum(grad * n, axis=0, keepdims=True)
    sums_ref[1:2, :] = jnp.sum(grad, axis=0, keepdims=True)
    sums_ref[2:3, :] = jnp.sum(low.astype(F32), axis=0, keepdims=True)
    sums_ref[3:4, :] = jnp.sum(gx.astype(BF).astype(F32), axis=0, keepdims=True)
    sums_ref[4:, :] = jnp.zeros((4, gx.shape[1]), F32)


def norm_backward(gx, a, b, y, table, gain_row):
    rows, width = gx.shape
    return call(
        partial(norm_back_kernel, gain_row),
        [shaped((rows, width), F32), shaped((rows, width), BF), shaped((8, width), F32)],
        [gx, a, b, y, table],
        rows * width * 25,
    )


def out_back_kernel(col, depth, g_own, g_oth, *refs):
    w_refs, out_ref = refs[:-1], refs[-1]
    g = jnp.concatenate([g_own[...], g_oth[...]], axis=0)
    heads_out(out_ref, dot(g, rows_of(w_refs, col, out_ref.shape[0] * HD, depth)), 0, 0)


def out_backward(g_own, g_oth, pack, col, depth, local):
    half, width = g_own.shape
    return call(
        partial(out_back_kernel, col, depth),
        shaped((local // HD, HD, 2 * half), BF),
        [g_own, g_oth, *pack],
        4 * half * width * local,
    )


def qkv_back_kernel(col, depth, extra, g_ref, *refs):
    w_refs, (rows_ref, sum_ref, oth_ref, own_ref) = refs[:-4], refs[-4:]
    heads = g_ref.shape[0]
    half = own_ref.shape[0]
    local = heads * HD
    planes = [
        jnp.concatenate([g_ref[j, i * HD : (i + 1) * HD, :] for j in range(heads)], axis=0).T
        for i in range(3)
    ]
    grads = jnp.concatenate(planes, axis=1)
    rows_ref[...] = grads
    total = dot(grads, rows_of(w_refs, col, 3 * local, depth, extra), NT)
    oth_ref[...] = total[half:].astype(BF)
    own_ref[...] = total[:half]
    sum_ref[...] = jnp.sum(grads.astype(F32), axis=0, keepdims=True)


def qkv_backward(g, pack, col, depth, extra, width):
    heads, _, rows = g.shape
    half = rows // 2
    cols = 3 * heads * HD
    return call(
        partial(qkv_back_kernel, col, depth, extra),
        [
            shaped((rows, cols), BF),
            shaped((1, cols), F32),
            shaped((half, width), BF),
            shaped((half, width), F32),
        ],
        [g, *pack],
        2 * rows * width * cols,
    )


def gather_blocks(source_ref, src_ref, dest_ref, per_device):
    for s in range(dest_ref.shape[1] // BLK):
        src = src_ref[s]
        z = src // per_device
        start = pl.multiple_of((src - z * per_device) * BLK, BLK)
        dest_ref[:, s * BLK : (s + 1) * BLK] = source_ref[z, :, pl.ds(start, BLK)]


def scatter_blocks(dest_ref, src_ref, source, per_device, low, first):
    depth, columns = source.shape
    for s in range(columns // BLK):
        src = src_ref[first + s]
        z = src // per_device
        start = pl.multiple_of((src - z * per_device) * BLK, BLK)
        dest_ref[z, low : low + depth, pl.ds(start, BLK)] = source[:, s * BLK : (s + 1) * BLK]


def segment_columns(seg_ref, column_ref):
    for s in range(seg_ref.shape[1] // BLK):
        row = seg_ref[:, s * BLK : (s + 1) * BLK]
        row = jnp.where(row < 0, -2, row).astype(F32)
        column_ref[s * BLK : (s + 1) * BLK, :] = jnp.broadcast_to(row, (BLK, BLK)).T


def score_tile(keys, queries, column_ref, seg_ref, slope, base, first, last):
    depth = keys.shape[0]
    width = last - first
    scores = dot(keys, queries)
    key_row = lax.broadcasted_iota(jnp.int32, (depth, width), 0)
    query_row = lax.broadcasted_iota(jnp.int32, (depth, width), 1) + (first - base)
    distance = query_row - key_row
    scores = scores - slope * distance.astype(F32)
    columns = column_ref[base : base + depth, :]
    key_seg = jnp.concatenate([columns] * (width // BLK), axis=1)
    query_seg = seg_ref[:, first:last].astype(F32)
    allowed = ((key_seg == query_seg) & (distance >= 0)) | (distance == 0)
    return scores, allowed


def attend_kernel(per_device, src_ref, slope_ref, seg_ref, qkv_ref, o_ref, lse_ref, stream_ref, column_ref):
    gather_blocks(qkv_ref, src_ref, stream_ref, per_device)
    segment_columns(seg_ref, column_ref)
    slope = slope_ref[0]
    run = RUN_BLOCKS * BLK
    for base in range(0, stream_ref.shape[1], run):
        keys = stream_ref[HD : 2 * HD, base : base + run].T
        for first in range(base, base + run, QB):
            last = first + QB
            depth = last - base
            queries = stream_ref[:HD, first:last] * jnp.asarray(HD**-0.5, BF)
            scores, allowed = score_tile(
                keys[:depth], queries, column_ref, seg_ref, slope, base, first, last
            )
            scores = jnp.where(allowed, scores, MASKED)
            top = jnp.max(scores, axis=0, keepdims=True)
            weights = jnp.exp(scores - top)
            total = jnp.sum(weights, axis=0, keepdims=True)
            lse_ref[:, first:last] = top + jnp.log(total)
            values = stream_ref[2 * HD :, base : base + depth]
            out = (dot(values, weights.astype(BF)) / total).astype(BF)
            scatter_blocks(o_ref, src_ref, out, per_device, 0, first // BLK)


def attend(qkv, source, slope, segments):
    nc, depth, rows = qkv.shape
    length = nc * rows
    smem = pl.BlockSpec(memory_space=pltpu.SMEM)
    return pl.pallas_call(
        partial(attend_kernel, rows // BLK),
        in_specs=[smem, smem, whole(), whole()],
        out_specs=[whole(), whole()],
        out_shape=[shaped((nc, HD, rows), BF), shaped((1, length), F32)],
        scratch_shapes=[pltpu.VMEM((3 * HD, length), BF), pltpu.VMEM((length, BLK), F32)],
        **params(length * RUN_BLOCKS * BLK * HD * 3, length * HD * 8, length * RUN_BLOCKS * BLK // 2),
    )(source, slope, segments, qkv)


def attend_back_kernel(
    per_device, src_ref, slope_ref, seg_ref, qkv_ref, g_ref, lse_ref, out_ref, stream_ref, grad_ref, column_ref, k_acc, v_acc
):
    gather_blocks(qkv_ref, src_ref, stream_ref, per_device)
    gather_blocks(g_ref, src_ref, grad_ref, per_device)
    segment_columns(seg_ref, column_ref)
    slope = slope_ref[0]
    run = RUN_BLOCKS * BLK
    scale = HD**-0.5
    for base in range(0, stream_ref.shape[1], run):
        rows = slice(base, base + run)
        keys_turned = stream_ref[HD : 2 * HD, rows]
        keys = keys_turned.T
        values = stream_ref[2 * HD :, rows].T
        queries_rows = stream_ref[:HD, rows].T
        grads_rows = grad_ref[:, rows].T
        for first in range(base + run - QB, base - 1, -QB):
            last = first + QB
            depth = last - base
            inner = slice(first - base, last - base)
            queries = stream_ref[:HD, first:last] * jnp.asarray(scale, BF)
            scores, allowed = score_tile(
                keys[:depth], queries, column_ref, seg_ref, slope, base, first, last
            )
            weights = jnp.where(allowed, jnp.exp(scores - lse_ref[:, first:last]), 0.0)
            back = dot(values[:depth], grad_ref[:, first:last])
            delta = jnp.sum(weights * back, axis=0, keepdims=True)
            low = (weights * (back - delta)).astype(BF)
            v_piece = dot(weights.astype(BF), grads_rows[inner])
            k_piece = dot(low, queries_rows[inner])
            if depth == run:
                v_acc[...] = v_piece
                k_acc[...] = k_piece
            else:
                v_acc[:depth, :] += v_piece
                k_acc[:depth, :] += k_piece
            q_grad = (dot(keys_turned[:, :depth], low) * scale).astype(BF)
            scatter_blocks(out_ref, src_ref, q_grad, per_device, 0, first // BLK)
        scatter_blocks(out_ref, src_ref, (k_acc[...] * scale).T.astype(BF), per_device, HD, base // BLK)
        scatter_blocks(out_ref, src_ref, v_acc[...].T.astype(BF), per_device, 2 * HD, base // BLK)


def attend_backward(qkv, grads, lse, source, slope, segments):
    nc, depth, rows = qkv.shape
    length = nc * rows
    run = RUN_BLOCKS * BLK
    smem = pl.BlockSpec(memory_space=pltpu.SMEM)
    return pl.pallas_call(
        partial(attend_back_kernel, rows // BLK),
        in_specs=[smem, smem, whole(), whole(), whole(), whole()],
        out_specs=whole(),
        out_shape=shaped((nc, depth, rows), BF),
        scratch_shapes=[
            pltpu.VMEM((3 * HD, length), BF),
            pltpu.VMEM((HD, length), BF),
            pltpu.VMEM((length, BLK), F32),
            pltpu.VMEM((run, HD), F32),
            pltpu.VMEM((run, HD), F32),
        ],
        **params(length * run * HD * 7, length * HD * 16, length * run // 2),
    )(source, slope, segments, qkv, grads, lse)


def on_device(
    nf,
    nc,
    nt,
    tokens,
    cotangent,
    block_place,
    segment_ids,
    qkv_weight,
    out_weight,
    up_weight,
    down_weight,
    query_value_bias,
    up_bias,
    norm_gains,
    row_biases,
):
    rows, width = tokens.shape
    half = rows // 2
    depth = qkv_weight.shape[1]
    local = qkv_weight.shape[3]
    heads = local // HD
    hidden = up_weight.shape[2]
    span = nc * depth
    y_index = lax.axis_index("fsdp")
    z_index = lax.axis_index("ctx")
    t_index = lax.axis_index("tp")
    side = t_index % 2

    def swap(value, axis, size, bit):
        return lax.ppermute(value, axis, [(i, i ^ bit) for i in range(size)])

    def sibling(value):
        return swap(value, "tp", nt, 1)

    def across(value):
        return lax.all_to_all(value, "ctx", 0, 0)

    def tie(value, *others):
        return lax.optimization_barrier((value, *others))[0]

    def gather_z(shard):
        return [swap(shard, "ctx", nc, bit) for bit in range(1, nc)]

    def gather_y(shard, came, apart=False):
        pack = [shard, *came]
        for bit in range(1, nf):
            if apart:
                pack.append(swap(shard, "fsdp", nf, bit))
                pack.append(swap(jnp.concatenate(came, axis=0), "fsdp", nf, bit))
            else:
                pack.append(swap(jnp.concatenate([shard, *came], axis=0), "fsdp", nf, bit))
        return pack

    def send_y(parts):
        return [swap(parts[bit], "fsdp", nf, bit) for bit in range(1, nf)]

    def send_z(pieces):
        return [pieces[0]] + [swap(pieces[bit], "ctx", nc, bit) for bit in range(1, nc)]

    def tensor_sum(other, own):
        term = (own + sibling(other).astype(F32)).astype(BF)
        bit = 2
        while bit * 2 < nt:
            term = (term.astype(F32) + swap(term, "tp", nt, bit).astype(F32)).astype(BF)
            bit *= 2
        return term, swap(term, "tp", nt, bit)

    def columns_relative(value):
        return jnp.concatenate(
            [
                lax.dynamic_slice_in_dim(
                    value, ((y_index ^ a) * nc + (z_index ^ b)) * depth, depth, axis=1
                )
                for a in range(nf)
                for b in range(nc)
            ],
            axis=1,
        )

    def take_half(value, which):
        return lax.dynamic_slice_in_dim(value, which * half, half)

    def columns_canonical(own, oth):
        rows_all = jnp.where(
            side == 0, jnp.concatenate([own, oth], axis=0), jnp.concatenate([oth, own], axis=0)
        )
        return columns_relative(rows_all)

    per_device = rows // BLK
    count = nc * per_device
    place = block_place[0]
    stored = jnp.arange(count, dtype=jnp.int32)
    relative = (stored // per_device) * per_device + (stored % per_device + side * (per_device // 2)) % per_device
    source = jnp.sum(
        jnp.where(place[None, :] == jnp.arange(count, dtype=jnp.int32)[:, None], relative[None, :], 0), axis=1
    ).astype(jnp.int32)
    head = (t_index * heads + z_index).astype(F32)
    slope = jnp.exp2(-8.0 * (head + 1.0) / HEADS).reshape(1)
    segments = segment_ids

    def qkv_shard(layer):
        return [qkv_weight[layer, :, i, :] for i in range(3)]

    table_rows = []
    for layer in range(LAYERS):
        table_rows += [norm_gains[layer].T, row_biases[layer].T, jnp.zeros((2, depth), BF)]
    table_shard = jnp.concatenate(table_rows, axis=0)
    extra = table_shard.shape[0]
    table_padded = jnp.pad(table_shard, ((0, 0), (0, 3 * local - depth)))
    first_shard = jnp.concatenate([jnp.concatenate(qkv_shard(0), axis=1), table_padded], axis=0)
    first_z = gather_z(first_shard)
    first_pack = gather_y(first_shard, first_z, apart=True)
    table = jnp.concatenate(
        [
            ref[start + depth : start + depth + extra, :depth]
            for ref in first_pack
            for start in range(0, ref.shape[0], depth + extra)
        ],
        axis=1,
    ).astype(F32)

    biases = [
        jnp.stack([query_value_bias[l, 0], jnp.zeros((local,), BF), query_value_bias[l, 1]]).astype(F32)
        for l in range(LAYERS)
    ]
    up_biases = [up_bias[l].astype(F32).reshape(1, hidden) for l in range(LAYERS)]

    x_all = columns_relative(tokens)
    x_half = take_half(x_all, side)
    n_own = norm_stats(x_half.astype(F32))[0]
    n_oth = norm_stats(take_half(x_all, 1 - side).astype(F32))[0]
    h_own, h_oth, qkv_sent = first_qkv(n_own, n_oth, table, 0, biases[0], first_pack, depth, extra)

    out_up_shard = tie(jnp.concatenate([out_weight[0], up_weight[0]], axis=1), *first_z)
    out_up_z = gather_z(out_up_shard)
    out_up = gather_y(out_up_shard, out_up_z)
    out_packs, up_packs, down_packs, qkv_packs = [(out_up, 0)], [(out_up, local)], [], [(first_pack, 0, extra)]

    records = []
    last_other = last_own = None
    for l in range(LAYERS):
        row = l * NORM_ROWS
        qkv = across(qkv_sent)
        if l == 0:
            down_shard = tie(down_weight[0], qkv, *out_up_z)
            down_z = gather_z(down_shard)
            down_packs.append((gather_y(down_shard, down_z), 0))
            next_shard = tie(jnp.concatenate([out_weight[1], *qkv_shard(1)], axis=1), *down_z)
            next_z = gather_z(next_shard)
            next_pack = gather_y(next_shard, next_z)
            out_packs.append((next_pack, 0))
            qkv_packs.append((next_pack, local, 0))
            up_shard = tie(up_weight[1], *next_z)
            up_z = gather_z(up_shard)
            up_packs.append((gather_y(up_shard, up_z), 0))
            down_shard = tie(down_weight[1], *up_z)
            down_packs.append((gather_y(down_shard, gather_z(down_shard)), 0))
        o_stream, lse = attend(qkv, source, slope, segments)
        o_rows = across(o_stream)
        other = out_project(o_rows, *out_packs[l], depth, width, half, BF)
        own = out_project(tie(o_rows, other), *out_packs[l], depth, width, 0, F32)
        a, b = tensor_sum(other, own)
        y_half, h2_own = add_norm(x_half, a, b, table, row + 3, row + 1, row + 4)
        h2_oth = sibling(h2_own)
        u, other, own = mlp_forward(h2_own, h2_oth, up_biases[l], up_packs[l], down_packs[l], depth)
        records.append((x_half, h_own, h_oth, qkv, lse, o_rows, y_half, h2_own, h2_oth, u))
        if l + 1 < LAYERS:
            a, b = tensor_sum(other, own)
            following = row + NORM_ROWS
            x_half, h_own = add_norm(y_half, a, b, table, row + 5, following, following + 2)
            h_oth = sibling(h_own)
            qkv_sent = qkv_project(h_own, h_oth, biases[l + 1], *qkv_packs[l + 1][:2], depth)
        else:
            last_other, last_own = other, own

    g_all = columns_relative(cotangent)
    gz_own, gz_oth = take_half(g_all, side), take_half(g_all, 1 - side)
    gx_half = gz_own.astype(F32)
    sums = [None] * LAYERS
    pieces = [None] * LAYERS
    waiting = None
    for l in reversed(range(LAYERS)):
        row = l * NORM_ROWS
        x_half, h_own, h_oth, qkv, lse, o_rows, y_half, h2_own, h2_oth, u = records[l]
        act, gu, up_sum, other, own = mlp_backward(gz_own, gz_oth, u, up_packs[l], down_packs[l], depth)
        a, b = tensor_sum(other, own)
        parts = mlp_grad(gz_own, gz_oth, h2_own, h2_oth, tie(act, a), gu, nf)
        mlp_came = send_y(parts)
        mlp_own = parts[0]
        b = tie(b, *parts)
        if waiting is not None:
            out_q, kv = (part_sum(tie(mine, a), came, depth) for mine, came in waiting)
            b = tie(b, *out_q, *kv)
            pieces[l + 1] = (pieces[l + 1], send_z(out_q), send_z(kv))
        gy_half, ga_own, sums_two = norm_backward(gx_half, a, b, y_half, table, row + 1)
        ga_oth = sibling(ga_own)
        g_stream = across(out_backward(ga_own, ga_oth, *out_packs[l], depth, local))
        if l == LAYERS - 1:
            a, b = tensor_sum(tie(last_other, g_stream), last_own)
            final_half = y_half + (a.astype(F32) + b.astype(F32) + table[row + 5])
            final_low = final_half.astype(BF)
            block_output = columns_canonical(final_low, sibling(final_low))
        g_sent = attend_backward(qkv, g_stream, lse, source, slope, segments)
        mlp_pieces = part_sum(tie(mlp_own, g_sent), mlp_came, depth)
        g_rows = tie(across(g_sent), *mlp_pieces)
        pieces[l] = send_z(mlp_pieces)
        g_proj, qkv_sum, other, own = qkv_backward(
            g_rows, qkv_packs[l][0], qkv_packs[l][1], depth, qkv_packs[l][2], width
        )
        a, b = tensor_sum(other, own)
        out_q_parts = out_q_grad(ga_own, ga_oth, o_rows, h_own, h_oth, tie(g_proj, a), nf)
        out_q_came = send_y(out_q_parts)
        kv_parts = kv_grad(h_own, h_oth, tie(g_proj, *out_q_parts), nf)
        kv_came = send_y(kv_parts)
        b = tie(b, *kv_parts)
        waiting = [(out_q_parts[0], out_q_came), (kv_parts[0], kv_came)]
        gx_half, gz_own, sums_one = norm_backward(gy_half, a, b, x_half, table, row)
        if l > 0:
            gz_oth = sibling(gz_own)
        sums[l] = (sums_one, sums_two, qkv_sum, up_sum)
    out_q, kv = (part_sum(mine, came, depth) for mine, came in waiting)
    pieces[0] = (pieces[0], send_z(out_q), send_z(kv))

    grad_tokens = columns_canonical(gx_half, sibling(gx_half))

    def plan(which, col, index=lambda layer: layer):
        return [(index(layer), which * LAYERS * nc + layer * nc, nc, col) for layer in range(LAYERS)]

    def weight_sums(which, plans, shapes):
        return final_sums(plans, shapes, [p for layer in range(LAYERS) for p in pieces[layer][which]])

    grad_up, grad_down = weight_sums(
        0, [plan(0, 0), plan(0, hidden)], [shaped((LAYERS, depth, hidden), F32)] * 2
    )
    out_q_all = [p for layer in range(LAYERS) for p in pieces[layer][1]]
    kv_all = [p for layer in range(LAYERS) for p in pieces[layer][2]]
    qkv_plan = []
    for i in range(3):
        which, col = (0, local) if i == 0 else (1, (i - 1) * local)
        qkv_plan += [
            ((layer, i), which * LAYERS * nc + layer * nc, nc, col) for layer in range(LAYERS)
        ]
    grad_out, grad_qkv = final_sums(
        [plan(0, 0), qkv_plan],
        [shaped((LAYERS, depth, local), F32), shaped((LAYERS, 3, depth, local), F32)],
        out_q_all + kv_all,
    )
    grad_qkv = grad_qkv.transpose(0, 2, 1, 3)

    norm_parts = []
    for l in range(LAYERS):
        one, two = sums[l][0], sums[l][1]
        norm_parts += [one[0], two[0], one[1], two[2], two[1], two[3]]
    norm_all = jnp.stack(norm_parts)
    bias_all = jnp.concatenate(
        [sums[l][2][0, :local] for l in range(LAYERS)]
        + [sums[l][2][0, 2 * local :] for l in range(LAYERS)]
        + [sums[l][3][0] for l in range(LAYERS)]
    )
    count_norm = norm_all.shape[0]
    by_part = norm_all.reshape(count_norm, nf, nc, depth).transpose(1, 2, 3, 0).reshape(nf, nc, -1)
    norm_total = by_part[0]
    bias_total = bias_all
    size = nc * depth * count_norm
    for bit in range(1, nf):
        came = swap(jnp.concatenate([by_part[bit].reshape(-1), bias_all]), "fsdp", nf, bit)
        norm_total = norm_total + came[:size].reshape(norm_total.shape)
        bias_total = bias_total + came[size:]
    norm_mine = norm_total[0]
    bias_sum = bias_total
    for bit in range(1, nc):
        came = swap(jnp.concatenate([norm_total[bit], bias_total]), "ctx", nc, bit)
        norm_mine = norm_mine + came[: depth * count_norm]
        bias_sum = bias_sum + came[depth * count_norm :]
    norm_mine = (norm_mine + sibling(norm_mine)).reshape(depth, LAYERS, count_norm // LAYERS)
    norm_mine = norm_mine.transpose(1, 0, 2)
    queries, values = bias_sum[: LAYERS * local], bias_sum[LAYERS * local : 2 * LAYERS * local]
    grad_bias = jnp.stack([queries.reshape(LAYERS, local), values.reshape(LAYERS, local)], axis=1)
    grad_up_bias = bias_sum[2 * LAYERS * local :].reshape(LAYERS, hidden)

    return (
        block_output,
        grad_tokens,
        grad_qkv,
        grad_out,
        grad_up,
        grad_down,
        grad_bias,
        grad_up_bias,
        norm_mine[:, :, :2],
        norm_mine[:, :, 2:],
    )


def solution(mesh):
    placed = (
        P(("fsdp", "ctx"), None),
        P(("fsdp", "ctx"), None),
        P("fsdp", None),
        P("fsdp", None),
        P(None, ("fsdp", "ctx"), None, "tp"),
        P(None, ("fsdp", "ctx"), "tp"),
        P(None, ("fsdp", "ctx"), "tp"),
        P(None, ("fsdp", "ctx"), "tp"),
        P(None, None, "tp"),
        P(None, "tp"),
        P(None, ("fsdp", "ctx"), None),
        P(None, ("fsdp", "ctx"), None),
    )
    return jax.shard_map(
        partial(on_device, mesh.shape["fsdp"], mesh.shape["ctx"], mesh.shape["tp"]),
        mesh=mesh,
        in_specs=placed,
        out_specs=(
            P(("fsdp", "ctx"), None),
            P(("fsdp", "ctx"), None),
            P(None, ("fsdp", "ctx"), None, "tp"),
            P(None, ("fsdp", "ctx"), "tp"),
            P(None, ("fsdp", "ctx"), "tp"),
            P(None, ("fsdp", "ctx"), "tp"),
            P(None, None, "tp"),
            P(None, "tp"),
            P(None, ("fsdp", "ctx"), None),
            P(None, ("fsdp", "ctx"), None),
        ),
        check_vma=False,
    )
```

```python
from functools import partial

import jax
import jax.numpy as jnp
from jax import lax
from jax.experimental import pallas as pl
from jax.experimental.pallas import tpu as pltpu
from jax.sharding import PartitionSpec as P

HEADS = 16
HD = 64
BLK = 128
RUN_BLOCKS = 8
LAYERS = 2
NORM_ROWS = 8
NORM_EPS = 1e-05
MASKED = -1000000000.0
QB = 256
GELU_A = 0.7978845608028654
GELU_B = 0.044715
BF = jnp.bfloat16
F32 = jnp.float32
NN = ((1,), (0,))
NT = ((1,), (1,))
VMEM_LIMIT = 40 * 1024 * 1024


def dot(left, right, dims=NN):
    return lax.dot_general(left, right, (dims, ((), ())), preferred_element_type=F32)


def shaped(shape, dtype):
    return jax.ShapeDtypeStruct(shape, dtype)


def whole():
    return pl.BlockSpec(memory_space=pltpu.VMEM)


def params(flops, bytes_accessed, transcendentals=0):
    return dict(
        compiler_params=pltpu.CompilerParams(vmem_limit_bytes=VMEM_LIMIT),
        cost_estimate=pl.CostEstimate(
            flops=int(flops), bytes_accessed=int(bytes_accessed), transcendentals=int(transcendentals)
        ),
    )


def rows_of(order, refs, col, cols, depth, extra=0):
    pieces = []
    if all(ref.shape == refs[0].shape for ref in refs):
        held = refs[0].shape[0] // depth
        for number in range(order.shape[0]):
            start = pl.multiple_of(lax.rem(order[number], held) * depth, depth)
            pieces.append(refs[number // held][pl.ds(start, depth), col : col + cols])
        return jnp.concatenate(pieces, axis=0)
    for ref in refs:
        for start in range(0, ref.shape[0], depth + extra):
            pieces.append(ref[start : start + depth, col : col + cols])
    return jnp.concatenate(pieces, axis=0)


def call(kernel, out_shape, args, flops, scratch=(), transcendentals=0, smem=0):
    outs = out_shape if isinstance(out_shape, (list, tuple)) else [out_shape]
    moved = sum(a.size * a.dtype.itemsize for a in args) + sum(
        o.size * jnp.dtype(o.dtype).itemsize for o in outs
    )
    specs = [pl.BlockSpec(memory_space=pltpu.SMEM)] * smem + [whole()] * (len(args) - smem)
    return pl.pallas_call(
        kernel,
        in_specs=specs,
        out_specs=[whole()] * len(outs) if outs is out_shape else whole(),
        out_shape=out_shape,
        scratch_shapes=list(scratch),
        **params(flops, moved, transcendentals),
    )(*args)


def norm_stats(values):
    average = jnp.mean(values, axis=-1, keepdims=True)
    centred = values - average
    variance = jnp.mean(centred * centred, axis=-1, keepdims=True)
    scale = lax.rsqrt(variance + NORM_EPS)
    return centred * scale, scale


def gelu_parts(u):
    inner = GELU_A * (u + GELU_B * u * u * u)
    t = jnp.tanh(inner)
    return t


def add_norm_kernel(bias_row, gain_row, shift_row, x_ref, a_ref, b_ref, table_ref, y_ref, h_ref):
    branch = a_ref[...].astype(F32) + b_ref[...].astype(F32) + table_ref[bias_row : bias_row + 1, :]
    y = x_ref[...].astype(F32) + branch
    y_ref[...] = y
    n, _ = norm_stats(y)
    h_ref[...] = (
        n * table_ref[gain_row : gain_row + 1, :] + table_ref[shift_row : shift_row + 1, :]
    ).astype(BF)


def add_norm(x, a, b, table, bias_row, gain_row, shift_row):
    rows, width = x.shape
    return call(
        partial(add_norm_kernel, bias_row, gain_row, shift_row),
        [shaped((rows, width), F32), shaped((rows, width), BF)],
        [x, a, b, table],
        rows * width * 12,
    )


def heads_out(out_ref, total, number, row):
    half = total.shape[0]
    turned = total.astype(BF).T
    for j in range(out_ref.shape[0]):
        out_ref[j, row : row + HD, number * half : (number + 1) * half] = turned[j * HD : (j + 1) * HD, :]


def qkv_rows(order, h_refs, bias_ref, w_refs, out_ref, col, depth, extra):
    local = out_ref.shape[0] * HD
    h = jnp.concatenate([h_ref[...] for h_ref in h_refs], axis=0)
    for i in range(3):
        weights = rows_of(order, w_refs, col + i * local, local, depth, extra)
        heads_out(out_ref, dot(h, weights) + bias_ref[i : i + 1, :], 0, i * HD)


def qkv_kernel(col, depth, order, h_own, h_oth, bias_ref, *refs):
    qkv_rows(order, [h_own, h_oth], bias_ref, refs[:-1], refs[-1], col, depth, 0)


def qkv_project(order, h_own, h_oth, bias, pack, col, depth):
    half, width = h_own.shape
    local = bias.shape[1]
    return call(
        partial(qkv_kernel, col, depth),
        shaped((local // HD, 3 * HD, 2 * half), BF),
        [order, h_own, h_oth, bias, *pack],
        12 * half * width * local,
        smem=1,
    )


def first_qkv_kernel(row, depth, extra, order, n_own, n_oth, table_ref, bias_ref, *refs):
    w_refs, (h_own, h_oth, out_ref) = refs[:-3], refs[-3:]
    for n_ref, h_ref in ((n_own, h_own), (n_oth, h_oth)):
        h_ref[...] = (n_ref[...] * table_ref[row : row + 1, :] + table_ref[row + 2 : row + 3, :]).astype(BF)
    qkv_rows(order, [h_own, h_oth], bias_ref, w_refs, out_ref, 0, depth, extra)


def first_qkv(order, n_own, n_oth, table, row, bias, pack, depth, extra):
    half, width = n_own.shape
    local = bias.shape[1]
    return call(
        partial(first_qkv_kernel, row, depth, extra),
        [
            shaped((half, width), BF),
            shaped((half, width), BF),
            shaped((local // HD, 3 * HD, 2 * half), BF),
        ],
        [order, n_own, n_oth, table, bias, *pack],
        12 * half * width * local,
        smem=1,
    )


def out_kernel(col, depth, start, order, o_ref, *refs):
    w_refs, out_ref = refs[:-1], refs[-1]
    half = out_ref.shape[0]
    heads = o_ref.shape[0]
    o = jnp.concatenate([o_ref[j, :, start : start + half] for j in range(heads)], axis=0).T
    weights = rows_of(order, w_refs, col, heads * HD, depth)
    out_ref[...] = dot(o, weights, NT).astype(out_ref.dtype)


def out_project(order, o_rows, pack, col, depth, width, start, dtype):
    heads, _, rows = o_rows.shape
    half = rows // 2
    return call(
        partial(out_kernel, col, depth, start),
        shaped((half, width), dtype),
        [order, o_rows, *pack],
        2 * half * width * heads * HD,
        smem=1,
    )


def mlp_kernel(counts, up_col, down_col, depth, order, h_own, h_oth, bias_ref, *refs):
    ups, downs = refs[: counts[0]], refs[counts[0] : counts[0] + counts[1]]
    u_ref, oth_ref, own_ref = refs[counts[0] + counts[1] :]
    half = h_own.shape[0]
    hidden = u_ref.shape[1]
    h = jnp.concatenate([h_own[...], h_oth[...]], axis=0)
    u = dot(h, rows_of(order, ups, up_col, hidden, depth)) + bias_ref[...]
    u_ref[...] = u
    act = (0.5 * u * (1.0 + gelu_parts(u))).astype(BF)
    total = dot(act, rows_of(order, downs, down_col, hidden, depth), NT)
    own_ref[...] = total[:half, :]
    oth_ref[...] = total[half:, :].astype(BF)


def mlp_forward(order, h_own, h_oth, bias, up, down, depth):
    half, width = h_own.shape
    hidden = bias.shape[1]
    return call(
        partial(mlp_kernel, (len(up[0]), len(down[0])), up[1], down[1], depth),
        [
            shaped((2 * half, hidden), F32),
            shaped((half, width), BF),
            shaped((half, width), F32),
        ],
        [order, h_own, h_oth, bias, *up[0], *down[0]],
        8 * half * width * hidden,
        transcendentals=2 * half * hidden,
        smem=1,
    )


def mlp_back_kernel(counts, up_col, down_col, depth, order, g_own, g_oth, u_ref, *refs):
    ups, downs = refs[: counts[0]], refs[counts[0] : counts[0] + counts[1]]
    act_ref, gu_ref, sum_ref, oth_ref, own_ref = refs[counts[0] + counts[1] :]
    half = g_own.shape[0]
    hidden = u_ref.shape[1]
    g = jnp.concatenate([g_own[...], g_oth[...]], axis=0)
    grad = dot(g, rows_of(order, downs, down_col, hidden, depth))
    u = u_ref[...]
    t = gelu_parts(u)
    act_ref[...] = (0.5 * u * (1.0 + t)).astype(BF)
    slope = 0.5 * (1.0 + t) + 0.5 * u * (1.0 - t * t) * (GELU_A * (1.0 + 3.0 * GELU_B * u * u))
    gu = (grad * slope).astype(BF)
    gu_ref[...] = gu
    sum_ref[...] = jnp.sum(gu.astype(F32), axis=0, keepdims=True)
    total = dot(gu, rows_of(order, ups, up_col, hidden, depth), NT)
    own_ref[...] = total[:half, :]
    oth_ref[...] = total[half:, :].astype(BF)


def mlp_backward(order, g_own, g_oth, u, up, down, depth):
    half, width = g_own.shape
    hidden = u.shape[1]
    return call(
        partial(mlp_back_kernel, (len(up[0]), len(down[0])), up[1], down[1], depth),
        [
            shaped((2 * half, hidden), BF),
            shaped((2 * half, hidden), BF),
            shaped((1, hidden), F32),
            shaped((half, width), BF),
            shaped((half, width), F32),
        ],
        [order, g_own, g_oth, u, *up[0], *down[0]],
        8 * half * width * hidden,
        transcendentals=2 * half * hidden,
        smem=1,
    )


def grads_out(order, out_refs, total, col):
    cols = slice(col, col + total.shape[1])
    if len(out_refs) == 1:
        depth = total.shape[0] // order.shape[0]
        for number in range(order.shape[0]):
            start = pl.multiple_of(order[number] * depth, depth)
            out_refs[0][pl.ds(start, depth), cols] = total[number * depth : (number + 1) * depth].astype(BF)
        return
    span = out_refs[0].shape[0]
    for y, out_ref in enumerate(out_refs):
        out_ref[:, cols] = total[y * span : (y + 1) * span].astype(BF)


def mlp_grad_kernel(order, g_own, g_oth, h_own, h_oth, act_ref, gu_ref, *out_refs):
    hidden = act_ref.shape[1]
    h = jnp.concatenate([h_own[...], h_oth[...]], axis=0).T
    grads_out(order, out_refs, dot(h, gu_ref[...]), 0)
    g = jnp.concatenate([g_own[...], g_oth[...]], axis=0).T
    grads_out(order, out_refs, dot(g, act_ref[...]), hidden)


def mlp_grad(order, g_own, g_oth, h_own, h_oth, act, gu, nf):
    half, width = g_own.shape
    hidden = act.shape[1]
    return call(
        mlp_grad_kernel,
        [shaped((width // nf, 2 * hidden), BF)] * nf,
        [order, g_own, g_oth, h_own, h_oth, act, gu],
        8 * half * width * hidden,
        smem=1,
    )


def attention_grad_kernel(first, last, order, g_own, g_oth, o_ref, h_own, h_oth, p_ref, *out_refs):
    heads = o_ref.shape[0]
    local = heads * HD
    col = 0
    if first == 0:
        g = jnp.concatenate([g_own[...], g_oth[...]], axis=0).T
        o = jnp.concatenate([o_ref[j] for j in range(heads)], axis=0)
        grads_out(order, out_refs, dot(g, o, NT), 0)
        col = local
    h = jnp.concatenate([h_own[...], h_oth[...]], axis=0).T
    grads_out(order, out_refs, dot(h, p_ref[:, (max(first, 1) - 1) * local : (last - 1) * local]), col)


def attention_grad(first, last, order, g_own, g_oth, o_rows, h_own, h_oth, g_proj, nf):
    half, width = g_own.shape
    local = o_rows.shape[0] * HD
    cols = (last - first) * local
    return call(
        partial(attention_grad_kernel, first, last),
        [shaped((width // nf, cols), BF)] * nf,
        [order, g_own, g_oth, o_rows, h_own, h_oth, g_proj],
        4 * half * width * cols,
        smem=1,
    )


def part_sum_kernel(order, own_ref, *refs):
    came, out_ref = refs[:-1], refs[-1]
    slots, depth, _ = out_ref.shape
    for number in range(slots):
        rows = slice(number * depth, (number + 1) * depth)
        total = own_ref[rows, :].astype(F32)
        for ref in came:
            total = total + ref[rows, :].astype(F32)
        out_ref[lax.rem(order[number], slots)] = total.astype(BF)


def part_sum(order, own, came, depth):
    rows, cols = own.shape
    return call(
        part_sum_kernel,
        shaped((rows // depth, depth, cols), BF),
        [order, own, *came],
        rows * cols * 2,
        smem=1,
    )


def final_kernel(plans, *refs):
    outs = refs[-len(plans) :]
    for out_ref, plan in zip(outs, plans):
        cols = out_ref.shape[-1]
        for index, which, col in plan:
            ref = refs[which]
            if len(ref.shape) == 2:
                out_ref[index] = ref[:, col : col + cols].astype(F32)
                continue
            total = ref[0, :, col : col + cols].astype(F32)
            for slot in range(1, ref.shape[0]):
                total = total + ref[slot, :, col : col + cols].astype(F32)
            out_ref[index] = total


def final_sums(plans, shapes, pieces):
    return call(partial(final_kernel, plans), shapes, pieces, sum(p.size for p in pieces))


def norm_back_kernel(gain_row, gx_ref, a_ref, b_ref, y_ref, table_ref, gy_ref, low_ref, sums_ref):
    grad = a_ref[...].astype(F32) + b_ref[...].astype(F32)
    n, scale = norm_stats(y_ref[...].astype(F32))
    e = grad * table_ref[gain_row : gain_row + 1, :]
    mean_e = jnp.mean(e, axis=-1, keepdims=True)
    mean_en = jnp.mean(e * n, axis=-1, keepdims=True)
    gx = gx_ref[...].astype(F32)
    gy = gx + scale * (e - mean_e - n * mean_en)
    gy_ref[...] = gy
    low = gy.astype(BF)
    low_ref[...] = low
    sums_ref[0:1, :] = jnp.sum(grad * n, axis=0, keepdims=True)
    sums_ref[1:2, :] = jnp.sum(grad, axis=0, keepdims=True)
    sums_ref[2:3, :] = jnp.sum(low.astype(F32), axis=0, keepdims=True)
    sums_ref[3:4, :] = jnp.sum(gx.astype(BF).astype(F32), axis=0, keepdims=True)
    sums_ref[4:, :] = jnp.zeros((4, gx.shape[1]), F32)


def norm_backward(gx, a, b, y, table, gain_row):
    rows, width = gx.shape
    return call(
        partial(norm_back_kernel, gain_row),
        [shaped((rows, width), F32), shaped((rows, width), BF), shaped((8, width), F32)],
        [gx, a, b, y, table],
        rows * width * 25,
    )


def out_back_kernel(col, depth, order, g_own, g_oth, *refs):
    w_refs, out_ref = refs[:-1], refs[-1]
    g = jnp.concatenate([g_own[...], g_oth[...]], axis=0)
    heads_out(out_ref, dot(g, rows_of(order, w_refs, col, out_ref.shape[0] * HD, depth)), 0, 0)


def out_backward(order, g_own, g_oth, pack, col, depth, local):
    half, width = g_own.shape
    return call(
        partial(out_back_kernel, col, depth),
        shaped((local // HD, HD, 2 * half), BF),
        [order, g_own, g_oth, *pack],
        4 * half * width * local,
        smem=1,
    )


def qkv_back_kernel(col, depth, extra, order, g_ref, *refs):
    w_refs, (rows_ref, sum_ref, oth_ref, own_ref) = refs[:-4], refs[-4:]
    heads = g_ref.shape[0]
    half = own_ref.shape[0]
    local = heads * HD
    planes = [
        jnp.concatenate([g_ref[j, i * HD : (i + 1) * HD, :] for j in range(heads)], axis=0).T
        for i in range(3)
    ]
    grads = jnp.concatenate(planes, axis=1)
    rows_ref[...] = grads
    total = dot(grads, rows_of(order, w_refs, col, 3 * local, depth, extra), NT)
    oth_ref[...] = total[half:].astype(BF)
    own_ref[...] = total[:half]
    sum_ref[...] = jnp.sum(grads.astype(F32), axis=0, keepdims=True)


def qkv_backward(order, g, pack, col, depth, extra, width):
    heads, _, rows = g.shape
    half = rows // 2
    cols = 3 * heads * HD
    return call(
        partial(qkv_back_kernel, col, depth, extra),
        [
            shaped((rows, cols), BF),
            shaped((1, cols), F32),
            shaped((half, width), BF),
            shaped((half, width), F32),
        ],
        [order, g, *pack],
        2 * rows * width * cols,
        smem=1,
    )


def gather_blocks(source_ref, src_ref, dest_ref, per_device):
    for s in range(dest_ref.shape[1] // BLK):
        src = src_ref[s]
        z = src // per_device
        start = pl.multiple_of((src - z * per_device) * BLK, BLK)
        dest_ref[:, s * BLK : (s + 1) * BLK] = source_ref[z, :, pl.ds(start, BLK)]


def scatter_blocks(dest_ref, src_ref, source, per_device, low, first):
    depth, columns = source.shape
    for s in range(columns // BLK):
        src = src_ref[first + s]
        z = src // per_device
        start = pl.multiple_of((src - z * per_device) * BLK, BLK)
        dest_ref[z, low : low + depth, pl.ds(start, BLK)] = source[:, s * BLK : (s + 1) * BLK]


def segment_columns(seg_ref, column_ref):
    for s in range(seg_ref.shape[1] // BLK):
        row = seg_ref[:, s * BLK : (s + 1) * BLK]
        row = jnp.where(row < 0, -2, row).astype(F32)
        column_ref[s * BLK : (s + 1) * BLK, :] = jnp.broadcast_to(row, (BLK, BLK)).T


def score_tile(keys, queries, column_ref, seg_ref, slope, base, first, last):
    depth = keys.shape[0]
    width = last - first
    scores = dot(keys, queries)
    key_row = lax.broadcasted_iota(jnp.int32, (depth, width), 0)
    query_row = lax.broadcasted_iota(jnp.int32, (depth, width), 1) + (first - base)
    distance = query_row - key_row
    scores = scores - slope * distance.astype(F32)
    columns = column_ref[base : base + depth, :]
    key_seg = jnp.concatenate([columns] * (width // BLK), axis=1)
    query_seg = seg_ref[:, first:last].astype(F32)
    allowed = ((key_seg == query_seg) & (distance >= 0)) | (distance == 0)
    return scores, allowed


def attend_kernel(per_device, src_ref, slope_ref, seg_ref, qkv_ref, o_ref, lse_ref, stream_ref, column_ref):
    gather_blocks(qkv_ref, src_ref, stream_ref, per_device)
    segment_columns(seg_ref, column_ref)
    slope = slope_ref[0]
    run = RUN_BLOCKS * BLK
    for base in range(0, stream_ref.shape[1], run):
        keys = stream_ref[HD : 2 * HD, base : base + run].T
        for first in range(base, base + run, QB):
            last = first + QB
            depth = last - base
            queries = stream_ref[:HD, first:last] * jnp.asarray(HD**-0.5, BF)
            scores, allowed = score_tile(
                keys[:depth], queries, column_ref, seg_ref, slope, base, first, last
            )
            scores = jnp.where(allowed, scores, MASKED)
            top = jnp.max(scores, axis=0, keepdims=True)
            weights = jnp.exp(scores - top)
            total = jnp.sum(weights, axis=0, keepdims=True)
            lse_ref[:, first:last] = top + jnp.log(total)
            values = stream_ref[2 * HD :, base : base + depth]
            out = (dot(values, weights.astype(BF)) / total).astype(BF)
            scatter_blocks(o_ref, src_ref, out, per_device, 0, first // BLK)


def attend(qkv, source, slope, segments):
    nc, depth, rows = qkv.shape
    length = nc * rows
    smem = pl.BlockSpec(memory_space=pltpu.SMEM)
    return pl.pallas_call(
        partial(attend_kernel, rows // BLK),
        in_specs=[smem, smem, whole(), whole()],
        out_specs=[whole(), whole()],
        out_shape=[shaped((nc, HD, rows), BF), shaped((1, length), F32)],
        scratch_shapes=[pltpu.VMEM((3 * HD, length), BF), pltpu.VMEM((length, BLK), F32)],
        **params(length * RUN_BLOCKS * BLK * HD * 3, length * HD * 8, length * RUN_BLOCKS * BLK // 2),
    )(source, slope, segments, qkv)


def attend_back_kernel(
    per_device, src_ref, slope_ref, seg_ref, qkv_ref, g_ref, lse_ref, out_ref, stream_ref, grad_ref, column_ref, k_acc, v_acc
):
    gather_blocks(qkv_ref, src_ref, stream_ref, per_device)
    gather_blocks(g_ref, src_ref, grad_ref, per_device)
    segment_columns(seg_ref, column_ref)
    slope = slope_ref[0]
    run = RUN_BLOCKS * BLK
    scale = HD**-0.5
    for base in range(0, stream_ref.shape[1], run):
        rows = slice(base, base + run)
        keys_turned = stream_ref[HD : 2 * HD, rows]
        keys = keys_turned.T
        values = stream_ref[2 * HD :, rows].T
        queries_rows = stream_ref[:HD, rows].T
        grads_rows = grad_ref[:, rows].T
        for first in range(base + run - QB, base - 1, -QB):
            last = first + QB
            depth = last - base
            inner = slice(first - base, last - base)
            queries = stream_ref[:HD, first:last] * jnp.asarray(scale, BF)
            scores, allowed = score_tile(
                keys[:depth], queries, column_ref, seg_ref, slope, base, first, last
            )
            weights = jnp.where(allowed, jnp.exp(scores - lse_ref[:, first:last]), 0.0)
            back = dot(values[:depth], grad_ref[:, first:last])
            delta = jnp.sum(weights * back, axis=0, keepdims=True)
            low = (weights * (back - delta)).astype(BF)
            v_piece = dot(weights.astype(BF), grads_rows[inner])
            k_piece = dot(low, queries_rows[inner])
            if depth == run:
                v_acc[...] = v_piece
                k_acc[...] = k_piece
            else:
                v_acc[:depth, :] += v_piece
                k_acc[:depth, :] += k_piece
            q_grad = (dot(keys_turned[:, :depth], low) * scale).astype(BF)
            scatter_blocks(out_ref, src_ref, q_grad, per_device, 0, first // BLK)
        scatter_blocks(out_ref, src_ref, (k_acc[...] * scale).T.astype(BF), per_device, HD, base // BLK)
        scatter_blocks(out_ref, src_ref, v_acc[...].T.astype(BF), per_device, 2 * HD, base // BLK)


def attend_backward(qkv, grads, lse, source, slope, segments):
    nc, depth, rows = qkv.shape
    length = nc * rows
    run = RUN_BLOCKS * BLK
    smem = pl.BlockSpec(memory_space=pltpu.SMEM)
    return pl.pallas_call(
        partial(attend_back_kernel, rows // BLK),
        in_specs=[smem, smem, whole(), whole(), whole(), whole()],
        out_specs=whole(),
        out_shape=shaped((nc, depth, rows), BF),
        scratch_shapes=[
            pltpu.VMEM((3 * HD, length), BF),
            pltpu.VMEM((HD, length), BF),
            pltpu.VMEM((length, BLK), F32),
            pltpu.VMEM((run, HD), F32),
            pltpu.VMEM((run, HD), F32),
        ],
        **params(length * run * HD * 7, length * HD * 16, length * run // 2),
    )(source, slope, segments, qkv, grads, lse)


def on_device(
    nf,
    nc,
    nt,
    tokens,
    cotangent,
    block_place,
    segment_ids,
    qkv_weight,
    out_weight,
    up_weight,
    down_weight,
    query_value_bias,
    up_bias,
    norm_gains,
    row_biases,
):
    rows, width = tokens.shape
    half = rows // 2
    depth = qkv_weight.shape[1]
    local = qkv_weight.shape[3]
    heads = local // HD
    hidden = up_weight.shape[2]
    span = nc * depth
    y_index = lax.axis_index("fsdp")
    z_index = lax.axis_index("ctx")
    t_index = lax.axis_index("tp")
    side = t_index % 2

    def swap(value, axis, size, bit):
        return lax.ppermute(value, axis, [(i, i ^ bit) for i in range(size)])

    def sibling(value):
        return swap(value, "tp", nt, 1)

    def across(value):
        return lax.all_to_all(value, "ctx", 0, 0)

    def tie(value, *others):
        return lax.optimization_barrier((value, *others))[0]

    def gather_z(shard, doubling=False):
        if not doubling:
            return [swap(shard, "ctx", nc, bit) for bit in range(1, nc)]
        came, bit = [], 1
        while bit < nc:
            came.append(swap(jnp.concatenate([shard, *came], axis=0) if came else shard, "ctx", nc, bit))
            bit *= 2
        return came

    def gather_y(shard, came, apart=False):
        pack = [shard, *came]
        for bit in range(1, nf):
            if apart:
                pack.append(swap(shard, "fsdp", nf, bit))
                pack.append(swap(jnp.concatenate(came, axis=0), "fsdp", nf, bit))
            else:
                pack.append(swap(jnp.concatenate([shard, *came], axis=0), "fsdp", nf, bit))
        return pack

    def whole_gather(shard):
        return lax.all_gather(shard, ("fsdp", "ctx"), axis=0, tiled=True)

    def whole_scatter(total):
        return lax.psum_scatter(total, ("fsdp", "ctx"), scatter_dimension=0, tiled=True)

    def send_y(parts):
        return [swap(parts[bit], "fsdp", nf, bit) for bit in range(1, nf)]

    def reduce_z(parts, came, *others):
        return across(part_sum(order, tie(parts[0], *others), came, depth))

    def tensor_sum(other, own):
        term = (own + sibling(other).astype(F32)).astype(BF)
        bit = 2
        while bit * 2 < nt:
            term = (term.astype(F32) + swap(term, "tp", nt, bit).astype(F32)).astype(BF)
            bit *= 2
        return term, swap(term, "tp", nt, bit)

    def columns_relative(value):
        return jnp.concatenate(
            [
                lax.dynamic_slice_in_dim(
                    value, ((y_index ^ a) * nc + (z_index ^ b)) * depth, depth, axis=1
                )
                for a in range(nf)
                for b in range(nc)
            ],
            axis=1,
        )

    def take_half(value, which):
        return lax.dynamic_slice_in_dim(value, which * half, half)

    def columns_canonical(own, oth):
        rows_all = jnp.where(
            side == 0, jnp.concatenate([own, oth], axis=0), jnp.concatenate([oth, own], axis=0)
        )
        return columns_relative(rows_all)

    per_device = rows // BLK
    count = nc * per_device
    place = block_place[0]
    stored = jnp.arange(count, dtype=jnp.int32)
    relative = (stored // per_device) * per_device + (stored % per_device + side * (per_device // 2)) % per_device
    source = jnp.sum(
        jnp.where(place[None, :] == jnp.arange(count, dtype=jnp.int32)[:, None], relative[None, :], 0), axis=1
    ).astype(jnp.int32)
    head = (t_index * heads + z_index).astype(F32)
    slope = jnp.exp2(-8.0 * (head + 1.0) / HEADS).reshape(1)
    segments = segment_ids
    order = jnp.stack(
        [(y_index ^ a) * nc + (z_index ^ b) for a in range(nf) for b in range(nc)]
    ).astype(jnp.int32)

    def qkv_shard(layer):
        return [qkv_weight[layer, :, i, :] for i in range(3)]

    table_rows = []
    for layer in range(LAYERS):
        table_rows += [norm_gains[layer].T, row_biases[layer].T, jnp.zeros((2, depth), BF)]
    table_shard = jnp.concatenate(table_rows, axis=0)
    extra = table_shard.shape[0]
    table_padded = jnp.pad(table_shard, ((0, 0), (0, 3 * local - depth)))
    first_shard = jnp.concatenate([jnp.concatenate(qkv_shard(0), axis=1), table_padded], axis=0)
    first_z = gather_z(first_shard)
    first_pack = gather_y(first_shard, first_z, apart=True)
    table = jnp.concatenate(
        [
            ref[start + depth : start + depth + extra, :depth]
            for ref in first_pack
            for start in range(0, ref.shape[0], depth + extra)
        ],
        axis=1,
    ).astype(F32)

    biases = [
        jnp.stack([query_value_bias[l, 0], jnp.zeros((local,), BF), query_value_bias[l, 1]]).astype(F32)
        for l in range(LAYERS)
    ]
    up_biases = [up_bias[l].astype(F32).reshape(1, hidden) for l in range(LAYERS)]

    x_all = columns_relative(tokens)
    x_half = take_half(x_all, side)
    n_own = norm_stats(x_half.astype(F32))[0]
    n_oth = norm_stats(take_half(x_all, 1 - side).astype(F32))[0]
    h_own, h_oth, qkv_sent = first_qkv(order, n_own, n_oth, table, 0, biases[0], first_pack, depth, extra)

    out_up_shard = tie(jnp.concatenate([out_weight[0], up_weight[0]], axis=1), *first_z)
    out_up_z = gather_z(out_up_shard)
    out_up = gather_y(out_up_shard, out_up_z)
    out_packs, qkv_packs, up_packs = [(out_up, 0)], [(first_pack, 0, extra)], [(out_up, local)]
    shared = whole_gather(
        tie(jnp.concatenate([down_weight[0], out_weight[1], *qkv_shard(1)], axis=1), *first_z)
    )
    down_packs = [([shared], 0)]
    out_packs.append(([shared], hidden))
    qkv_packs.append(([shared], hidden + local, 0))

    records = []
    last_other = last_own = None
    for l in range(LAYERS):
        row = l * NORM_ROWS
        qkv = across(qkv_sent)
        if l == 0:
            next_mlp = whole_gather(
                tie(jnp.concatenate([up_weight[1], down_weight[1]], axis=1), shared)
            )
            up_packs.append(([next_mlp], 0))
            down_packs.append(([next_mlp], hidden))
        o_stream, lse = attend(qkv, source, slope, segments)
        o_rows = across(o_stream)
        if l == 0:
            pass
        other = out_project(order, o_rows, *out_packs[l], depth, width, half, BF)
        own = out_project(order, tie(o_rows, other), *out_packs[l], depth, width, 0, F32)
        a, b = tensor_sum(other, own)
        y_half, h2_own = add_norm(x_half, a, b, table, row + 3, row + 1, row + 4)
        h2_oth = sibling(h2_own)
        u, other, own = mlp_forward(order, h2_own, h2_oth, up_biases[l], up_packs[l], down_packs[l], depth)
        records.append((x_half, h_own, h_oth, qkv, lse, o_rows, y_half, h2_own, h2_oth, u))
        if l + 1 < LAYERS:
            a, b = tensor_sum(other, own)
            following = row + NORM_ROWS
            x_half, h_own = add_norm(y_half, a, b, table, row + 5, following, following + 2)
            h_oth = sibling(h_own)
            qkv_sent = qkv_project(order, h_own, h_oth, biases[l + 1], *qkv_packs[l + 1][:2], depth)
        else:
            last_other, last_own = other, own

    g_all = columns_relative(cotangent)
    gz_own, gz_oth = take_half(g_all, side), take_half(g_all, 1 - side)
    gx_half = gz_own.astype(F32)
    sums = [None] * LAYERS
    mlp_pieces = [None] * LAYERS
    above = None
    for l in reversed(range(LAYERS)):
        row = l * NORM_ROWS
        x_half, h_own, h_oth, qkv, lse, o_rows, y_half, h2_own, h2_oth, u = records[l]
        act, gu, up_sum, other, own = mlp_backward(order, gz_own, gz_oth, u, up_packs[l], down_packs[l], depth)
        a, b = tensor_sum(other, own)
        parts = mlp_grad(order, gz_own, gz_oth, h2_own, h2_oth, tie(act, a), gu, 1)
        b = tie(b, *parts)
        mlp_pieces[l] = whole_scatter(parts[0])
        gy_half, ga_own, sums_two = norm_backward(gx_half, a, b, y_half, table, row + 1)
        ga_oth = sibling(ga_own)
        g_stream = across(out_backward(order, ga_own, ga_oth, *out_packs[l], depth, local))
        if l == LAYERS - 1:
            a, b = tensor_sum(tie(last_other, g_stream), last_own)
            final_half = y_half + (a.astype(F32) + b.astype(F32) + table[row + 5])
            final_low = final_half.astype(BF)
            block_output = columns_canonical(final_low, sibling(final_low))
        g_sent = attend_backward(qkv, g_stream, lse, source, slope, segments)
        g_rows = across(g_sent)
        if l < LAYERS - 1:
            above = reduce_z(*above, g_rows)
        g_proj, qkv_sum, other, own = qkv_backward(
            order, g_rows, qkv_packs[l][0], qkv_packs[l][1], depth, qkv_packs[l][2], width
        )
        a, b = tensor_sum(other, own)
        sources = (order, ga_own, ga_oth, o_rows, h_own, h_oth)
        if l == LAYERS - 1:
            attn = attention_grad(0, 4, *sources, tie(g_proj, a), nf)
            above = (attn, send_y(attn))
            b = tie(b, *attn)
        else:
            out_q = attention_grad(0, 2, *sources, g_proj, nf)
            out_q_came = send_y(out_q)
            kv = attention_grad(2, 4, *sources, tie(g_proj, *out_q), nf)
            kv_came = send_y(kv)
            b = tie(b, *kv)
        gx_half, gz_own, sums_one = norm_backward(gy_half, a, b, x_half, table, row)
        if l > 0:
            gz_oth = sibling(gz_own)
        sums[l] = (sums_one, sums_two, qkv_sum, up_sum)
    out_q_pieces = reduce_z(out_q, out_q_came, above)
    kv_pieces = reduce_z(kv, kv_came, out_q_pieces)

    grad_tokens = columns_canonical(gx_half, sibling(gx_half))

    grad_up, grad_down = final_sums(
        [[(l, l, col) for l in range(LAYERS)] for col in (0, hidden)],
        [shaped((LAYERS, depth, hidden), F32)] * 2,
        mlp_pieces,
    )
    qkv_plan = [((1, i), 2, (i + 1) * local) for i in range(3)]
    qkv_plan += [((0, 0), 0, local), ((0, 1), 1, 0), ((0, 2), 1, local)]
    grad_out, grad_qkv = final_sums(
        [[(0, 0, 0), (1, 2, 0)], qkv_plan],
        [shaped((LAYERS, depth, local), F32), shaped((LAYERS, 3, depth, local), F32)],
        [out_q_pieces, kv_pieces, above],
    )
    grad_qkv = grad_qkv.transpose(0, 2, 1, 3)

    norm_parts = []
    for l in range(LAYERS):
        one, two = sums[l][0], sums[l][1]
        norm_parts += [one[0], two[0], one[1], two[2], two[1], two[3]]
    norm_all = jnp.stack(norm_parts)
    bias_all = jnp.concatenate(
        [sums[l][2][0, :local] for l in range(LAYERS)]
        + [sums[l][2][0, 2 * local :] for l in range(LAYERS)]
        + [sums[l][3][0] for l in range(LAYERS)]
    )
    count_norm = norm_all.shape[0]
    by_part = norm_all.reshape(count_norm, nf, nc, depth).transpose(1, 2, 3, 0).reshape(nf, nc, -1)
    norm_total = by_part[0]
    bias_total = bias_all
    size = nc * depth * count_norm
    for bit in range(1, nf):
        came = swap(jnp.concatenate([by_part[bit].reshape(-1), bias_all]), "fsdp", nf, bit)
        norm_total = norm_total + came[:size].reshape(norm_total.shape)
        bias_total = bias_total + came[size:]
    norm_mine = norm_total[0]
    bias_sum = bias_total
    for bit in range(1, nc):
        came = swap(jnp.concatenate([norm_total[bit], bias_total]), "ctx", nc, bit)
        norm_mine = norm_mine + came[: depth * count_norm]
        bias_sum = bias_sum + came[depth * count_norm :]
    norm_mine = (norm_mine + sibling(norm_mine)).reshape(depth, LAYERS, count_norm // LAYERS)
    norm_mine = norm_mine.transpose(1, 0, 2)
    queries, values = bias_sum[: LAYERS * local], bias_sum[LAYERS * local : 2 * LAYERS * local]
    grad_bias = jnp.stack([queries.reshape(LAYERS, local), values.reshape(LAYERS, local)], axis=1)
    grad_up_bias = bias_sum[2 * LAYERS * local :].reshape(LAYERS, hidden)

    return (
        block_output,
        grad_tokens,
        grad_qkv,
        grad_out,
        grad_up,
        grad_down,
        grad_bias,
        grad_up_bias,
        norm_mine[:, :, :2],
        norm_mine[:, :, 2:],
    )


def solution(mesh):
    placed = (
        P(("fsdp", "ctx"), None),
        P(("fsdp", "ctx"), None),
        P("fsdp", None),
        P("fsdp", None),
        P(None, ("fsdp", "ctx"), None, "tp"),
        P(None, ("fsdp", "ctx"), "tp"),
        P(None, ("fsdp", "ctx"), "tp"),
        P(None, ("fsdp", "ctx"), "tp"),
        P(None, None, "tp"),
        P(None, "tp"),
        P(None, ("fsdp", "ctx"), None),
        P(None, ("fsdp", "ctx"), None),
    )
    return jax.shard_map(
        partial(on_device, mesh.shape["fsdp"], mesh.shape["ctx"], mesh.shape["tp"]),
        mesh=mesh,
        in_specs=placed,
        out_specs=(
            P(("fsdp", "ctx"), None),
            P(("fsdp", "ctx"), None),
            P(None, ("fsdp", "ctx"), None, "tp"),
            P(None, ("fsdp", "ctx"), "tp"),
            P(None, ("fsdp", "ctx"), "tp"),
            P(None, ("fsdp", "ctx"), "tp"),
            P(None, None, "tp"),
            P(None, "tp"),
            P(None, ("fsdp", "ctx"), None),
            P(None, ("fsdp", "ctx"), None),
        ),
        check_vma=False,
    )
```

```python
from functools import partial

import jax
import jax.numpy as jnp
from jax import lax
from jax.experimental import pallas as pl
from jax.experimental.pallas import tpu as pltpu
from jax.sharding import PartitionSpec as P

HEADS = 16
HD = 64
BLK = 128
RUN_BLOCKS = 8
LAYERS = 2
NORM_ROWS = 8
NORM_EPS = 1e-05
MASKED = -1000000000.0
QB = 256
GELU_A = 0.7978845608028654
GELU_B = 0.044715
BF = jnp.bfloat16
F32 = jnp.float32
NN = ((1,), (0,))
NT = ((1,), (1,))
VMEM_LIMIT = 40 * 1024 * 1024


def dot(left, right, dims=NN):
    return lax.dot_general(left, right, (dims, ((), ())), preferred_element_type=F32)


def shaped(shape, dtype):
    return jax.ShapeDtypeStruct(shape, dtype)


def whole():
    return pl.BlockSpec(memory_space=pltpu.VMEM)


def params(flops, bytes_accessed, transcendentals=0):
    return dict(
        compiler_params=pltpu.CompilerParams(vmem_limit_bytes=VMEM_LIMIT),
        cost_estimate=pl.CostEstimate(
            flops=int(flops), bytes_accessed=int(bytes_accessed), transcendentals=int(transcendentals)
        ),
    )


def rows_of(order, refs, col, cols, depth, extra=0):
    pieces = []
    if all(ref.shape == refs[0].shape for ref in refs):
        held = refs[0].shape[0] // depth
        for number in range(order.shape[0]):
            start = pl.multiple_of(lax.rem(order[number], held) * depth, depth)
            pieces.append(refs[number // held][pl.ds(start, depth), col : col + cols])
        return jnp.concatenate(pieces, axis=0)
    for ref in refs:
        for start in range(0, ref.shape[0], depth + extra):
            pieces.append(ref[start : start + depth, col : col + cols])
    return jnp.concatenate(pieces, axis=0)


def call(kernel, out_shape, args, flops, scratch=(), transcendentals=0, smem=0):
    outs = out_shape if isinstance(out_shape, (list, tuple)) else [out_shape]
    moved = sum(a.size * a.dtype.itemsize for a in args) + sum(
        o.size * jnp.dtype(o.dtype).itemsize for o in outs
    )
    specs = [pl.BlockSpec(memory_space=pltpu.SMEM)] * smem + [whole()] * (len(args) - smem)
    return pl.pallas_call(
        kernel,
        in_specs=specs,
        out_specs=[whole()] * len(outs) if outs is out_shape else whole(),
        out_shape=out_shape,
        scratch_shapes=list(scratch),
        **params(flops, moved, transcendentals),
    )(*args)


def norm_stats(values):
    average = jnp.mean(values, axis=-1, keepdims=True)
    centred = values - average
    variance = jnp.mean(centred * centred, axis=-1, keepdims=True)
    scale = lax.rsqrt(variance + NORM_EPS)
    return centred * scale, scale


def gelu_parts(u):
    inner = GELU_A * (u + GELU_B * u * u * u)
    t = jnp.tanh(inner)
    return t


def add_norm_kernel(bias_row, gain_row, shift_row, x_ref, a_ref, b_ref, table_ref, y_ref, h_ref):
    branch = a_ref[...].astype(F32) + b_ref[...].astype(F32) + table_ref[bias_row : bias_row + 1, :]
    y = x_ref[...].astype(F32) + branch
    y_ref[...] = y
    n, _ = norm_stats(y)
    h_ref[...] = (
        n * table_ref[gain_row : gain_row + 1, :] + table_ref[shift_row : shift_row + 1, :]
    ).astype(BF)


def add_norm(x, a, b, table, bias_row, gain_row, shift_row):
    rows, width = x.shape
    return call(
        partial(add_norm_kernel, bias_row, gain_row, shift_row),
        [shaped((rows, width), F32), shaped((rows, width), BF)],
        [x, a, b, table],
        rows * width * 12,
    )


def heads_out(out_ref, total, number, row):
    half = total.shape[0]
    turned = total.astype(BF).T
    for j in range(out_ref.shape[0]):
        out_ref[j, row : row + HD, number * half : (number + 1) * half] = turned[j * HD : (j + 1) * HD, :]


def qkv_rows(order, h_refs, bias_ref, w_refs, out_ref, col, depth, extra):
    local = out_ref.shape[0] * HD
    h = jnp.concatenate([h_ref[...] for h_ref in h_refs], axis=0)
    for i in range(3):
        weights = rows_of(order, w_refs, col + i * local, local, depth, extra)
        heads_out(out_ref, dot(h, weights) + bias_ref[i : i + 1, :], 0, i * HD)


def qkv_kernel(col, depth, order, h_own, h_oth, bias_ref, *refs):
    qkv_rows(order, [h_own, h_oth], bias_ref, refs[:-1], refs[-1], col, depth, 0)


def qkv_project(order, h_own, h_oth, bias, pack, col, depth):
    half, width = h_own.shape
    local = bias.shape[1]
    return call(
        partial(qkv_kernel, col, depth),
        shaped((local // HD, 3 * HD, 2 * half), BF),
        [order, h_own, h_oth, bias, *pack],
        12 * half * width * local,
        smem=1,
    )


def first_qkv_kernel(row, depth, extra, order, n_own, n_oth, table_ref, bias_ref, *refs):
    w_refs, (h_own, h_oth, out_ref) = refs[:-3], refs[-3:]
    for n_ref, h_ref in ((n_own, h_own), (n_oth, h_oth)):
        h_ref[...] = (n_ref[...] * table_ref[row : row + 1, :] + table_ref[row + 2 : row + 3, :]).astype(BF)
    qkv_rows(order, [h_own, h_oth], bias_ref, w_refs, out_ref, 0, depth, extra)


def first_qkv(order, n_own, n_oth, table, row, bias, pack, depth, extra):
    half, width = n_own.shape
    local = bias.shape[1]
    return call(
        partial(first_qkv_kernel, row, depth, extra),
        [
            shaped((half, width), BF),
            shaped((half, width), BF),
            shaped((local // HD, 3 * HD, 2 * half), BF),
        ],
        [order, n_own, n_oth, table, bias, *pack],
        12 * half * width * local,
        smem=1,
    )


def out_kernel(col, depth, start, order, o_ref, *refs):
    w_refs, out_ref = refs[:-1], refs[-1]
    half = out_ref.shape[0]
    heads = o_ref.shape[0]
    o = jnp.concatenate([o_ref[j, :, start : start + half] for j in range(heads)], axis=0).T
    weights = rows_of(order, w_refs, col, heads * HD, depth)
    out_ref[...] = dot(o, weights, NT).astype(out_ref.dtype)


def out_project(order, o_rows, pack, col, depth, width, start, dtype):
    heads, _, rows = o_rows.shape
    half = rows // 2
    return call(
        partial(out_kernel, col, depth, start),
        shaped((half, width), dtype),
        [order, o_rows, *pack],
        2 * half * width * heads * HD,
        smem=1,
    )


def mlp_kernel(counts, up_col, down_col, depth, order, h_own, h_oth, bias_ref, *refs):
    ups, downs = refs[: counts[0]], refs[counts[0] : counts[0] + counts[1]]
    u_ref, oth_ref, own_ref = refs[counts[0] + counts[1] :]
    half = h_own.shape[0]
    hidden = u_ref.shape[1]
    h = jnp.concatenate([h_own[...], h_oth[...]], axis=0)
    u = dot(h, rows_of(order, ups, up_col, hidden, depth)) + bias_ref[...]
    u_ref[...] = u
    act = (0.5 * u * (1.0 + gelu_parts(u))).astype(BF)
    total = dot(act, rows_of(order, downs, down_col, hidden, depth), NT)
    own_ref[...] = total[:half, :]
    oth_ref[...] = total[half:, :].astype(BF)


def mlp_forward(order, h_own, h_oth, bias, up, down, depth):
    half, width = h_own.shape
    hidden = bias.shape[1]
    return call(
        partial(mlp_kernel, (len(up[0]), len(down[0])), up[1], down[1], depth),
        [
            shaped((2 * half, hidden), F32),
            shaped((half, width), BF),
            shaped((half, width), F32),
        ],
        [order, h_own, h_oth, bias, *up[0], *down[0]],
        8 * half * width * hidden,
        transcendentals=2 * half * hidden,
        smem=1,
    )


def mlp_back_kernel(counts, up_col, down_col, depth, order, g_own, g_oth, u_ref, *refs):
    ups, downs = refs[: counts[0]], refs[counts[0] : counts[0] + counts[1]]
    act_ref, gu_ref, sum_ref, oth_ref, own_ref = refs[counts[0] + counts[1] :]
    half = g_own.shape[0]
    hidden = u_ref.shape[1]
    g = jnp.concatenate([g_own[...], g_oth[...]], axis=0)
    grad = dot(g, rows_of(order, downs, down_col, hidden, depth))
    u = u_ref[...]
    t = gelu_parts(u)
    act_ref[...] = (0.5 * u * (1.0 + t)).astype(BF)
    slope = 0.5 * (1.0 + t) + 0.5 * u * (1.0 - t * t) * (GELU_A * (1.0 + 3.0 * GELU_B * u * u))
    gu = (grad * slope).astype(BF)
    gu_ref[...] = gu
    sum_ref[...] = jnp.sum(gu.astype(F32), axis=0, keepdims=True)
    total = dot(gu, rows_of(order, ups, up_col, hidden, depth), NT)
    own_ref[...] = total[:half, :]
    oth_ref[...] = total[half:, :].astype(BF)


def mlp_backward(order, g_own, g_oth, u, up, down, depth):
    half, width = g_own.shape
    hidden = u.shape[1]
    return call(
        partial(mlp_back_kernel, (len(up[0]), len(down[0])), up[1], down[1], depth),
        [
            shaped((2 * half, hidden), BF),
            shaped((2 * half, hidden), BF),
            shaped((1, hidden), F32),
            shaped((half, width), BF),
            shaped((half, width), F32),
        ],
        [order, g_own, g_oth, u, *up[0], *down[0]],
        8 * half * width * hidden,
        transcendentals=2 * half * hidden,
        smem=1,
    )


def grads_out(order, out_refs, total, col):
    cols = slice(col, col + total.shape[1])
    if len(out_refs) == 1:
        depth = total.shape[0] // order.shape[0]
        for number in range(order.shape[0]):
            start = pl.multiple_of(order[number] * depth, depth)
            out_refs[0][pl.ds(start, depth), cols] = total[number * depth : (number + 1) * depth].astype(BF)
        return
    span = out_refs[0].shape[0]
    for y, out_ref in enumerate(out_refs):
        out_ref[:, cols] = total[y * span : (y + 1) * span].astype(BF)


def late_grad_kernel(count, order, *refs):
    g_own, g_oth, h_own, h_oth, act_ref, gu_ref = refs[:6]
    out_refs = refs[count:]
    hidden = act_ref.shape[1]
    h = jnp.concatenate([h_own[...], h_oth[...]], axis=0).T
    grads_out(order, out_refs, dot(h, gu_ref[...]), 0)
    g = jnp.concatenate([g_own[...], g_oth[...]], axis=0).T
    grads_out(order, out_refs, dot(g, act_ref[...]), hidden)
    if count > 6:
        attention_grad_body(0, 4, 2 * hidden, order, *refs[6:count], out_refs)


def late_grad(order, mlp, attention):
    half, width = mlp[0].shape
    cols = 2 * mlp[4].shape[1]
    if attention:
        cols += 4 * attention[2].shape[0] * HD
    args = [*mlp, *attention]
    return call(
        partial(late_grad_kernel, len(args)),
        [shaped((width, cols), BF)],
        [order, *args],
        4 * half * width * cols,
        smem=1,
    )[0]


def attention_grad_body(first, last, col, order, g_own, g_oth, o_ref, h_own, h_oth, p_ref, out_refs):
    heads = o_ref.shape[0]
    local = heads * HD
    if first == 0:
        g = jnp.concatenate([g_own[...], g_oth[...]], axis=0).T
        o = jnp.concatenate([o_ref[j] for j in range(heads)], axis=0)
        grads_out(order, out_refs, dot(g, o, NT), col)
        col += local
        first = 1
    h = jnp.concatenate([h_own[...], h_oth[...]], axis=0).T
    grads_out(order, out_refs, dot(h, p_ref[:, (first - 1) * local : (last - 1) * local]), col)


def attention_grad_kernel(first, last, order, *refs):
    attention_grad_body(first, last, 0, order, *refs[:6], refs[6:])


def attention_grad(first, last, order, g_own, g_oth, o_rows, h_own, h_oth, g_proj, nf):
    half, width = g_own.shape
    local = o_rows.shape[0] * HD
    cols = (last - first) * local
    return call(
        partial(attention_grad_kernel, first, last),
        [shaped((width // nf, cols), BF)] * nf,
        [order, g_own, g_oth, o_rows, h_own, h_oth, g_proj],
        4 * half * width * cols,
        smem=1,
    )


def part_sum_kernel(order, own_ref, small_ref, *refs):
    came, out_ref = refs[:-1], refs[-1]
    slots = out_ref.shape[0]
    depth = own_ref.shape[0] // slots
    for number in range(slots):
        rows = slice(number * depth, (number + 1) * depth)
        total = own_ref[rows, :].astype(F32)
        for ref in came:
            total = total + ref[rows, :].astype(F32)
        slot = lax.rem(order[number], slots)
        out_ref[slot, :depth, :] = total.astype(BF)
        out_ref[slot, depth:, :] = small_ref[number].astype(BF)


def part_sum(order, own, small, came):
    rows, cols = own.shape
    slots, extra, _ = small.shape
    return call(
        part_sum_kernel,
        shaped((slots, rows // slots + extra, cols), BF),
        [order, own, small, *came],
        rows * cols * 2,
        smem=1,
    )


def final_kernel(plans, *refs):
    outs = refs[-len(plans) :]
    for out_ref, plan in zip(outs, plans):
        cols = out_ref.shape[-1]
        for index, which, col in plan:
            ref = refs[which]
            if len(ref.shape) == 2:
                out_ref[index] = ref[: out_ref.shape[-2], col : col + cols].astype(F32)
                continue
            rows = slice(0, out_ref.shape[-2])
            total = ref[0, rows, col : col + cols].astype(F32)
            for slot in range(1, ref.shape[0]):
                total = total + ref[slot, rows, col : col + cols].astype(F32)
            out_ref[index] = total


def final_sums(plans, shapes, pieces):
    return call(partial(final_kernel, plans), shapes, pieces, sum(p.size for p in pieces))


def norm_back_kernel(gain_row, gx_ref, a_ref, b_ref, y_ref, table_ref, gy_ref, low_ref, sums_ref):
    grad = a_ref[...].astype(F32) + b_ref[...].astype(F32)
    n, scale = norm_stats(y_ref[...].astype(F32))
    e = grad * table_ref[gain_row : gain_row + 1, :]
    mean_e = jnp.mean(e, axis=-1, keepdims=True)
    mean_en = jnp.mean(e * n, axis=-1, keepdims=True)
    gx = gx_ref[...].astype(F32)
    gy = gx + scale * (e - mean_e - n * mean_en)
    gy_ref[...] = gy
    low = gy.astype(BF)
    low_ref[...] = low
    sums_ref[0:1, :] = jnp.sum(grad * n, axis=0, keepdims=True)
    sums_ref[1:2, :] = jnp.sum(grad, axis=0, keepdims=True)
    sums_ref[2:3, :] = jnp.sum(low.astype(F32), axis=0, keepdims=True)
    sums_ref[3:4, :] = jnp.sum(gx.astype(BF).astype(F32), axis=0, keepdims=True)
    sums_ref[4:, :] = jnp.zeros((4, gx.shape[1]), F32)


def norm_backward(gx, a, b, y, table, gain_row):
    rows, width = gx.shape
    return call(
        partial(norm_back_kernel, gain_row),
        [shaped((rows, width), F32), shaped((rows, width), BF), shaped((8, width), F32)],
        [gx, a, b, y, table],
        rows * width * 25,
    )


def out_back_kernel(col, depth, order, g_own, g_oth, *refs):
    w_refs, out_ref = refs[:-1], refs[-1]
    g = jnp.concatenate([g_own[...], g_oth[...]], axis=0)
    heads_out(out_ref, dot(g, rows_of(order, w_refs, col, out_ref.shape[0] * HD, depth)), 0, 0)


def out_backward(order, g_own, g_oth, pack, col, depth, local):
    half, width = g_own.shape
    return call(
        partial(out_back_kernel, col, depth),
        shaped((local // HD, HD, 2 * half), BF),
        [order, g_own, g_oth, *pack],
        4 * half * width * local,
        smem=1,
    )


def qkv_back_kernel(col, depth, extra, order, g_ref, *refs):
    w_refs, (rows_ref, sum_ref, oth_ref, own_ref) = refs[:-4], refs[-4:]
    heads = g_ref.shape[0]
    half = own_ref.shape[0]
    local = heads * HD
    planes = [
        jnp.concatenate([g_ref[j, i * HD : (i + 1) * HD, :] for j in range(heads)], axis=0).T
        for i in range(3)
    ]
    grads = jnp.concatenate(planes, axis=1)
    rows_ref[...] = grads
    total = dot(grads, rows_of(order, w_refs, col, 3 * local, depth, extra), NT)
    oth_ref[...] = total[half:].astype(BF)
    own_ref[...] = total[:half]
    sum_ref[...] = jnp.sum(grads.astype(F32), axis=0, keepdims=True)


def qkv_backward(order, g, pack, col, depth, extra, width):
    heads, _, rows = g.shape
    half = rows // 2
    cols = 3 * heads * HD
    return call(
        partial(qkv_back_kernel, col, depth, extra),
        [
            shaped((rows, cols), BF),
            shaped((1, cols), F32),
            shaped((half, width), BF),
            shaped((half, width), F32),
        ],
        [order, g, *pack],
        2 * rows * width * cols,
        smem=1,
    )


def gather_blocks(source_ref, src_ref, dest_ref, per_device):
    for s in range(dest_ref.shape[1] // BLK):
        src = src_ref[s]
        z = src // per_device
        start = pl.multiple_of((src - z * per_device) * BLK, BLK)
        dest_ref[:, s * BLK : (s + 1) * BLK] = source_ref[z, :, pl.ds(start, BLK)]


def scatter_blocks(dest_ref, src_ref, source, per_device, low, first):
    depth, columns = source.shape
    for s in range(columns // BLK):
        src = src_ref[first + s]
        z = src // per_device
        start = pl.multiple_of((src - z * per_device) * BLK, BLK)
        dest_ref[z, low : low + depth, pl.ds(start, BLK)] = source[:, s * BLK : (s + 1) * BLK]


def segment_columns(seg_ref, column_ref):
    for s in range(seg_ref.shape[1] // BLK):
        row = seg_ref[:, s * BLK : (s + 1) * BLK]
        row = jnp.where(row < 0, -2, row).astype(F32)
        column_ref[s * BLK : (s + 1) * BLK, :] = jnp.broadcast_to(row, (BLK, BLK)).T


def score_tile(keys, queries, column_ref, seg_ref, slope, base, first, last):
    depth = keys.shape[0]
    width = last - first
    scores = dot(keys, queries)
    key_row = lax.broadcasted_iota(jnp.int32, (depth, width), 0)
    query_row = lax.broadcasted_iota(jnp.int32, (depth, width), 1) + (first - base)
    distance = query_row - key_row
    scores = scores - slope * distance.astype(F32)
    columns = column_ref[base : base + depth, :]
    key_seg = jnp.concatenate([columns] * (width // BLK), axis=1)
    query_seg = seg_ref[:, first:last].astype(F32)
    allowed = ((key_seg == query_seg) & (distance >= 0)) | (distance == 0)
    return scores, allowed


def attend_kernel(per_device, src_ref, slope_ref, seg_ref, qkv_ref, o_ref, lse_ref, stream_ref, column_ref):
    gather_blocks(qkv_ref, src_ref, stream_ref, per_device)
    segment_columns(seg_ref, column_ref)
    slope = slope_ref[0]
    run = RUN_BLOCKS * BLK
    for base in range(0, stream_ref.shape[1], run):
        keys = stream_ref[HD : 2 * HD, base : base + run].T
        for first in range(base, base + run, QB):
            last = first + QB
            depth = last - base
            queries = stream_ref[:HD, first:last] * jnp.asarray(HD**-0.5, BF)
            scores, allowed = score_tile(
                keys[:depth], queries, column_ref, seg_ref, slope, base, first, last
            )
            scores = jnp.where(allowed, scores, MASKED)
            top = jnp.max(scores, axis=0, keepdims=True)
            weights = jnp.exp(scores - top)
            total = jnp.sum(weights, axis=0, keepdims=True)
            lse_ref[:, first:last] = top + jnp.log(total)
            values = stream_ref[2 * HD :, base : base + depth]
            out = (dot(values, weights.astype(BF)) / total).astype(BF)
            scatter_blocks(o_ref, src_ref, out, per_device, 0, first // BLK)


def attend(qkv, source, slope, segments):
    nc, depth, rows = qkv.shape
    length = nc * rows
    smem = pl.BlockSpec(memory_space=pltpu.SMEM)
    return pl.pallas_call(
        partial(attend_kernel, rows // BLK),
        in_specs=[smem, smem, whole(), whole()],
        out_specs=[whole(), whole()],
        out_shape=[shaped((nc, HD, rows), BF), shaped((1, length), F32)],
        scratch_shapes=[pltpu.VMEM((3 * HD, length), BF), pltpu.VMEM((length, BLK), F32)],
        **params(length * RUN_BLOCKS * BLK * HD * 3, length * HD * 8, length * RUN_BLOCKS * BLK // 2),
    )(source, slope, segments, qkv)


def attend_back_kernel(
    per_device, src_ref, slope_ref, seg_ref, qkv_ref, g_ref, lse_ref, out_ref, stream_ref, grad_ref, column_ref, k_acc, v_acc
):
    gather_blocks(qkv_ref, src_ref, stream_ref, per_device)
    gather_blocks(g_ref, src_ref, grad_ref, per_device)
    segment_columns(seg_ref, column_ref)
    slope = slope_ref[0]
    run = RUN_BLOCKS * BLK
    scale = HD**-0.5
    for base in range(0, stream_ref.shape[1], run):
        rows = slice(base, base + run)
        keys_turned = stream_ref[HD : 2 * HD, rows]
        keys = keys_turned.T
        values = stream_ref[2 * HD :, rows].T
        queries_rows = stream_ref[:HD, rows].T
        grads_rows = grad_ref[:, rows].T
        for first in range(base + run - QB, base - 1, -QB):
            last = first + QB
            depth = last - base
            inner = slice(first - base, last - base)
            queries = stream_ref[:HD, first:last] * jnp.asarray(scale, BF)
            scores, allowed = score_tile(
                keys[:depth], queries, column_ref, seg_ref, slope, base, first, last
            )
            weights = jnp.where(allowed, jnp.exp(scores - lse_ref[:, first:last]), 0.0)
            back = dot(values[:depth], grad_ref[:, first:last])
            delta = jnp.sum(weights * back, axis=0, keepdims=True)
            low = (weights * (back - delta)).astype(BF)
            v_piece = dot(weights.astype(BF), grads_rows[inner])
            k_piece = dot(low, queries_rows[inner])
            if depth == run:
                v_acc[...] = v_piece
                k_acc[...] = k_piece
            else:
                v_acc[:depth, :] += v_piece
                k_acc[:depth, :] += k_piece
            q_grad = (dot(keys_turned[:, :depth], low) * scale).astype(BF)
            scatter_blocks(out_ref, src_ref, q_grad, per_device, 0, first // BLK)
        scatter_blocks(out_ref, src_ref, (k_acc[...] * scale).T.astype(BF), per_device, HD, base // BLK)
        scatter_blocks(out_ref, src_ref, v_acc[...].T.astype(BF), per_device, 2 * HD, base // BLK)


def attend_backward(qkv, grads, lse, source, slope, segments):
    nc, depth, rows = qkv.shape
    length = nc * rows
    run = RUN_BLOCKS * BLK
    smem = pl.BlockSpec(memory_space=pltpu.SMEM)
    return pl.pallas_call(
        partial(attend_back_kernel, rows // BLK),
        in_specs=[smem, smem, whole(), whole(), whole(), whole()],
        out_specs=whole(),
        out_shape=shaped((nc, depth, rows), BF),
        scratch_shapes=[
            pltpu.VMEM((3 * HD, length), BF),
            pltpu.VMEM((HD, length), BF),
            pltpu.VMEM((length, BLK), F32),
            pltpu.VMEM((run, HD), F32),
            pltpu.VMEM((run, HD), F32),
        ],
        **params(length * run * HD * 7, length * HD * 16, length * run // 2),
    )(source, slope, segments, qkv, grads, lse)


def to_relative_kernel(place_ref, value_ref, own_ref, oth_ref):
    half = own_ref.shape[0]
    for ref, side in ((own_ref, place_ref[0]), (oth_ref, 1 - place_ref[0])):
        rows = pl.ds(pl.multiple_of(side * half, half), half)
        for number in range(place_ref.shape[0] - 1):
            depth = value_ref.shape[1] // (place_ref.shape[0] - 1)
            start = pl.multiple_of(place_ref[number + 1] * depth, depth)
            ref[:, number * depth : (number + 1) * depth] = value_ref[rows, pl.ds(start, depth)]


def from_relative_kernel(place_ref, own_ref, oth_ref, value_ref):
    half = own_ref.shape[0]
    for ref, side in ((own_ref, place_ref[0]), (oth_ref, 1 - place_ref[0])):
        rows = pl.ds(pl.multiple_of(side * half, half), half)
        for number in range(place_ref.shape[0] - 1):
            depth = value_ref.shape[1] // (place_ref.shape[0] - 1)
            start = pl.multiple_of(place_ref[number + 1] * depth, depth)
            value_ref[rows, pl.ds(start, depth)] = ref[:, number * depth : (number + 1) * depth].astype(
                value_ref.dtype
            )


def on_device(
    nf,
    nc,
    nt,
    tokens,
    cotangent,
    block_place,
    segment_ids,
    qkv_weight,
    out_weight,
    up_weight,
    down_weight,
    query_value_bias,
    up_bias,
    norm_gains,
    row_biases,
):
    rows, width = tokens.shape
    half = rows // 2
    depth = qkv_weight.shape[1]
    local = qkv_weight.shape[3]
    heads = local // HD
    hidden = up_weight.shape[2]
    span = nc * depth
    y_index = lax.axis_index("fsdp")
    z_index = lax.axis_index("ctx")
    t_index = lax.axis_index("tp")
    side = t_index % 2

    def swap(value, axis, size, bit):
        return lax.ppermute(value, axis, [(i, i ^ bit) for i in range(size)])

    def sibling(value):
        return swap(value, "tp", nt, 1)

    def across(value):
        return lax.all_to_all(value, "ctx", 0, 0)

    def tie(value, *others):
        return lax.optimization_barrier((value, *others))[0]

    def gather_z(shard, doubling=False):
        if not doubling:
            return [swap(shard, "ctx", nc, bit) for bit in range(1, nc)]
        came, bit = [], 1
        while bit < nc:
            came.append(swap(jnp.concatenate([shard, *came], axis=0) if came else shard, "ctx", nc, bit))
            bit *= 2
        return came

    def gather_y(shard, came, apart=False):
        pack = [shard, *came]
        for bit in range(1, nf):
            if apart:
                own = swap(shard, "fsdp", nf, bit)
                pack.append(own)
                pack.append(swap(tie(jnp.concatenate(came, axis=0), own), "fsdp", nf, bit))
            else:
                pack.append(swap(jnp.concatenate([shard, *came], axis=0), "fsdp", nf, bit))
        return pack

    def whole_gather(shard):
        return lax.all_gather(shard, ("fsdp", "ctx"), axis=0, tiled=True)

    def whole_scatter(total):
        return lax.psum_scatter(total, ("fsdp", "ctx"), scatter_dimension=0, tiled=True)

    def send_y(parts):
        return [swap(parts[bit], "fsdp", nf, bit) for bit in range(1, nf)]

    def tensor_sum(other, own):
        term = (own + sibling(other).astype(F32)).astype(BF)
        bit = 2
        while bit * 2 < nt:
            term = (term.astype(F32) + swap(term, "tp", nt, bit).astype(F32)).astype(BF)
            bit *= 2
        return term, swap(term, "tp", nt, bit)

    order = jnp.stack(
        [(y_index ^ a) * nc + (z_index ^ b) for a in range(nf) for b in range(nc)]
    ).astype(jnp.int32)
    place = jnp.concatenate([side.reshape(1).astype(jnp.int32), order])

    def columns_moved(value):
        return jnp.concatenate(
            [
                lax.dynamic_slice_in_dim(value, order[number] * depth, depth, axis=1)
                for number in range(nf * nc)
            ],
            axis=1,
        )

    def to_relative(value):
        if depth % 128 == 0:
            return call(
                to_relative_kernel,
                [shaped((half, width), value.dtype)] * 2,
                [place, value],
                value.size,
                smem=1,
            )
        moved = columns_moved(value)
        return [lax.dynamic_slice_in_dim(moved, which * half, half) for which in (side, 1 - side)]

    def from_relative(own, oth):
        if depth % 128 == 0:
            return call(
                from_relative_kernel, shaped((rows, width), own.dtype), [place, own, oth], 2 * own.size, smem=1
            )
        return columns_moved(
            jnp.where(side == 0, jnp.concatenate([own, oth], axis=0), jnp.concatenate([oth, own], axis=0))
        )

    per_device = rows // BLK
    count = nc * per_device
    stored_place = block_place[0]
    stored = jnp.arange(count, dtype=jnp.int32)
    relative = (stored // per_device) * per_device + (stored % per_device + side * (per_device // 2)) % per_device
    source = jnp.sum(
        jnp.where(stored_place[None, :] == jnp.arange(count, dtype=jnp.int32)[:, None], relative[None, :], 0), axis=1
    ).astype(jnp.int32)
    head = (t_index * heads + z_index).astype(F32)
    slope = jnp.exp2(-8.0 * (head + 1.0) / HEADS).reshape(1)
    segments = segment_ids

    def qkv_shard(layer):
        return [qkv_weight[layer, :, i, :] for i in range(3)]

    table_rows = []
    for layer in range(LAYERS):
        table_rows += [norm_gains[layer].T, row_biases[layer].T, jnp.zeros((2, depth), BF)]
    table_shard = jnp.concatenate(table_rows, axis=0)
    extra = table_shard.shape[0]
    table_padded = jnp.pad(table_shard, ((0, 0), (0, 3 * local - depth)))
    first_shard = jnp.concatenate([jnp.concatenate(qkv_shard(0), axis=1), table_padded], axis=0)
    first_z = gather_z(first_shard)
    first_pack = gather_y(first_shard, first_z, apart=True)
    table = jnp.concatenate(
        [
            ref[start + depth : start + depth + extra, :depth]
            for ref in first_pack
            for start in range(0, ref.shape[0], depth + extra)
        ],
        axis=1,
    ).astype(F32)

    biases = [
        jnp.stack([query_value_bias[l, 0], jnp.zeros((local,), BF), query_value_bias[l, 1]]).astype(F32)
        for l in range(LAYERS)
    ]
    up_biases = [up_bias[l].astype(F32).reshape(1, hidden) for l in range(LAYERS)]

    x_half, x_oth = to_relative(tokens)
    n_own = norm_stats(x_half.astype(F32))[0]
    n_oth = norm_stats(x_oth.astype(F32))[0]
    h_own, h_oth, qkv_sent = first_qkv(order, n_own, n_oth, table, 0, biases[0], first_pack, depth, extra)

    out_up_shard = tie(jnp.concatenate([out_weight[0], up_weight[0]], axis=1), *first_z)
    out_up_z = gather_z(out_up_shard)
    out_up = gather_y(out_up_shard, out_up_z)
    out_packs, qkv_packs, up_packs = [(out_up, 0)], [(first_pack, 0, extra)], [(out_up, local)]
    next_out_qkv = whole_gather(
        tie(jnp.concatenate([out_weight[1], *qkv_shard(1)], axis=1), *first_z)
    )
    down_shard = tie(down_weight[0], *out_up_z)
    down_z = gather_z(down_shard, True)
    down_packs = [(gather_y(down_shard, down_z), 0)]
    out_packs.append(([next_out_qkv], 0))
    qkv_packs.append(([next_out_qkv], local, 0))

    records = []
    last_other = last_own = None
    for l in range(LAYERS):
        row = l * NORM_ROWS
        qkv = across(qkv_sent)
        if l == 0:
            next_mlp = whole_gather(
                tie(jnp.concatenate([up_weight[1], down_weight[1]], axis=1), next_out_qkv)
            )
            up_packs.append(([next_mlp], 0))
            down_packs.append(([next_mlp], hidden))
        o_stream, lse = attend(qkv, source, slope, segments)
        o_rows = across(o_stream)
        if l == 0:
            o_rows = tie(o_rows, *down_z)
        other = out_project(order, o_rows, *out_packs[l], depth, width, half, BF)
        own = out_project(order, tie(o_rows, other), *out_packs[l], depth, width, 0, F32)
        a, b = tensor_sum(other, own)
        y_half, h2_own = add_norm(x_half, a, b, table, row + 3, row + 1, row + 4)
        h2_oth = sibling(h2_own)
        u, other, own = mlp_forward(order, h2_own, h2_oth, up_biases[l], up_packs[l], down_packs[l], depth)
        records.append((x_half, h_own, h_oth, qkv, lse, o_rows, y_half, h2_own, h2_oth, u))
        if l + 1 < LAYERS:
            a, b = tensor_sum(other, own)
            following = row + NORM_ROWS
            x_half, h_own = add_norm(y_half, a, b, table, row + 5, following, following + 2)
            h_oth = sibling(h_own)
            qkv_sent = qkv_project(order, h_own, h_oth, biases[l + 1], *qkv_packs[l + 1][:2], depth)
        else:
            last_other, last_own = other, own

    gz_own, gz_oth = to_relative(cotangent)
    gx_half = gz_own.astype(F32)
    sums = [None] * LAYERS
    late = [None] * LAYERS
    above = ()
    for l in reversed(range(LAYERS)):
        row = l * NORM_ROWS
        x_half, h_own, h_oth, qkv, lse, o_rows, y_half, h2_own, h2_oth, u = records[l]
        act, gu, up_sum, other, own = mlp_backward(order, gz_own, gz_oth, u, up_packs[l], down_packs[l], depth)
        a, b = tensor_sum(other, own)
        total = late_grad(order, (gz_own, gz_oth, h2_own, h2_oth, tie(act, a), gu), above)
        b = tie(b, total)
        late[l] = whole_scatter(tie(total, *late[l + 1 :]))
        gy_half, ga_own, sums_two = norm_backward(gx_half, a, b, y_half, table, row + 1)
        ga_oth = sibling(ga_own)
        g_stream = across(out_backward(order, ga_own, ga_oth, *out_packs[l], depth, local))
        if l == LAYERS - 1:
            a, b = tensor_sum(tie(last_other, g_stream), last_own)
            final_half = y_half + (a.astype(F32) + b.astype(F32) + table[row + 5])
            final_low = final_half.astype(BF)
            block_output = from_relative(final_low, sibling(final_low))
        g_sent = attend_backward(qkv, g_stream, lse, source, slope, segments)
        g_rows = across(g_sent)
        g_proj, qkv_sum, other, own = qkv_backward(
            order, g_rows, qkv_packs[l][0], qkv_packs[l][1], depth, qkv_packs[l][2], width
        )
        a, b = tensor_sum(other, own)
        sources = (order, ga_own, ga_oth, o_rows, h_own, h_oth)
        if l > 0:
            above = (*sources[1:], g_proj)
        else:
            out_q = attention_grad(0, 2, *sources, tie(g_proj, a), nf)
            out_q_came = send_y(out_q)
            last_parts = attention_grad(2, 4, *sources, tie(g_proj, *out_q), nf)
            last_came = send_y(last_parts)
            b = tie(b, *last_parts)
        gx_half, gz_own, sums_one = norm_backward(gy_half, a, b, x_half, table, row)
        if l > 0:
            gz_oth = sibling(gz_own)
        sums[l] = (sums_one, sums_two, qkv_sum, up_sum)
    grad_tokens = from_relative(gx_half, sibling(gx_half))

    norm_all = jnp.concatenate([sums[l][which] for l in range(LAYERS) for which in (0, 1)], axis=0)
    bias_all = jnp.concatenate(
        [sums[l][2][:, :local] for l in range(LAYERS)]
        + [sums[l][2][:, 2 * local :] for l in range(LAYERS)]
        + [sums[l][3] for l in range(LAYERS)],
        axis=1,
    ).reshape(-1, depth)
    count = norm_all.shape[0]
    norm_total = norm_all[:, :span]
    bias_total = bias_all
    for bit in range(1, nf):
        sent = jnp.concatenate(
            [norm_all[:, bit * span + b * depth : bit * span + (b + 1) * depth] for b in range(nc)] + [bias_all],
            axis=0,
        )
        came = swap(sent, "fsdp", nf, bit)
        norm_total = norm_total + jnp.concatenate(
            [came[b * count : (b + 1) * count] for b in range(nc)], axis=1
        )
        bias_total = bias_total + came[nc * count :]
    cols = last_parts[0].shape[1]
    held = count * depth + bias_total.size
    extra_rows = -(-held // (16 * cols)) * 16
    small = jnp.concatenate(
        [
            norm_total.reshape(count, nc, depth).transpose(1, 0, 2).reshape(nc, -1),
            jnp.broadcast_to(bias_total.reshape(1, -1), (nc, bias_total.size)),
            jnp.zeros((nc, extra_rows * cols - held), F32),
        ],
        axis=1,
    ).reshape(nc, extra_rows, cols)
    nothing = jnp.zeros((nc, 16, cols), F32)
    out_q_sums = part_sum(order, out_q[0], nothing, out_q_came)
    out_q_pieces = across(out_q_sums)
    last_sums = part_sum(order, tie(last_parts[0], out_q_pieces), small, last_came)
    last_pieces = across(last_sums)
    small = jnp.sum(last_pieces[:, depth:, :].astype(F32), axis=0).reshape(-1)
    norm_mine = small[: count * depth].reshape(count, depth)
    bias_sum = small[count * depth : held]
    grad_up, grad_down = final_sums(
        [[(l, l, col) for l in range(LAYERS)] for col in (0, hidden)],
        [shaped((LAYERS, depth, hidden), F32)] * 2,
        late,
    )
    qkv_plan = [((1, i), 1, 2 * hidden + (i + 1) * local) for i in range(3)]
    qkv_plan += [((0, 0), 2, local), ((0, 1), 0, 0), ((0, 2), 0, local)]
    grad_out, grad_qkv = final_sums(
        [[(0, 2, 0), (1, 1, 2 * hidden)], qkv_plan],
        [shaped((LAYERS, depth, local), F32), shaped((LAYERS, 3, depth, local), F32)],
        [last_pieces, late[0], out_q_pieces],
    )
    grad_qkv = grad_qkv.transpose(0, 2, 1, 3)

    norm_mine = (norm_mine + sibling(norm_mine)).reshape(LAYERS, 2, 8, depth)
    grad_gains = norm_mine[:, :, 0].transpose(0, 2, 1)
    grad_shifts = jnp.stack(
        [norm_mine[:, 0, 1], norm_mine[:, 1, 2], norm_mine[:, 1, 1], norm_mine[:, 1, 3]], axis=1
    ).transpose(0, 2, 1)
    queries, values = bias_sum[: LAYERS * local], bias_sum[LAYERS * local : 2 * LAYERS * local]
    grad_bias = jnp.stack([queries.reshape(LAYERS, local), values.reshape(LAYERS, local)], axis=1)
    grad_up_bias = bias_sum[2 * LAYERS * local :].reshape(LAYERS, hidden)

    return (
        block_output,
        grad_tokens,
        grad_qkv,
        grad_out,
        grad_up,
        grad_down,
        grad_bias,
        grad_up_bias,
        grad_gains,
        grad_shifts,
    )


def solution(mesh):
    placed = (
        P(("fsdp", "ctx"), None),
        P(("fsdp", "ctx"), None),
        P("fsdp", None),
        P("fsdp", None),
        P(None, ("fsdp", "ctx"), None, "tp"),
        P(None, ("fsdp", "ctx"), "tp"),
        P(None, ("fsdp", "ctx"), "tp"),
        P(None, ("fsdp", "ctx"), "tp"),
        P(None, None, "tp"),
        P(None, "tp"),
        P(None, ("fsdp", "ctx"), None),
        P(None, ("fsdp", "ctx"), None),
    )
    return jax.shard_map(
        partial(on_device, mesh.shape["fsdp"], mesh.shape["ctx"], mesh.shape["tp"]),
        mesh=mesh,
        in_specs=placed,
        out_specs=(
            P(("fsdp", "ctx"), None),
            P(("fsdp", "ctx"), None),
            P(None, ("fsdp", "ctx"), None, "tp"),
            P(None, ("fsdp", "ctx"), "tp"),
            P(None, ("fsdp", "ctx"), "tp"),
            P(None, ("fsdp", "ctx"), "tp"),
            P(None, None, "tp"),
            P(None, "tp"),
            P(None, ("fsdp", "ctx"), None),
            P(None, ("fsdp", "ctx"), None),
        ),
        check_vma=False,
    )
```

```python
from functools import partial

import jax
import jax.numpy as jnp
from jax import lax
from jax.experimental import pallas as pl
from jax.experimental.pallas import tpu as pltpu
from jax.sharding import PartitionSpec as P

HEADS = 16
HD = 64
BLK = 128
RUN_BLOCKS = 8
LAYERS = 2
NORM_ROWS = 8
NORM_EPS = 1e-05
MASKED = -1000000000.0
QB = 256
GELU_A = 0.7978845608028654
GELU_B = 0.044715
BF = jnp.bfloat16
F32 = jnp.float32
NN = ((1,), (0,))
NT = ((1,), (1,))
VMEM_LIMIT = 40 * 1024 * 1024


def dot(left, right, dims=NN):
    return lax.dot_general(left, right, (dims, ((), ())), preferred_element_type=F32)


def shaped(shape, dtype):
    return jax.ShapeDtypeStruct(shape, dtype)


def whole():
    return pl.BlockSpec(memory_space=pltpu.VMEM)


def params(flops, bytes_accessed, transcendentals=0):
    return dict(
        compiler_params=pltpu.CompilerParams(vmem_limit_bytes=VMEM_LIMIT),
        cost_estimate=pl.CostEstimate(
            flops=int(flops), bytes_accessed=int(bytes_accessed), transcendentals=int(transcendentals)
        ),
    )


def rows_of(order, refs, col, cols, depth, extra=0):
    pieces = []
    if all(ref.shape == refs[0].shape for ref in refs):
        held = refs[0].shape[0] // depth
        for number in range(order.shape[0]):
            start = pl.multiple_of(lax.rem(order[number], held) * depth, depth)
            pieces.append(refs[number // held][pl.ds(start, depth), col : col + cols])
        return jnp.concatenate(pieces, axis=0)
    for ref in refs:
        for start in range(0, ref.shape[0], depth + extra):
            pieces.append(ref[start : start + depth, col : col + cols])
    return jnp.concatenate(pieces, axis=0)


def call(kernel, out_shape, args, flops, scratch=(), transcendentals=0, smem=0):
    outs = out_shape if isinstance(out_shape, (list, tuple)) else [out_shape]
    moved = sum(a.size * a.dtype.itemsize for a in args) + sum(
        o.size * jnp.dtype(o.dtype).itemsize for o in outs
    )
    specs = [pl.BlockSpec(memory_space=pltpu.SMEM)] * smem + [whole()] * (len(args) - smem)
    return pl.pallas_call(
        kernel,
        in_specs=specs,
        out_specs=[whole()] * len(outs) if outs is out_shape else whole(),
        out_shape=out_shape,
        scratch_shapes=list(scratch),
        **params(flops, moved, transcendentals),
    )(*args)


def norm_stats(values):
    average = jnp.mean(values, axis=-1, keepdims=True)
    centred = values - average
    variance = jnp.mean(centred * centred, axis=-1, keepdims=True)
    scale = lax.rsqrt(variance + NORM_EPS)
    return centred * scale, scale


def gelu_parts(u):
    inner = GELU_A * (u + GELU_B * u * u * u)
    t = jnp.tanh(inner)
    return t


def add_norm_kernel(bias_row, gain_row, shift_row, x_ref, a_ref, b_ref, table_ref, y_ref, h_ref):
    branch = a_ref[...].astype(F32) + b_ref[...].astype(F32) + table_ref[bias_row : bias_row + 1, :]
    y = x_ref[...].astype(F32) + branch
    y_ref[...] = y
    n, _ = norm_stats(y)
    h_ref[...] = (
        n * table_ref[gain_row : gain_row + 1, :] + table_ref[shift_row : shift_row + 1, :]
    ).astype(BF)


def add_norm(x, a, b, table, bias_row, gain_row, shift_row):
    rows, width = x.shape
    return call(
        partial(add_norm_kernel, bias_row, gain_row, shift_row),
        [shaped((rows, width), F32), shaped((rows, width), BF)],
        [x, a, b, table],
        rows * width * 12,
    )


def heads_out(out_ref, total, number, row):
    half = total.shape[0]
    turned = total.astype(BF).T
    for j in range(out_ref.shape[0]):
        out_ref[j, row : row + HD, number * half : (number + 1) * half] = turned[j * HD : (j + 1) * HD, :]


def qkv_rows(order, h_refs, bias_ref, w_refs, out_ref, col, depth, extra):
    local = out_ref.shape[0] * HD
    h = jnp.concatenate([h_ref[...] for h_ref in h_refs], axis=0)
    for i in range(3):
        weights = rows_of(order, w_refs, col + i * local, local, depth, extra)
        heads_out(out_ref, dot(h, weights) + bias_ref[i : i + 1, :], 0, i * HD)


def qkv_kernel(col, depth, order, h_own, h_oth, bias_ref, *refs):
    qkv_rows(order, [h_own, h_oth], bias_ref, refs[:-1], refs[-1], col, depth, 0)


def qkv_project(order, h_own, h_oth, bias, pack, col, depth):
    half, width = h_own.shape
    local = bias.shape[1]
    return call(
        partial(qkv_kernel, col, depth),
        shaped((local // HD, 3 * HD, 2 * half), BF),
        [order, h_own, h_oth, bias, *pack],
        12 * half * width * local,
        smem=1,
    )


def first_qkv_kernel(row, depth, extra, order, n_own, n_oth, table_ref, bias_ref, *refs):
    w_refs, (h_own, h_oth, out_ref) = refs[:-3], refs[-3:]
    for n_ref, h_ref in ((n_own, h_own), (n_oth, h_oth)):
        h_ref[...] = (n_ref[...] * table_ref[row : row + 1, :] + table_ref[row + 2 : row + 3, :]).astype(BF)
    qkv_rows(order, [h_own, h_oth], bias_ref, w_refs, out_ref, 0, depth, extra)


def first_qkv(order, n_own, n_oth, table, row, bias, pack, depth, extra):
    half, width = n_own.shape
    local = bias.shape[1]
    return call(
        partial(first_qkv_kernel, row, depth, extra),
        [
            shaped((half, width), BF),
            shaped((half, width), BF),
            shaped((local // HD, 3 * HD, 2 * half), BF),
        ],
        [order, n_own, n_oth, table, bias, *pack],
        12 * half * width * local,
        smem=1,
    )


def out_kernel(col, depth, start, order, o_ref, *refs):
    w_refs, out_ref = refs[:-1], refs[-1]
    half = out_ref.shape[0]
    heads = o_ref.shape[0]
    o = jnp.concatenate([o_ref[j, :, start : start + half] for j in range(heads)], axis=0).T
    weights = rows_of(order, w_refs, col, heads * HD, depth)
    out_ref[...] = dot(o, weights, NT).astype(out_ref.dtype)


def out_project(order, o_rows, pack, col, depth, width, start, dtype):
    heads, _, rows = o_rows.shape
    half = rows // 2
    return call(
        partial(out_kernel, col, depth, start),
        shaped((half, width), dtype),
        [order, o_rows, *pack],
        2 * half * width * heads * HD,
        smem=1,
    )


def mlp_kernel(counts, up_col, down_col, depth, order, h_own, h_oth, bias_ref, *refs):
    ups, downs = refs[: counts[0]], refs[counts[0] : counts[0] + counts[1]]
    u_ref, oth_ref, own_ref = refs[counts[0] + counts[1] :]
    half = h_own.shape[0]
    hidden = u_ref.shape[1]
    h = jnp.concatenate([h_own[...], h_oth[...]], axis=0)
    u = dot(h, rows_of(order, ups, up_col, hidden, depth)) + bias_ref[...]
    u_ref[...] = u
    act = (0.5 * u * (1.0 + gelu_parts(u))).astype(BF)
    total = dot(act, rows_of(order, downs, down_col, hidden, depth), NT)
    own_ref[...] = total[:half, :]
    oth_ref[...] = total[half:, :].astype(BF)


def mlp_forward(order, h_own, h_oth, bias, up, down, depth):
    half, width = h_own.shape
    hidden = bias.shape[1]
    return call(
        partial(mlp_kernel, (len(up[0]), len(down[0])), up[1], down[1], depth),
        [
            shaped((2 * half, hidden), F32),
            shaped((half, width), BF),
            shaped((half, width), F32),
        ],
        [order, h_own, h_oth, bias, *up[0], *down[0]],
        8 * half * width * hidden,
        transcendentals=2 * half * hidden,
        smem=1,
    )


def mlp_back_kernel(counts, up_col, down_col, depth, order, g_own, g_oth, u_ref, *refs):
    ups, downs = refs[: counts[0]], refs[counts[0] : counts[0] + counts[1]]
    act_ref, gu_ref, sum_ref, oth_ref, own_ref = refs[counts[0] + counts[1] :]
    half = g_own.shape[0]
    hidden = u_ref.shape[1]
    g = jnp.concatenate([g_own[...], g_oth[...]], axis=0)
    grad = dot(g, rows_of(order, downs, down_col, hidden, depth))
    u = u_ref[...]
    t = gelu_parts(u)
    act_ref[...] = (0.5 * u * (1.0 + t)).astype(BF)
    slope = 0.5 * (1.0 + t) + 0.5 * u * (1.0 - t * t) * (GELU_A * (1.0 + 3.0 * GELU_B * u * u))
    gu = (grad * slope).astype(BF)
    gu_ref[...] = gu
    sum_ref[...] = jnp.sum(gu.astype(F32), axis=0, keepdims=True)
    total = dot(gu, rows_of(order, ups, up_col, hidden, depth), NT)
    own_ref[...] = total[:half, :]
    oth_ref[...] = total[half:, :].astype(BF)


def mlp_backward(order, g_own, g_oth, u, up, down, depth):
    half, width = g_own.shape
    hidden = u.shape[1]
    return call(
        partial(mlp_back_kernel, (len(up[0]), len(down[0])), up[1], down[1], depth),
        [
            shaped((2 * half, hidden), BF),
            shaped((2 * half, hidden), BF),
            shaped((1, hidden), F32),
            shaped((half, width), BF),
            shaped((half, width), F32),
        ],
        [order, g_own, g_oth, u, *up[0], *down[0]],
        8 * half * width * hidden,
        transcendentals=2 * half * hidden,
        smem=1,
    )


def grads_out(order, out_refs, total, col):
    cols = slice(col, col + total.shape[1])
    if len(out_refs) == 1:
        depth = total.shape[0] // order.shape[0]
        for number in range(order.shape[0]):
            start = pl.multiple_of(order[number] * depth, depth)
            out_refs[0][pl.ds(start, depth), cols] = total[number * depth : (number + 1) * depth].astype(BF)
        return
    span = out_refs[0].shape[0]
    for y, out_ref in enumerate(out_refs):
        out_ref[:, cols] = total[y * span : (y + 1) * span].astype(BF)


def late_grad_kernel(count, order, *refs):
    g_own, g_oth, h_own, h_oth, act_ref, gu_ref = refs[:6]
    out_refs = refs[count:]
    hidden = act_ref.shape[1]
    h = jnp.concatenate([h_own[...], h_oth[...]], axis=0).T
    grads_out(order, out_refs, dot(h, gu_ref[...]), 0)
    g = jnp.concatenate([g_own[...], g_oth[...]], axis=0).T
    grads_out(order, out_refs, dot(g, act_ref[...]), hidden)
    if count > 6:
        attention_grad_body(0, 4, 2 * hidden, order, *refs[6:count], out_refs)


def late_grad(order, mlp, attention):
    half, width = mlp[0].shape
    cols = 2 * mlp[4].shape[1]
    if attention:
        cols += 4 * attention[2].shape[0] * HD
    args = [*mlp, *attention]
    return call(
        partial(late_grad_kernel, len(args)),
        [shaped((width, cols), BF)],
        [order, *args],
        4 * half * width * cols,
        smem=1,
    )[0]


def attention_grad_body(first, last, col, order, g_own, g_oth, o_ref, h_own, h_oth, p_ref, out_refs):
    heads = o_ref.shape[0]
    local = heads * HD
    if first == 0:
        g = jnp.concatenate([g_own[...], g_oth[...]], axis=0).T
        o = jnp.concatenate([o_ref[j] for j in range(heads)], axis=0)
        grads_out(order, out_refs, dot(g, o, NT), col)
        col += local
        first = 1
    h = jnp.concatenate([h_own[...], h_oth[...]], axis=0).T
    grads_out(order, out_refs, dot(h, p_ref[:, (first - 1) * local : (last - 1) * local]), col)


def attention_grad_kernel(first, last, order, *refs):
    attention_grad_body(first, last, 0, order, *refs[:6], refs[6:])


def attention_grad(first, last, order, g_own, g_oth, o_rows, h_own, h_oth, g_proj, nf):
    half, width = g_own.shape
    local = o_rows.shape[0] * HD
    cols = (last - first) * local
    return call(
        partial(attention_grad_kernel, first, last),
        [shaped((width // nf, cols), BF)] * nf,
        [order, g_own, g_oth, o_rows, h_own, h_oth, g_proj],
        4 * half * width * cols,
        smem=1,
    )


def part_sum_kernel(order, own_ref, small_ref, *refs):
    came, out_ref = refs[:-1], refs[-1]
    slots = out_ref.shape[0]
    depth = own_ref.shape[0] // slots
    for number in range(slots):
        rows = slice(number * depth, (number + 1) * depth)
        total = own_ref[rows, :].astype(F32)
        for ref in came:
            total = total + ref[rows, :].astype(F32)
        slot = lax.rem(order[number], slots)
        out_ref[slot, :depth, :] = total.astype(BF)
        out_ref[slot, depth:, :] = small_ref[number].astype(BF)


def part_sum(order, own, small, came):
    rows, cols = own.shape
    slots, extra, _ = small.shape
    return call(
        part_sum_kernel,
        shaped((slots, rows // slots + extra, cols), BF),
        [order, own, small, *came],
        rows * cols * 2,
        smem=1,
    )


def final_kernel(plans, *refs):
    outs = refs[-len(plans) :]
    for out_ref, plan in zip(outs, plans):
        cols = out_ref.shape[-1]
        for index, which, col in plan:
            ref = refs[which]
            if len(ref.shape) == 2:
                out_ref[index] = ref[: out_ref.shape[-2], col : col + cols].astype(F32)
                continue
            rows = slice(0, out_ref.shape[-2])
            total = ref[0, rows, col : col + cols].astype(F32)
            for slot in range(1, ref.shape[0]):
                total = total + ref[slot, rows, col : col + cols].astype(F32)
            out_ref[index] = total


def final_sums(plans, shapes, pieces):
    return call(partial(final_kernel, plans), shapes, pieces, sum(p.size for p in pieces))


def norm_back_kernel(gain_row, gx_ref, a_ref, b_ref, y_ref, table_ref, gy_ref, low_ref, sums_ref):
    grad = a_ref[...].astype(F32) + b_ref[...].astype(F32)
    n, scale = norm_stats(y_ref[...].astype(F32))
    e = grad * table_ref[gain_row : gain_row + 1, :]
    mean_e = jnp.mean(e, axis=-1, keepdims=True)
    mean_en = jnp.mean(e * n, axis=-1, keepdims=True)
    gx = gx_ref[...].astype(F32)
    gy = gx + scale * (e - mean_e - n * mean_en)
    gy_ref[...] = gy
    low = gy.astype(BF)
    low_ref[...] = low
    sums_ref[0:1, :] = jnp.sum(grad * n, axis=0, keepdims=True)
    sums_ref[1:2, :] = jnp.sum(grad, axis=0, keepdims=True)
    sums_ref[2:3, :] = jnp.sum(low.astype(F32), axis=0, keepdims=True)
    sums_ref[3:4, :] = jnp.sum(gx.astype(BF).astype(F32), axis=0, keepdims=True)
    sums_ref[4:, :] = jnp.zeros((4, gx.shape[1]), F32)


def norm_backward(gx, a, b, y, table, gain_row):
    rows, width = gx.shape
    return call(
        partial(norm_back_kernel, gain_row),
        [shaped((rows, width), F32), shaped((rows, width), BF), shaped((8, width), F32)],
        [gx, a, b, y, table],
        rows * width * 25,
    )


def out_back_kernel(col, depth, order, g_own, g_oth, *refs):
    w_refs, out_ref = refs[:-1], refs[-1]
    g = jnp.concatenate([g_own[...], g_oth[...]], axis=0)
    heads_out(out_ref, dot(g, rows_of(order, w_refs, col, out_ref.shape[0] * HD, depth)), 0, 0)


def out_backward(order, g_own, g_oth, pack, col, depth, local):
    half, width = g_own.shape
    return call(
        partial(out_back_kernel, col, depth),
        shaped((local // HD, HD, 2 * half), BF),
        [order, g_own, g_oth, *pack],
        4 * half * width * local,
        smem=1,
    )


def qkv_back_kernel(col, depth, extra, order, g_ref, *refs):
    w_refs, (rows_ref, sum_ref, oth_ref, own_ref) = refs[:-4], refs[-4:]
    heads = g_ref.shape[0]
    half = own_ref.shape[0]
    local = heads * HD
    planes = [
        jnp.concatenate([g_ref[j, i * HD : (i + 1) * HD, :] for j in range(heads)], axis=0).T
        for i in range(3)
    ]
    grads = jnp.concatenate(planes, axis=1)
    rows_ref[...] = grads
    total = dot(grads, rows_of(order, w_refs, col, 3 * local, depth, extra), NT)
    oth_ref[...] = total[half:].astype(BF)
    own_ref[...] = total[:half]
    sum_ref[...] = jnp.sum(grads.astype(F32), axis=0, keepdims=True)


def qkv_backward(order, g, pack, col, depth, extra, width):
    heads, _, rows = g.shape
    half = rows // 2
    cols = 3 * heads * HD
    return call(
        partial(qkv_back_kernel, col, depth, extra),
        [
            shaped((rows, cols), BF),
            shaped((1, cols), F32),
            shaped((half, width), BF),
            shaped((half, width), F32),
        ],
        [order, g, *pack],
        2 * rows * width * cols,
        smem=1,
    )


def gather_blocks(source_ref, src_ref, dest_ref, per_device):
    for s in range(dest_ref.shape[1] // BLK):
        src = src_ref[s]
        z = src // per_device
        start = pl.multiple_of((src - z * per_device) * BLK, BLK)
        dest_ref[:, s * BLK : (s + 1) * BLK] = source_ref[z, :, pl.ds(start, BLK)]


def scatter_blocks(dest_ref, src_ref, source, per_device, low, first):
    depth, columns = source.shape
    for s in range(columns // BLK):
        src = src_ref[first + s]
        z = src // per_device
        start = pl.multiple_of((src - z * per_device) * BLK, BLK)
        dest_ref[z, low : low + depth, pl.ds(start, BLK)] = source[:, s * BLK : (s + 1) * BLK]


def segment_columns(seg_ref, column_ref):
    for s in range(seg_ref.shape[1] // BLK):
        row = seg_ref[:, s * BLK : (s + 1) * BLK]
        row = jnp.where(row < 0, -2, row).astype(F32)
        column_ref[s * BLK : (s + 1) * BLK, :] = jnp.broadcast_to(row, (BLK, BLK)).T


def score_tile(keys, queries, column_ref, seg_ref, slope, base, first, last):
    depth = keys.shape[0]
    width = last - first
    scores = dot(keys, queries)
    key_row = lax.broadcasted_iota(jnp.int32, (depth, width), 0)
    query_row = lax.broadcasted_iota(jnp.int32, (depth, width), 1) + (first - base)
    distance = query_row - key_row
    scores = scores - slope * distance.astype(F32)
    columns = column_ref[base : base + depth, :]
    key_seg = jnp.concatenate([columns] * (width // BLK), axis=1)
    query_seg = seg_ref[:, first:last].astype(F32)
    allowed = ((key_seg == query_seg) & (distance >= 0)) | (distance == 0)
    return scores, allowed


def attend_kernel(per_device, src_ref, slope_ref, seg_ref, qkv_ref, o_ref, lse_ref, stream_ref, column_ref):
    gather_blocks(qkv_ref, src_ref, stream_ref, per_device)
    segment_columns(seg_ref, column_ref)
    slope = slope_ref[0]
    run = RUN_BLOCKS * BLK
    for base in range(0, stream_ref.shape[1], run):
        keys = stream_ref[HD : 2 * HD, base : base + run].T
        for first in range(base, base + run, QB):
            last = first + QB
            depth = last - base
            queries = stream_ref[:HD, first:last] * jnp.asarray(HD**-0.5, BF)
            scores, allowed = score_tile(
                keys[:depth], queries, column_ref, seg_ref, slope, base, first, last
            )
            scores = jnp.where(allowed, scores, MASKED)
            top = jnp.max(scores, axis=0, keepdims=True)
            weights = jnp.exp(scores - top)
            total = jnp.sum(weights, axis=0, keepdims=True)
            lse_ref[:, first:last] = top + jnp.log(total)
            values = stream_ref[2 * HD :, base : base + depth]
            out = (dot(values, weights.astype(BF)) / total).astype(BF)
            scatter_blocks(o_ref, src_ref, out, per_device, 0, first // BLK)


def attend(qkv, source, slope, segments):
    nc, depth, rows = qkv.shape
    length = nc * rows
    smem = pl.BlockSpec(memory_space=pltpu.SMEM)
    return pl.pallas_call(
        partial(attend_kernel, rows // BLK),
        in_specs=[smem, smem, whole(), whole()],
        out_specs=[whole(), whole()],
        out_shape=[shaped((nc, HD, rows), BF), shaped((1, length), F32)],
        scratch_shapes=[pltpu.VMEM((3 * HD, length), BF), pltpu.VMEM((length, BLK), F32)],
        **params(length * RUN_BLOCKS * BLK * HD * 3, length * HD * 8, length * RUN_BLOCKS * BLK // 2),
    )(source, slope, segments, qkv)


def attend_back_kernel(
    per_device, src_ref, slope_ref, seg_ref, qkv_ref, g_ref, lse_ref, out_ref, stream_ref, grad_ref, column_ref, k_acc, v_acc
):
    gather_blocks(qkv_ref, src_ref, stream_ref, per_device)
    gather_blocks(g_ref, src_ref, grad_ref, per_device)
    segment_columns(seg_ref, column_ref)
    slope = slope_ref[0]
    run = RUN_BLOCKS * BLK
    scale = HD**-0.5
    for base in range(0, stream_ref.shape[1], run):
        rows = slice(base, base + run)
        keys_turned = stream_ref[HD : 2 * HD, rows]
        keys = keys_turned.T
        values = stream_ref[2 * HD :, rows].T
        queries_rows = stream_ref[:HD, rows].T
        grads_rows = grad_ref[:, rows].T
        for first in range(base + run - QB, base - 1, -QB):
            last = first + QB
            depth = last - base
            inner = slice(first - base, last - base)
            queries = stream_ref[:HD, first:last] * jnp.asarray(scale, BF)
            scores, allowed = score_tile(
                keys[:depth], queries, column_ref, seg_ref, slope, base, first, last
            )
            weights = jnp.where(allowed, jnp.exp(scores - lse_ref[:, first:last]), 0.0)
            back = dot(values[:depth], grad_ref[:, first:last])
            delta = jnp.sum(weights * back, axis=0, keepdims=True)
            low = (weights * (back - delta)).astype(BF)
            v_piece = dot(weights.astype(BF), grads_rows[inner])
            k_piece = dot(low, queries_rows[inner])
            if depth == run:
                v_acc[...] = v_piece
                k_acc[...] = k_piece
            else:
                v_acc[:depth, :] += v_piece
                k_acc[:depth, :] += k_piece
            q_grad = (dot(keys_turned[:, :depth], low) * scale).astype(BF)
            scatter_blocks(out_ref, src_ref, q_grad, per_device, 0, first // BLK)
        scatter_blocks(out_ref, src_ref, (k_acc[...] * scale).T.astype(BF), per_device, HD, base // BLK)
        scatter_blocks(out_ref, src_ref, v_acc[...].T.astype(BF), per_device, 2 * HD, base // BLK)


def attend_backward(qkv, grads, lse, source, slope, segments):
    nc, depth, rows = qkv.shape
    length = nc * rows
    run = RUN_BLOCKS * BLK
    smem = pl.BlockSpec(memory_space=pltpu.SMEM)
    return pl.pallas_call(
        partial(attend_back_kernel, rows // BLK),
        in_specs=[smem, smem, whole(), whole(), whole(), whole()],
        out_specs=whole(),
        out_shape=shaped((nc, depth, rows), BF),
        scratch_shapes=[
            pltpu.VMEM((3 * HD, length), BF),
            pltpu.VMEM((HD, length), BF),
            pltpu.VMEM((length, BLK), F32),
            pltpu.VMEM((run, HD), F32),
            pltpu.VMEM((run, HD), F32),
        ],
        **params(length * run * HD * 7, length * HD * 16, length * run // 2),
    )(source, slope, segments, qkv, grads, lse)


def to_relative_kernel(place_ref, value_ref, own_ref, oth_ref):
    half = own_ref.shape[0]
    for ref, side in ((own_ref, place_ref[0]), (oth_ref, 1 - place_ref[0])):
        rows = pl.ds(pl.multiple_of(side * half, half), half)
        for number in range(place_ref.shape[0] - 1):
            depth = value_ref.shape[1] // (place_ref.shape[0] - 1)
            start = pl.multiple_of(place_ref[number + 1] * depth, depth)
            ref[:, number * depth : (number + 1) * depth] = value_ref[rows, pl.ds(start, depth)]


def from_relative_kernel(place_ref, own_ref, oth_ref, value_ref):
    half = own_ref.shape[0]
    for ref, side in ((own_ref, place_ref[0]), (oth_ref, 1 - place_ref[0])):
        rows = pl.ds(pl.multiple_of(side * half, half), half)
        for number in range(place_ref.shape[0] - 1):
            depth = value_ref.shape[1] // (place_ref.shape[0] - 1)
            start = pl.multiple_of(place_ref[number + 1] * depth, depth)
            value_ref[rows, pl.ds(start, depth)] = ref[:, number * depth : (number + 1) * depth].astype(
                value_ref.dtype
            )


def on_device(
    nf,
    nc,
    nt,
    tokens,
    cotangent,
    block_place,
    segment_ids,
    qkv_weight,
    out_weight,
    up_weight,
    down_weight,
    query_value_bias,
    up_bias,
    norm_gains,
    row_biases,
):
    rows, width = tokens.shape
    half = rows // 2
    depth = qkv_weight.shape[1]
    local = qkv_weight.shape[3]
    heads = local // HD
    hidden = up_weight.shape[2]
    span = nc * depth
    y_index = lax.axis_index("fsdp")
    z_index = lax.axis_index("ctx")
    t_index = lax.axis_index("tp")
    side = t_index % 2

    def swap(value, axis, size, bit):
        return lax.ppermute(value, axis, [(i, i ^ bit) for i in range(size)])

    def sibling(value):
        return swap(value, "tp", nt, 1)

    def across(value):
        return lax.all_to_all(value, "ctx", 0, 0)

    def tie(value, *others):
        return lax.optimization_barrier((value, *others))[0]

    def gather_z(shard, doubling=False):
        if not doubling:
            return [swap(shard, "ctx", nc, bit) for bit in range(1, nc)]
        came, bit = [], 1
        while bit < nc:
            came.append(swap(jnp.concatenate([shard, *came], axis=0) if came else shard, "ctx", nc, bit))
            bit *= 2
        return came

    def gather_y(shard, came, apart=False):
        pack = [shard, *came]
        for bit in range(1, nf):
            if apart:
                own = swap(shard, "fsdp", nf, bit)
                pack.append(own)
                pack.append(swap(tie(jnp.concatenate(came, axis=0), own), "fsdp", nf, bit))
            else:
                pack.append(swap(jnp.concatenate([shard, *came], axis=0), "fsdp", nf, bit))
        return pack

    def whole_gather(shard):
        return lax.all_gather(shard, ("fsdp", "ctx"), axis=0, tiled=True)

    def whole_scatter(total):
        return lax.psum_scatter(total, ("fsdp", "ctx"), scatter_dimension=0, tiled=True)

    def send_y(parts):
        return [swap(parts[bit], "fsdp", nf, bit) for bit in range(1, nf)]

    def tensor_sum(other, own):
        term = (own + sibling(other).astype(F32)).astype(BF)
        bit = 2
        while bit * 2 < nt:
            term = (term.astype(F32) + swap(term, "tp", nt, bit).astype(F32)).astype(BF)
            bit *= 2
        return term, swap(term, "tp", nt, bit)

    order = jnp.stack(
        [(y_index ^ a) * nc + (z_index ^ b) for a in range(nf) for b in range(nc)]
    ).astype(jnp.int32)
    place = jnp.concatenate([side.reshape(1).astype(jnp.int32), order])

    def columns_moved(value):
        return jnp.concatenate(
            [
                lax.dynamic_slice_in_dim(value, order[number] * depth, depth, axis=1)
                for number in range(nf * nc)
            ],
            axis=1,
        )

    def to_relative(value):
        if depth % 128 == 0:
            return call(
                to_relative_kernel,
                [shaped((half, width), value.dtype)] * 2,
                [place, value],
                value.size,
                smem=1,
            )
        moved = columns_moved(value)
        return [lax.dynamic_slice_in_dim(moved, which * half, half) for which in (side, 1 - side)]

    def from_relative(own, oth):
        if depth % 128 == 0:
            return call(
                from_relative_kernel, shaped((rows, width), own.dtype), [place, own, oth], 2 * own.size, smem=1
            )
        return columns_moved(
            jnp.where(side == 0, jnp.concatenate([own, oth], axis=0), jnp.concatenate([oth, own], axis=0))
        )

    per_device = rows // BLK
    count = nc * per_device
    stored_place = block_place[0]
    stored = jnp.arange(count, dtype=jnp.int32)
    relative = (stored // per_device) * per_device + (stored % per_device + side * (per_device // 2)) % per_device
    source = jnp.sum(
        jnp.where(stored_place[None, :] == jnp.arange(count, dtype=jnp.int32)[:, None], relative[None, :], 0), axis=1
    ).astype(jnp.int32)
    head = (t_index * heads + z_index).astype(F32)
    slope = jnp.exp2(-8.0 * (head + 1.0) / HEADS).reshape(1)
    segments = segment_ids

    def qkv_shard(layer):
        return [qkv_weight[layer, :, i, :] for i in range(3)]

    table_rows = []
    for layer in range(LAYERS):
        table_rows += [norm_gains[layer].T, row_biases[layer].T, jnp.zeros((2, depth), BF)]
    table_shard = jnp.concatenate(table_rows, axis=0)
    extra = table_shard.shape[0]
    table_padded = jnp.pad(table_shard, ((0, 0), (0, 3 * local - depth)))
    first_shard = jnp.concatenate([jnp.concatenate(qkv_shard(0), axis=1), table_padded], axis=0)
    first_z = gather_z(first_shard)
    first_pack = gather_y(first_shard, first_z, apart=True)
    table = jnp.concatenate(
        [
            ref[start + depth : start + depth + extra, :depth]
            for ref in first_pack
            for start in range(0, ref.shape[0], depth + extra)
        ],
        axis=1,
    ).astype(F32)

    biases = [
        jnp.stack([query_value_bias[l, 0], jnp.zeros((local,), BF), query_value_bias[l, 1]]).astype(F32)
        for l in range(LAYERS)
    ]
    up_biases = [up_bias[l].astype(F32).reshape(1, hidden) for l in range(LAYERS)]

    x_half, x_oth = to_relative(tokens)
    n_own = norm_stats(x_half.astype(F32))[0]
    n_oth = norm_stats(x_oth.astype(F32))[0]
    h_own, h_oth, qkv_sent = first_qkv(order, n_own, n_oth, table, 0, biases[0], first_pack, depth, extra)

    out_up_shard = tie(jnp.concatenate([out_weight[0], up_weight[0]], axis=1), *first_z)
    out_up_z = gather_z(out_up_shard)
    out_up = gather_y(out_up_shard, out_up_z)
    out_packs, qkv_packs, up_packs = [(out_up, 0)], [(first_pack, 0, extra)], [(out_up, local)]
    next_out_qkv = whole_gather(
        tie(jnp.concatenate([out_weight[1], *qkv_shard(1)], axis=1), *first_z)
    )
    down_shard = tie(down_weight[0], *out_up_z)
    down_z = gather_z(down_shard, True)
    down_packs = [(gather_y(down_shard, down_z), 0)]
    out_packs.append(([next_out_qkv], 0))
    qkv_packs.append(([next_out_qkv], local, 0))

    records = []
    last_other = last_own = None
    for l in range(LAYERS):
        row = l * NORM_ROWS
        qkv = across(qkv_sent)
        if l == 0:
            next_mlp = whole_gather(
                tie(jnp.concatenate([up_weight[1], down_weight[1]], axis=1), next_out_qkv)
            )
            up_packs.append(([next_mlp], 0))
            down_packs.append(([next_mlp], hidden))
        o_stream, lse = attend(qkv, source, slope, segments)
        o_rows = across(o_stream)
        if l == 0:
            o_rows = tie(o_rows, *down_z)
        other = out_project(order, o_rows, *out_packs[l], depth, width, half, BF)
        own = out_project(order, tie(o_rows, other), *out_packs[l], depth, width, 0, F32)
        a, b = tensor_sum(other, own)
        y_half, h2_own = add_norm(x_half, a, b, table, row + 3, row + 1, row + 4)
        h2_oth = sibling(h2_own)
        u, other, own = mlp_forward(order, h2_own, h2_oth, up_biases[l], up_packs[l], down_packs[l], depth)
        records.append((x_half, h_own, h_oth, qkv, lse, o_rows, y_half, h2_own, h2_oth, u))
        if l + 1 < LAYERS:
            a, b = tensor_sum(other, own)
            following = row + NORM_ROWS
            x_half, h_own = add_norm(y_half, a, b, table, row + 5, following, following + 2)
            h_oth = sibling(h_own)
            qkv_sent = qkv_project(order, h_own, h_oth, biases[l + 1], *qkv_packs[l + 1][:2], depth)
        else:
            last_other, last_own = other, own

    gz_own, gz_oth = to_relative(cotangent)
    gx_half = gz_own.astype(F32)
    sums = [None] * LAYERS
    late = [None] * LAYERS
    for l in reversed(range(LAYERS)):
        row = l * NORM_ROWS
        x_half, h_own, h_oth, qkv, lse, o_rows, y_half, h2_own, h2_oth, u = records[l]
        act, gu, up_sum, other, own = mlp_backward(order, gz_own, gz_oth, u, up_packs[l], down_packs[l], depth)
        a, b = tensor_sum(other, own)
        total = late_grad(order, (gz_own, gz_oth, h2_own, h2_oth, tie(act, a), gu), ())
        b = tie(b, total)
        late[l] = whole_scatter(tie(total, *late[l + 1 :]))
        gy_half, ga_own, sums_two = norm_backward(gx_half, a, b, y_half, table, row + 1)
        ga_oth = sibling(ga_own)
        g_stream = across(out_backward(order, ga_own, ga_oth, *out_packs[l], depth, local))
        if l == LAYERS - 1:
            a, b = tensor_sum(tie(last_other, g_stream), last_own)
            final_half = y_half + (a.astype(F32) + b.astype(F32) + table[row + 5])
            final_low = final_half.astype(BF)
            block_output = from_relative(final_low, sibling(final_low))
        if l < LAYERS - 1:
            g_stream = tie(g_stream, *above_came)
        g_sent = attend_backward(qkv, g_stream, lse, source, slope, segments)
        g_rows = across(g_sent)
        if l < LAYERS - 1:
            above_sums = part_sum(
                order, tie(above[0], g_sent), jnp.zeros((nc, 16, 4 * local), F32), above_came
            )
            g_rows = tie(g_rows, above_sums)
        g_proj, qkv_sum, other, own = qkv_backward(
            order, g_rows, qkv_packs[l][0], qkv_packs[l][1], depth, qkv_packs[l][2], width
        )
        a, b = tensor_sum(other, own)
        sources = (order, ga_own, ga_oth, o_rows, h_own, h_oth)
        if l > 0:
            above = attention_grad(0, 4, *sources, tie(g_proj, a), nf)
            above_came = send_y(above)
            b = tie(b, *above)
        else:
            above = across(tie(above_sums, g_proj))
            out_q = attention_grad(0, 2, *sources, tie(g_proj, a), nf)
            out_q_came = send_y(out_q)
            last_parts = attention_grad(2, 4, *sources, tie(g_proj, *out_q), nf)
            last_came = send_y(last_parts)
            b = tie(b, *last_parts)
        gx_half, gz_own, sums_one = norm_backward(gy_half, a, b, x_half, table, row)
        if l > 0:
            gz_oth = sibling(gz_own)
        sums[l] = (sums_one, sums_two, qkv_sum, up_sum)
    grad_tokens = from_relative(gx_half, sibling(gx_half))

    norm_all = jnp.concatenate([sums[l][which] for l in range(LAYERS) for which in (0, 1)], axis=0)
    bias_all = jnp.concatenate(
        [sums[l][2][:, :local] for l in range(LAYERS)]
        + [sums[l][2][:, 2 * local :] for l in range(LAYERS)]
        + [sums[l][3] for l in range(LAYERS)],
        axis=1,
    ).reshape(-1, depth)
    count = norm_all.shape[0]
    norm_total = norm_all[:, :span]
    bias_total = bias_all
    for bit in range(1, nf):
        sent = jnp.concatenate(
            [norm_all[:, bit * span + b * depth : bit * span + (b + 1) * depth] for b in range(nc)] + [bias_all],
            axis=0,
        )
        came = swap(sent, "fsdp", nf, bit)
        norm_total = norm_total + jnp.concatenate(
            [came[b * count : (b + 1) * count] for b in range(nc)], axis=1
        )
        bias_total = bias_total + came[nc * count :]
    cols = last_parts[0].shape[1]
    held = count * depth + bias_total.size
    extra_rows = -(-held // (16 * cols)) * 16
    small = jnp.concatenate(
        [
            norm_total.reshape(count, nc, depth).transpose(1, 0, 2).reshape(nc, -1),
            jnp.broadcast_to(bias_total.reshape(1, -1), (nc, bias_total.size)),
            jnp.zeros((nc, extra_rows * cols - held), F32),
        ],
        axis=1,
    ).reshape(nc, extra_rows, cols)
    nothing = jnp.zeros((nc, 16, cols), F32)
    out_q_sums = part_sum(order, tie(out_q[0], above), nothing, out_q_came)
    out_q_pieces = across(out_q_sums)
    last_sums = part_sum(order, tie(last_parts[0], out_q_pieces, late[0]), small, last_came)
    last_pieces = across(last_sums)
    small = jnp.sum(last_pieces[:, depth:, :].astype(F32), axis=0).reshape(-1)
    norm_mine = small[: count * depth].reshape(count, depth)
    bias_sum = small[count * depth : held]
    grad_up, grad_down = final_sums(
        [[(l, l, col) for l in range(LAYERS)] for col in (0, hidden)],
        [shaped((LAYERS, depth, hidden), F32)] * 2,
        late,
    )
    qkv_plan = [((1, i), 1, (i + 1) * local) for i in range(3)]
    qkv_plan += [((0, 0), 2, local), ((0, 1), 0, 0), ((0, 2), 0, local)]
    grad_out, grad_qkv = final_sums(
        [[(0, 2, 0), (1, 1, 0)], qkv_plan],
        [shaped((LAYERS, depth, local), F32), shaped((LAYERS, 3, depth, local), F32)],
        [last_pieces, above, out_q_pieces],
    )
    grad_qkv = grad_qkv.transpose(0, 2, 1, 3)

    norm_mine = (norm_mine + sibling(norm_mine)).reshape(LAYERS, 2, 8, depth)
    grad_gains = norm_mine[:, :, 0].transpose(0, 2, 1)
    grad_shifts = jnp.stack(
        [norm_mine[:, 0, 1], norm_mine[:, 1, 2], norm_mine[:, 1, 1], norm_mine[:, 1, 3]], axis=1
    ).transpose(0, 2, 1)
    queries, values = bias_sum[: LAYERS * local], bias_sum[LAYERS * local : 2 * LAYERS * local]
    grad_bias = jnp.stack([queries.reshape(LAYERS, local), values.reshape(LAYERS, local)], axis=1)
    grad_up_bias = bias_sum[2 * LAYERS * local :].reshape(LAYERS, hidden)

    return (
        block_output,
        grad_tokens,
        grad_qkv,
        grad_out,
        grad_up,
        grad_down,
        grad_bias,
        grad_up_bias,
        grad_gains,
        grad_shifts,
    )


def solution(mesh):
    placed = (
        P(("fsdp", "ctx"), None),
        P(("fsdp", "ctx"), None),
        P("fsdp", None),
        P("fsdp", None),
        P(None, ("fsdp", "ctx"), None, "tp"),
        P(None, ("fsdp", "ctx"), "tp"),
        P(None, ("fsdp", "ctx"), "tp"),
        P(None, ("fsdp", "ctx"), "tp"),
        P(None, None, "tp"),
        P(None, "tp"),
        P(None, ("fsdp", "ctx"), None),
        P(None, ("fsdp", "ctx"), None),
    )
    return jax.shard_map(
        partial(on_device, mesh.shape["fsdp"], mesh.shape["ctx"], mesh.shape["tp"]),
        mesh=mesh,
        in_specs=placed,
        out_specs=(
            P(("fsdp", "ctx"), None),
            P(("fsdp", "ctx"), None),
            P(None, ("fsdp", "ctx"), None, "tp"),
            P(None, ("fsdp", "ctx"), "tp"),
            P(None, ("fsdp", "ctx"), "tp"),
            P(None, ("fsdp", "ctx"), "tp"),
            P(None, None, "tp"),
            P(None, "tp"),
            P(None, ("fsdp", "ctx"), None),
            P(None, ("fsdp", "ctx"), None),
        ),
        check_vma=False,
    )
```

```python
from functools import partial

import jax
import jax.numpy as jnp
from jax import lax
from jax.experimental import pallas as pl
from jax.experimental.pallas import tpu as pltpu
from jax.sharding import PartitionSpec as P

HEADS = 16
HD = 64
BLK = 128
RUN_BLOCKS = 8
LAYERS = 2
NORM_ROWS = 8
NORM_EPS = 1e-05
MASKED = -1000000000.0
QB = 256
GELU_A = 0.7978845608028654
GELU_B = 0.044715
BF = jnp.bfloat16
F32 = jnp.float32
NN = ((1,), (0,))
NT = ((1,), (1,))
VMEM_LIMIT = 40 * 1024 * 1024


def dot(left, right, dims=NN):
    return lax.dot_general(left, right, (dims, ((), ())), preferred_element_type=F32)


def shaped(shape, dtype):
    return jax.ShapeDtypeStruct(shape, dtype)


def whole():
    return pl.BlockSpec(memory_space=pltpu.VMEM)


def params(flops, bytes_accessed, transcendentals=0):
    return dict(
        compiler_params=pltpu.CompilerParams(vmem_limit_bytes=VMEM_LIMIT),
        cost_estimate=pl.CostEstimate(
            flops=int(flops), bytes_accessed=int(bytes_accessed), transcendentals=int(transcendentals)
        ),
    )


def rows_of(order, refs, col, cols, depth, extra=0):
    pieces = []
    if all(ref.shape == refs[0].shape for ref in refs):
        held = refs[0].shape[0] // depth
        for number in range(order.shape[0]):
            start = pl.multiple_of(lax.rem(order[number], held) * depth, depth)
            pieces.append(refs[number // held][pl.ds(start, depth), col : col + cols])
        return jnp.concatenate(pieces, axis=0)
    for ref in refs:
        for start in range(0, ref.shape[0], depth + extra):
            pieces.append(ref[start : start + depth, col : col + cols])
    return jnp.concatenate(pieces, axis=0)


def call(kernel, out_shape, args, flops, scratch=(), transcendentals=0, smem=0):
    outs = out_shape if isinstance(out_shape, (list, tuple)) else [out_shape]
    moved = sum(a.size * a.dtype.itemsize for a in args) + sum(
        o.size * jnp.dtype(o.dtype).itemsize for o in outs
    )
    specs = [pl.BlockSpec(memory_space=pltpu.SMEM)] * smem + [whole()] * (len(args) - smem)
    return pl.pallas_call(
        kernel,
        in_specs=specs,
        out_specs=[whole()] * len(outs) if outs is out_shape else whole(),
        out_shape=out_shape,
        scratch_shapes=list(scratch),
        **params(flops, moved, transcendentals),
    )(*args)


def norm_stats(values):
    average = jnp.mean(values, axis=-1, keepdims=True)
    centred = values - average
    variance = jnp.mean(centred * centred, axis=-1, keepdims=True)
    scale = lax.rsqrt(variance + NORM_EPS)
    return centred * scale, scale


def gelu_parts(u):
    inner = GELU_A * (u + GELU_B * u * u * u)
    t = jnp.tanh(inner)
    return t


def add_norm_kernel(bias_row, gain_row, shift_row, x_ref, a_ref, b_ref, table_ref, y_ref, h_ref):
    branch = a_ref[...].astype(F32) + b_ref[...].astype(F32) + table_ref[bias_row : bias_row + 1, :]
    y = x_ref[...].astype(F32) + branch
    y_ref[...] = y
    n, _ = norm_stats(y)
    h_ref[...] = (
        n * table_ref[gain_row : gain_row + 1, :] + table_ref[shift_row : shift_row + 1, :]
    ).astype(BF)


def add_norm(x, a, b, table, bias_row, gain_row, shift_row):
    rows, width = x.shape
    return call(
        partial(add_norm_kernel, bias_row, gain_row, shift_row),
        [shaped((rows, width), F32), shaped((rows, width), BF)],
        [x, a, b, table],
        rows * width * 12,
    )


def heads_out(out_ref, total, number, row):
    half = total.shape[0]
    turned = total.astype(BF).T
    for j in range(out_ref.shape[0]):
        out_ref[j, row : row + HD, number * half : (number + 1) * half] = turned[j * HD : (j + 1) * HD, :]


def qkv_rows(order, h_refs, bias_ref, w_refs, out_ref, col, depth, extra):
    local = out_ref.shape[0] * HD
    h = jnp.concatenate([h_ref[...] for h_ref in h_refs], axis=0)
    for i in range(3):
        weights = rows_of(order, w_refs, col + i * local, local, depth, extra)
        heads_out(out_ref, dot(h, weights) + bias_ref[i : i + 1, :], 0, i * HD)


def qkv_kernel(col, depth, order, h_own, h_oth, bias_ref, *refs):
    qkv_rows(order, [h_own, h_oth], bias_ref, refs[:-1], refs[-1], col, depth, 0)


def qkv_project(order, h_own, h_oth, bias, pack, col, depth):
    half, width = h_own.shape
    local = bias.shape[1]
    return call(
        partial(qkv_kernel, col, depth),
        shaped((local // HD, 3 * HD, 2 * half), BF),
        [order, h_own, h_oth, bias, *pack],
        12 * half * width * local,
        smem=1,
    )


def first_qkv_kernel(row, depth, extra, order, n_own, n_oth, table_ref, bias_ref, *refs):
    w_refs, (h_own, h_oth, out_ref) = refs[:-3], refs[-3:]
    for n_ref, h_ref in ((n_own, h_own), (n_oth, h_oth)):
        h_ref[...] = (n_ref[...] * table_ref[row : row + 1, :] + table_ref[row + 2 : row + 3, :]).astype(BF)
    qkv_rows(order, [h_own, h_oth], bias_ref, w_refs, out_ref, 0, depth, extra)


def first_qkv(order, n_own, n_oth, table, row, bias, pack, depth, extra):
    half, width = n_own.shape
    local = bias.shape[1]
    return call(
        partial(first_qkv_kernel, row, depth, extra),
        [
            shaped((half, width), BF),
            shaped((half, width), BF),
            shaped((local // HD, 3 * HD, 2 * half), BF),
        ],
        [order, n_own, n_oth, table, bias, *pack],
        12 * half * width * local,
        smem=1,
    )


def out_kernel(col, depth, start, order, o_ref, *refs):
    w_refs, out_ref = refs[:-1], refs[-1]
    half = out_ref.shape[0]
    heads = o_ref.shape[0]
    o = jnp.concatenate([o_ref[j, :, start : start + half] for j in range(heads)], axis=0).T
    weights = rows_of(order, w_refs, col, heads * HD, depth)
    out_ref[...] = dot(o, weights, NT).astype(out_ref.dtype)


def out_project(order, o_rows, pack, col, depth, width, start, dtype):
    heads, _, rows = o_rows.shape
    half = rows // 2
    return call(
        partial(out_kernel, col, depth, start),
        shaped((half, width), dtype),
        [order, o_rows, *pack],
        2 * half * width * heads * HD,
        smem=1,
    )


def mlp_kernel(counts, up_col, down_col, depth, order, h_own, h_oth, bias_ref, *refs):
    ups, downs = refs[: counts[0]], refs[counts[0] : counts[0] + counts[1]]
    u_ref, oth_ref, own_ref = refs[counts[0] + counts[1] :]
    half = h_own.shape[0]
    hidden = u_ref.shape[1]
    h = jnp.concatenate([h_own[...], h_oth[...]], axis=0)
    u = dot(h, rows_of(order, ups, up_col, hidden, depth)) + bias_ref[...]
    u_ref[...] = u
    act = (0.5 * u * (1.0 + gelu_parts(u))).astype(BF)
    total = dot(act, rows_of(order, downs, down_col, hidden, depth), NT)
    own_ref[...] = total[:half, :]
    oth_ref[...] = total[half:, :].astype(BF)


def mlp_forward(order, h_own, h_oth, bias, up, down, depth):
    half, width = h_own.shape
    hidden = bias.shape[1]
    return call(
        partial(mlp_kernel, (len(up[0]), len(down[0])), up[1], down[1], depth),
        [
            shaped((2 * half, hidden), F32),
            shaped((half, width), BF),
            shaped((half, width), F32),
        ],
        [order, h_own, h_oth, bias, *up[0], *down[0]],
        8 * half * width * hidden,
        transcendentals=2 * half * hidden,
        smem=1,
    )


def mlp_back_kernel(counts, up_col, down_col, depth, order, g_own, g_oth, u_ref, *refs):
    ups, downs = refs[: counts[0]], refs[counts[0] : counts[0] + counts[1]]
    act_ref, gu_ref, sum_ref, oth_ref, own_ref = refs[counts[0] + counts[1] :]
    half = g_own.shape[0]
    hidden = u_ref.shape[1]
    g = jnp.concatenate([g_own[...], g_oth[...]], axis=0)
    grad = dot(g, rows_of(order, downs, down_col, hidden, depth))
    u = u_ref[...]
    t = gelu_parts(u)
    act_ref[...] = (0.5 * u * (1.0 + t)).astype(BF)
    slope = 0.5 * (1.0 + t) + 0.5 * u * (1.0 - t * t) * (GELU_A * (1.0 + 3.0 * GELU_B * u * u))
    gu = (grad * slope).astype(BF)
    gu_ref[...] = gu
    sum_ref[...] = jnp.sum(gu.astype(F32), axis=0, keepdims=True)
    total = dot(gu, rows_of(order, ups, up_col, hidden, depth), NT)
    own_ref[...] = total[:half, :]
    oth_ref[...] = total[half:, :].astype(BF)


def mlp_backward(order, g_own, g_oth, u, up, down, depth):
    half, width = g_own.shape
    hidden = u.shape[1]
    return call(
        partial(mlp_back_kernel, (len(up[0]), len(down[0])), up[1], down[1], depth),
        [
            shaped((2 * half, hidden), BF),
            shaped((2 * half, hidden), BF),
            shaped((1, hidden), F32),
            shaped((half, width), BF),
            shaped((half, width), F32),
        ],
        [order, g_own, g_oth, u, *up[0], *down[0]],
        8 * half * width * hidden,
        transcendentals=2 * half * hidden,
        smem=1,
    )


def grads_out(order, out_refs, total, col):
    cols = slice(col, col + total.shape[1])
    if len(out_refs) == 1:
        depth = total.shape[0] // order.shape[0]
        for number in range(order.shape[0]):
            start = pl.multiple_of(order[number] * depth, depth)
            out_refs[0][pl.ds(start, depth), cols] = total[number * depth : (number + 1) * depth].astype(BF)
        return
    span = out_refs[0].shape[0]
    for y, out_ref in enumerate(out_refs):
        out_ref[:, cols] = total[y * span : (y + 1) * span].astype(BF)


def late_grad_kernel(count, order, *refs):
    g_own, g_oth, h_own, h_oth, act_ref, gu_ref = refs[:6]
    out_refs = refs[count:]
    hidden = act_ref.shape[1]
    h = jnp.concatenate([h_own[...], h_oth[...]], axis=0).T
    grads_out(order, out_refs, dot(h, gu_ref[...]), 0)
    g = jnp.concatenate([g_own[...], g_oth[...]], axis=0).T
    grads_out(order, out_refs, dot(g, act_ref[...]), hidden)
    if count > 6:
        attention_grad_body(0, 4, 2 * hidden, order, *refs[6:count], out_refs)


def late_grad(order, mlp, attention):
    half, width = mlp[0].shape
    cols = 2 * mlp[4].shape[1]
    if attention:
        cols += 4 * attention[2].shape[0] * HD
    args = [*mlp, *attention]
    return call(
        partial(late_grad_kernel, len(args)),
        [shaped((width, cols), BF)],
        [order, *args],
        4 * half * width * cols,
        smem=1,
    )[0]


def attention_grad_body(first, last, col, order, g_own, g_oth, o_ref, h_own, h_oth, p_ref, out_refs):
    heads = o_ref.shape[0]
    local = heads * HD
    if first == 0:
        g = jnp.concatenate([g_own[...], g_oth[...]], axis=0).T
        o = jnp.concatenate([o_ref[j] for j in range(heads)], axis=0)
        grads_out(order, out_refs, dot(g, o, NT), col)
        col += local
        first = 1
    h = jnp.concatenate([h_own[...], h_oth[...]], axis=0).T
    grads_out(order, out_refs, dot(h, p_ref[:, (first - 1) * local : (last - 1) * local]), col)


def attention_grad_kernel(first, last, order, *refs):
    attention_grad_body(first, last, 0, order, *refs[:6], refs[6:])


def attention_grad(first, last, order, g_own, g_oth, o_rows, h_own, h_oth, g_proj, nf):
    half, width = g_own.shape
    local = o_rows.shape[0] * HD
    cols = (last - first) * local
    return call(
        partial(attention_grad_kernel, first, last),
        [shaped((width // nf, cols), BF)] * nf,
        [order, g_own, g_oth, o_rows, h_own, h_oth, g_proj],
        4 * half * width * cols,
        smem=1,
    )


def part_sum_kernel(order, own_ref, small_ref, *refs):
    came, out_ref = refs[:-1], refs[-1]
    slots = out_ref.shape[0]
    depth = own_ref.shape[0] // slots
    for number in range(slots):
        rows = slice(number * depth, (number + 1) * depth)
        total = own_ref[rows, :].astype(F32)
        for ref in came:
            total = total + ref[rows, :].astype(F32)
        slot = lax.rem(order[number], slots)
        out_ref[slot, :depth, :] = total.astype(BF)
        out_ref[slot, depth:, :] = small_ref[number].astype(BF)


def part_sum(order, own, small, came):
    rows, cols = own.shape
    slots, extra, _ = small.shape
    return call(
        part_sum_kernel,
        shaped((slots, rows // slots + extra, cols), BF),
        [order, own, small, *came],
        rows * cols * 2,
        smem=1,
    )


def part_pieces_kernel(own_ref, small_ref, *refs):
    slots, extra, _ = small_ref.shape
    came, outs = refs[:-slots], refs[-slots:]
    depth = own_ref.shape[0] // slots
    for number, out_ref in enumerate(outs):
        rows = slice(number * depth, (number + 1) * depth)
        total = own_ref[rows, :].astype(F32)
        for ref in came:
            total = total + ref[rows, :].astype(F32)
        out_ref[:depth, :] = total.astype(BF)
        out_ref[depth:, :] = small_ref[number].astype(BF)


def part_pieces(own, small, came):
    rows, cols = own.shape
    slots, extra, _ = small.shape
    return call(
        part_pieces_kernel,
        [shaped((rows // slots + extra, cols), BF)] * slots,
        [own, small, *came],
        rows * cols * 2,
    )


def final_kernel(plans, *refs):
    outs = refs[-len(plans) :]
    for out_ref, plan in zip(outs, plans):
        cols = out_ref.shape[-1]
        for index, which, col in plan:
            if isinstance(which, tuple):
                rows = slice(0, out_ref.shape[-2])
                total = refs[which[0]][rows, col : col + cols].astype(F32)
                for other in which[1:]:
                    total = total + refs[other][rows, col : col + cols].astype(F32)
                out_ref[index] = total
                continue
            ref = refs[which]
            if len(ref.shape) == 2:
                out_ref[index] = ref[: out_ref.shape[-2], col : col + cols].astype(F32)
                continue
            rows = slice(0, out_ref.shape[-2])
            total = ref[0, rows, col : col + cols].astype(F32)
            for slot in range(1, ref.shape[0]):
                total = total + ref[slot, rows, col : col + cols].astype(F32)
            out_ref[index] = total


def final_sums(plans, shapes, pieces):
    return call(partial(final_kernel, plans), shapes, pieces, sum(p.size for p in pieces))


def norm_back_kernel(gain_row, gx_ref, a_ref, b_ref, y_ref, table_ref, gy_ref, low_ref, sums_ref):
    grad = a_ref[...].astype(F32) + b_ref[...].astype(F32)
    n, scale = norm_stats(y_ref[...].astype(F32))
    e = grad * table_ref[gain_row : gain_row + 1, :]
    mean_e = jnp.mean(e, axis=-1, keepdims=True)
    mean_en = jnp.mean(e * n, axis=-1, keepdims=True)
    gx = gx_ref[...].astype(F32)
    gy = gx + scale * (e - mean_e - n * mean_en)
    gy_ref[...] = gy
    low = gy.astype(BF)
    low_ref[...] = low
    sums_ref[0:1, :] = jnp.sum(grad * n, axis=0, keepdims=True)
    sums_ref[1:2, :] = jnp.sum(grad, axis=0, keepdims=True)
    sums_ref[2:3, :] = jnp.sum(low.astype(F32), axis=0, keepdims=True)
    sums_ref[3:4, :] = jnp.sum(gx.astype(BF).astype(F32), axis=0, keepdims=True)
    sums_ref[4:, :] = jnp.zeros((4, gx.shape[1]), F32)


def norm_backward(gx, a, b, y, table, gain_row):
    rows, width = gx.shape
    return call(
        partial(norm_back_kernel, gain_row),
        [shaped((rows, width), F32), shaped((rows, width), BF), shaped((8, width), F32)],
        [gx, a, b, y, table],
        rows * width * 25,
    )


def out_back_kernel(col, depth, order, g_own, g_oth, *refs):
    w_refs, out_ref = refs[:-1], refs[-1]
    g = jnp.concatenate([g_own[...], g_oth[...]], axis=0)
    heads_out(out_ref, dot(g, rows_of(order, w_refs, col, out_ref.shape[0] * HD, depth)), 0, 0)


def out_backward(order, g_own, g_oth, pack, col, depth, local):
    half, width = g_own.shape
    return call(
        partial(out_back_kernel, col, depth),
        shaped((local // HD, HD, 2 * half), BF),
        [order, g_own, g_oth, *pack],
        4 * half * width * local,
        smem=1,
    )


def qkv_back_kernel(col, depth, extra, order, g_ref, *refs):
    w_refs, (rows_ref, sum_ref, oth_ref, own_ref) = refs[:-4], refs[-4:]
    heads = g_ref.shape[0]
    half = own_ref.shape[0]
    local = heads * HD
    planes = [
        jnp.concatenate([g_ref[j, i * HD : (i + 1) * HD, :] for j in range(heads)], axis=0).T
        for i in range(3)
    ]
    grads = jnp.concatenate(planes, axis=1)
    rows_ref[...] = grads
    total = dot(grads, rows_of(order, w_refs, col, 3 * local, depth, extra), NT)
    oth_ref[...] = total[half:].astype(BF)
    own_ref[...] = total[:half]
    sum_ref[...] = jnp.sum(grads.astype(F32), axis=0, keepdims=True)


def qkv_backward(order, g, pack, col, depth, extra, width):
    heads, _, rows = g.shape
    half = rows // 2
    cols = 3 * heads * HD
    return call(
        partial(qkv_back_kernel, col, depth, extra),
        [
            shaped((rows, cols), BF),
            shaped((1, cols), F32),
            shaped((half, width), BF),
            shaped((half, width), F32),
        ],
        [order, g, *pack],
        2 * rows * width * cols,
        smem=1,
    )


def gather_blocks(source_ref, src_ref, dest_ref, per_device):
    for s in range(dest_ref.shape[1] // BLK):
        src = src_ref[s]
        z = src // per_device
        start = pl.multiple_of((src - z * per_device) * BLK, BLK)
        dest_ref[:, s * BLK : (s + 1) * BLK] = source_ref[z, :, pl.ds(start, BLK)]


def scatter_blocks(dest_ref, src_ref, source, per_device, low, first):
    depth, columns = source.shape
    for s in range(columns // BLK):
        src = src_ref[first + s]
        z = src // per_device
        start = pl.multiple_of((src - z * per_device) * BLK, BLK)
        dest_ref[z, low : low + depth, pl.ds(start, BLK)] = source[:, s * BLK : (s + 1) * BLK]


def segment_columns(seg_ref, column_ref):
    for s in range(seg_ref.shape[1] // BLK):
        row = seg_ref[:, s * BLK : (s + 1) * BLK]
        row = jnp.where(row < 0, -2, row).astype(F32)
        column_ref[s * BLK : (s + 1) * BLK, :] = jnp.broadcast_to(row, (BLK, BLK)).T


def score_tile(keys, queries, column_ref, seg_ref, slope, base, first, last):
    depth = keys.shape[0]
    width = last - first
    scores = dot(keys, queries)
    key_row = lax.broadcasted_iota(jnp.int32, (depth, width), 0)
    query_row = lax.broadcasted_iota(jnp.int32, (depth, width), 1) + (first - base)
    distance = query_row - key_row
    scores = scores - slope * distance.astype(F32)
    columns = column_ref[base : base + depth, :]
    key_seg = jnp.concatenate([columns] * (width // BLK), axis=1)
    query_seg = seg_ref[:, first:last].astype(F32)
    allowed = ((key_seg == query_seg) & (distance >= 0)) | (distance == 0)
    return scores, allowed


def attend_kernel(per_device, src_ref, slope_ref, seg_ref, qkv_ref, o_ref, lse_ref, stream_ref, column_ref):
    gather_blocks(qkv_ref, src_ref, stream_ref, per_device)
    segment_columns(seg_ref, column_ref)
    slope = slope_ref[0]
    run = RUN_BLOCKS * BLK
    for base in range(0, stream_ref.shape[1], run):
        keys = stream_ref[HD : 2 * HD, base : base + run].T
        for first in range(base, base + run, QB):
            last = first + QB
            depth = last - base
            queries = stream_ref[:HD, first:last] * jnp.asarray(HD**-0.5, BF)
            scores, allowed = score_tile(
                keys[:depth], queries, column_ref, seg_ref, slope, base, first, last
            )
            scores = jnp.where(allowed, scores, MASKED)
            top = jnp.max(scores, axis=0, keepdims=True)
            weights = jnp.exp(scores - top)
            total = jnp.sum(weights, axis=0, keepdims=True)
            lse_ref[:, first:last] = top + jnp.log(total)
            values = stream_ref[2 * HD :, base : base + depth]
            out = (dot(values, weights.astype(BF)) / total).astype(BF)
            scatter_blocks(o_ref, src_ref, out, per_device, 0, first // BLK)


def attend(qkv, source, slope, segments):
    nc, depth, rows = qkv.shape
    length = nc * rows
    smem = pl.BlockSpec(memory_space=pltpu.SMEM)
    return pl.pallas_call(
        partial(attend_kernel, rows // BLK),
        in_specs=[smem, smem, whole(), whole()],
        out_specs=[whole(), whole()],
        out_shape=[shaped((nc, HD, rows), BF), shaped((1, length), F32)],
        scratch_shapes=[pltpu.VMEM((3 * HD, length), BF), pltpu.VMEM((length, BLK), F32)],
        **params(length * RUN_BLOCKS * BLK * HD * 3, length * HD * 8, length * RUN_BLOCKS * BLK // 2),
    )(source, slope, segments, qkv)


def attend_back_kernel(
    per_device, src_ref, slope_ref, seg_ref, qkv_ref, g_ref, lse_ref, out_ref, stream_ref, grad_ref, column_ref, k_acc, v_acc
):
    gather_blocks(qkv_ref, src_ref, stream_ref, per_device)
    gather_blocks(g_ref, src_ref, grad_ref, per_device)
    segment_columns(seg_ref, column_ref)
    slope = slope_ref[0]
    run = RUN_BLOCKS * BLK
    scale = HD**-0.5
    for base in range(0, stream_ref.shape[1], run):
        rows = slice(base, base + run)
        keys_turned = stream_ref[HD : 2 * HD, rows]
        keys = keys_turned.T
        values = stream_ref[2 * HD :, rows].T
        queries_rows = stream_ref[:HD, rows].T
        grads_rows = grad_ref[:, rows].T
        for first in range(base + run - QB, base - 1, -QB):
            last = first + QB
            depth = last - base
            inner = slice(first - base, last - base)
            queries = stream_ref[:HD, first:last] * jnp.asarray(scale, BF)
            scores, allowed = score_tile(
                keys[:depth], queries, column_ref, seg_ref, slope, base, first, last
            )
            weights = jnp.where(allowed, jnp.exp(scores - lse_ref[:, first:last]), 0.0)
            back = dot(values[:depth], grad_ref[:, first:last])
            delta = jnp.sum(weights * back, axis=0, keepdims=True)
            low = (weights * (back - delta)).astype(BF)
            v_piece = dot(weights.astype(BF), grads_rows[inner])
            k_piece = dot(low, queries_rows[inner])
            if depth == run:
                v_acc[...] = v_piece
                k_acc[...] = k_piece
            else:
                v_acc[:depth, :] += v_piece
                k_acc[:depth, :] += k_piece
            q_grad = (dot(keys_turned[:, :depth], low) * scale).astype(BF)
            scatter_blocks(out_ref, src_ref, q_grad, per_device, 0, first // BLK)
        scatter_blocks(out_ref, src_ref, (k_acc[...] * scale).T.astype(BF), per_device, HD, base // BLK)
        scatter_blocks(out_ref, src_ref, v_acc[...].T.astype(BF), per_device, 2 * HD, base // BLK)


def attend_backward(qkv, grads, lse, source, slope, segments):
    nc, depth, rows = qkv.shape
    length = nc * rows
    run = RUN_BLOCKS * BLK
    smem = pl.BlockSpec(memory_space=pltpu.SMEM)
    return pl.pallas_call(
        partial(attend_back_kernel, rows // BLK),
        in_specs=[smem, smem, whole(), whole(), whole(), whole()],
        out_specs=whole(),
        out_shape=shaped((nc, depth, rows), BF),
        scratch_shapes=[
            pltpu.VMEM((3 * HD, length), BF),
            pltpu.VMEM((HD, length), BF),
            pltpu.VMEM((length, BLK), F32),
            pltpu.VMEM((run, HD), F32),
            pltpu.VMEM((run, HD), F32),
        ],
        **params(length * run * HD * 7, length * HD * 16, length * run // 2),
    )(source, slope, segments, qkv, grads, lse)


def to_relative_kernel(place_ref, value_ref, own_ref, oth_ref):
    half = own_ref.shape[0]
    for ref, side in ((own_ref, place_ref[0]), (oth_ref, 1 - place_ref[0])):
        rows = pl.ds(pl.multiple_of(side * half, half), half)
        for number in range(place_ref.shape[0] - 1):
            depth = value_ref.shape[1] // (place_ref.shape[0] - 1)
            start = pl.multiple_of(place_ref[number + 1] * depth, depth)
            ref[:, number * depth : (number + 1) * depth] = value_ref[rows, pl.ds(start, depth)]


def from_relative_kernel(place_ref, own_ref, oth_ref, value_ref):
    half = own_ref.shape[0]
    for ref, side in ((own_ref, place_ref[0]), (oth_ref, 1 - place_ref[0])):
        rows = pl.ds(pl.multiple_of(side * half, half), half)
        for number in range(place_ref.shape[0] - 1):
            depth = value_ref.shape[1] // (place_ref.shape[0] - 1)
            start = pl.multiple_of(place_ref[number + 1] * depth, depth)
            value_ref[rows, pl.ds(start, depth)] = ref[:, number * depth : (number + 1) * depth].astype(
                value_ref.dtype
            )


def on_device(
    nf,
    nc,
    nt,
    tokens,
    cotangent,
    block_place,
    segment_ids,
    qkv_weight,
    out_weight,
    up_weight,
    down_weight,
    query_value_bias,
    up_bias,
    norm_gains,
    row_biases,
):
    rows, width = tokens.shape
    half = rows // 2
    depth = qkv_weight.shape[1]
    local = qkv_weight.shape[3]
    heads = local // HD
    hidden = up_weight.shape[2]
    span = nc * depth
    y_index = lax.axis_index("fsdp")
    z_index = lax.axis_index("ctx")
    t_index = lax.axis_index("tp")
    side = t_index % 2

    def swap(value, axis, size, bit):
        return lax.ppermute(value, axis, [(i, i ^ bit) for i in range(size)])

    def sibling(value):
        return swap(value, "tp", nt, 1)

    def across(value):
        return lax.all_to_all(value, "ctx", 0, 0)

    def tie(value, *others):
        return lax.optimization_barrier((value, *others))[0]

    def gather_z(shard, doubling=False):
        if not doubling:
            return [swap(shard, "ctx", nc, bit) for bit in range(1, nc)]
        came, bit = [], 1
        while bit < nc:
            came.append(swap(jnp.concatenate([shard, *came], axis=0) if came else shard, "ctx", nc, bit))
            bit *= 2
        return came

    def gather_y(shard, came, apart=False):
        pack = [shard, *came]
        for bit in range(1, nf):
            if apart:
                own = swap(shard, "fsdp", nf, bit)
                pack.append(own)
                pack.append(swap(tie(jnp.concatenate(came, axis=0), own), "fsdp", nf, bit))
            else:
                pack.append(swap(jnp.concatenate([shard, *came], axis=0), "fsdp", nf, bit))
        return pack

    def whole_gather(shard):
        return lax.all_gather(shard, ("fsdp", "ctx"), axis=0, tiled=True)

    def whole_scatter(total):
        return lax.psum_scatter(total, ("fsdp", "ctx"), scatter_dimension=0, tiled=True)

    def send_y(parts):
        return [swap(parts[bit], "fsdp", nf, bit) for bit in range(1, nf)]

    def tensor_sum(other, own):
        term = (own + sibling(other).astype(F32)).astype(BF)
        bit = 2
        while bit * 2 < nt:
            term = (term.astype(F32) + swap(term, "tp", nt, bit).astype(F32)).astype(BF)
            bit *= 2
        return term, swap(term, "tp", nt, bit)

    order = jnp.stack(
        [(y_index ^ a) * nc + (z_index ^ b) for a in range(nf) for b in range(nc)]
    ).astype(jnp.int32)
    place = jnp.concatenate([side.reshape(1).astype(jnp.int32), order])

    def columns_moved(value):
        return jnp.concatenate(
            [
                lax.dynamic_slice_in_dim(value, order[number] * depth, depth, axis=1)
                for number in range(nf * nc)
            ],
            axis=1,
        )

    def to_relative(value):
        if depth % 128 == 0:
            return call(
                to_relative_kernel,
                [shaped((half, width), value.dtype)] * 2,
                [place, value],
                value.size,
                smem=1,
            )
        moved = columns_moved(value)
        return [lax.dynamic_slice_in_dim(moved, which * half, half) for which in (side, 1 - side)]

    def from_relative(own, oth):
        if depth % 128 == 0:
            return call(
                from_relative_kernel, shaped((rows, width), own.dtype), [place, own, oth], 2 * own.size, smem=1
            )
        return columns_moved(
            jnp.where(side == 0, jnp.concatenate([own, oth], axis=0), jnp.concatenate([oth, own], axis=0))
        )

    per_device = rows // BLK
    count = nc * per_device
    stored_place = block_place[0]
    stored = jnp.arange(count, dtype=jnp.int32)
    relative = (stored // per_device) * per_device + (stored % per_device + side * (per_device // 2)) % per_device
    source = jnp.sum(
        jnp.where(stored_place[None, :] == jnp.arange(count, dtype=jnp.int32)[:, None], relative[None, :], 0), axis=1
    ).astype(jnp.int32)
    head = (t_index * heads + z_index).astype(F32)
    slope = jnp.exp2(-8.0 * (head + 1.0) / HEADS).reshape(1)
    segments = segment_ids

    def qkv_shard(layer):
        return [qkv_weight[layer, :, i, :] for i in range(3)]

    table_rows = []
    for layer in range(LAYERS):
        table_rows += [norm_gains[layer].T, row_biases[layer].T, jnp.zeros((2, depth), BF)]
    table_shard = jnp.concatenate(table_rows, axis=0)
    extra = table_shard.shape[0]
    table_padded = jnp.pad(table_shard, ((0, 0), (0, 3 * local - depth)))
    first_shard = jnp.concatenate([jnp.concatenate(qkv_shard(0), axis=1), table_padded], axis=0)
    first_z = gather_z(first_shard)
    first_pack = gather_y(first_shard, first_z, apart=True)
    table = jnp.concatenate(
        [
            ref[start + depth : start + depth + extra, :depth]
            for ref in first_pack
            for start in range(0, ref.shape[0], depth + extra)
        ],
        axis=1,
    ).astype(F32)

    biases = [
        jnp.stack([query_value_bias[l, 0], jnp.zeros((local,), BF), query_value_bias[l, 1]]).astype(F32)
        for l in range(LAYERS)
    ]
    up_biases = [up_bias[l].astype(F32).reshape(1, hidden) for l in range(LAYERS)]

    x_half, x_oth = to_relative(tokens)
    n_own = norm_stats(x_half.astype(F32))[0]
    n_oth = norm_stats(x_oth.astype(F32))[0]
    h_own, h_oth, qkv_sent = first_qkv(order, n_own, n_oth, table, 0, biases[0], first_pack, depth, extra)

    out_up_shard = tie(jnp.concatenate([out_weight[0], up_weight[0]], axis=1), *first_z)
    out_up_z = gather_z(out_up_shard)
    out_up = gather_y(out_up_shard, out_up_z)
    out_packs, qkv_packs, up_packs = [(out_up, 0)], [(first_pack, 0, extra)], [(out_up, local)]
    next_out_qkv = whole_gather(
        tie(jnp.concatenate([out_weight[1], *qkv_shard(1)], axis=1), *first_z)
    )
    down_shard = tie(down_weight[0], *out_up_z)
    down_z = gather_z(down_shard, True)
    down_packs = [(gather_y(down_shard, down_z), 0)]
    out_packs.append(([next_out_qkv], 0))
    qkv_packs.append(([next_out_qkv], local, 0))

    records = []
    last_other = last_own = None
    for l in range(LAYERS):
        row = l * NORM_ROWS
        qkv = across(qkv_sent)
        if l == 0:
            next_mlp = whole_gather(
                tie(jnp.concatenate([up_weight[1], down_weight[1]], axis=1), next_out_qkv)
            )
            up_packs.append(([next_mlp], 0))
            down_packs.append(([next_mlp], hidden))
        o_stream, lse = attend(qkv, source, slope, segments)
        o_rows = across(o_stream)
        if l == 0:
            o_rows = tie(o_rows, *down_z)
        other = out_project(order, o_rows, *out_packs[l], depth, width, half, BF)
        own = out_project(order, tie(o_rows, other), *out_packs[l], depth, width, 0, F32)
        a, b = tensor_sum(other, own)
        y_half, h2_own = add_norm(x_half, a, b, table, row + 3, row + 1, row + 4)
        h2_oth = sibling(h2_own)
        u, other, own = mlp_forward(order, h2_own, h2_oth, up_biases[l], up_packs[l], down_packs[l], depth)
        records.append((x_half, h_own, h_oth, qkv, lse, o_rows, y_half, h2_own, h2_oth, u))
        if l + 1 < LAYERS:
            a, b = tensor_sum(other, own)
            following = row + NORM_ROWS
            x_half, h_own = add_norm(y_half, a, b, table, row + 5, following, following + 2)
            h_oth = sibling(h_own)
            qkv_sent = qkv_project(order, h_own, h_oth, biases[l + 1], *qkv_packs[l + 1][:2], depth)
        else:
            last_other, last_own = other, own

    gz_own, gz_oth = to_relative(cotangent)
    gx_half = gz_own.astype(F32)
    sums = [None] * LAYERS
    late = [None] * LAYERS
    for l in reversed(range(LAYERS)):
        row = l * NORM_ROWS
        x_half, h_own, h_oth, qkv, lse, o_rows, y_half, h2_own, h2_oth, u = records[l]
        act, gu, up_sum, other, own = mlp_backward(order, gz_own, gz_oth, u, up_packs[l], down_packs[l], depth)
        a, b = tensor_sum(other, own)
        total = late_grad(order, (gz_own, gz_oth, h2_own, h2_oth, tie(act, a), gu), ())
        b = tie(b, total)
        late[l] = whole_scatter(tie(total, *late[l + 1 :]))
        gy_half, ga_own, sums_two = norm_backward(gx_half, a, b, y_half, table, row + 1)
        ga_oth = sibling(ga_own)
        g_stream = across(out_backward(order, ga_own, ga_oth, *out_packs[l], depth, local))
        if l == LAYERS - 1:
            a, b = tensor_sum(tie(last_other, g_stream), last_own)
            final_half = y_half + (a.astype(F32) + b.astype(F32) + table[row + 5])
            final_low = final_half.astype(BF)
            block_output = from_relative(final_low, sibling(final_low))
        if l < LAYERS - 1:
            g_stream = tie(g_stream, *above_came)
        g_sent = attend_backward(qkv, g_stream, lse, source, slope, segments)
        g_rows = across(g_sent)
        if l < LAYERS - 1:
            above_sums = part_sum(
                order, tie(above[0], g_sent), jnp.zeros((nc, 16, 4 * local), F32), above_came
            )
            g_rows = tie(g_rows, above_sums)
        g_proj, qkv_sum, other, own = qkv_backward(
            order, g_rows, qkv_packs[l][0], qkv_packs[l][1], depth, qkv_packs[l][2], width
        )
        a, b = tensor_sum(other, own)
        sources = (order, ga_own, ga_oth, o_rows, h_own, h_oth)
        if l > 0:
            above = attention_grad(0, 4, *sources, tie(g_proj, a), nf)
            above_came = send_y(above)
            b = tie(b, *above)
        else:
            above = across(tie(above_sums, g_proj))
            out_q = attention_grad(0, 2, *sources, tie(g_proj, a), nf)
            out_q_came = send_y(out_q)
            last_parts = attention_grad(2, 4, *sources, tie(g_proj, *out_q), nf)
            last_came = send_y(last_parts)
            b = tie(b, *last_parts)
        gx_half, gz_own, sums_one = norm_backward(gy_half, a, b, x_half, table, row)
        if l > 0:
            gz_oth = sibling(gz_own)
        sums[l] = (sums_one, sums_two, qkv_sum, up_sum)
    grad_tokens = from_relative(gx_half, sibling(gx_half))

    norm_all = jnp.concatenate([sums[l][which] for l in range(LAYERS) for which in (0, 1)], axis=0)
    bias_all = jnp.concatenate(
        [sums[l][2][:, :local] for l in range(LAYERS)]
        + [sums[l][2][:, 2 * local :] for l in range(LAYERS)]
        + [sums[l][3] for l in range(LAYERS)],
        axis=1,
    ).reshape(-1, depth)
    count = norm_all.shape[0]
    norm_total = norm_all[:, :span]
    bias_total = bias_all
    for bit in range(1, nf):
        sent = jnp.concatenate(
            [norm_all[:, bit * span + b * depth : bit * span + (b + 1) * depth] for b in range(nc)] + [bias_all],
            axis=0,
        )
        came = swap(sent, "fsdp", nf, bit)
        norm_total = norm_total + jnp.concatenate(
            [came[b * count : (b + 1) * count] for b in range(nc)], axis=1
        )
        bias_total = bias_total + came[nc * count :]
    cols = last_parts[0].shape[1]
    held = count * depth + bias_total.size
    extra_rows = -(-held // (16 * cols)) * 16
    small = jnp.concatenate(
        [
            norm_total.reshape(count, nc, depth).transpose(1, 0, 2).reshape(nc, -1),
            jnp.broadcast_to(bias_total.reshape(1, -1), (nc, bias_total.size)),
            jnp.zeros((nc, extra_rows * cols - held), F32),
        ],
        axis=1,
    ).reshape(nc, extra_rows, cols)
    nothing = jnp.zeros((nc, 16, cols), F32)
    out_q_sums = part_sum(order, tie(out_q[0], above), nothing, out_q_came)
    out_q_pieces = across(out_q_sums)
    last_sums = part_pieces(tie(last_parts[0], out_q_sums, late[0]), small, last_came)
    last_pieces = [last_sums[0]] + [swap(last_sums[bit], "ctx", nc, bit) for bit in range(1, nc)]
    small = sum(piece[depth:, :].astype(F32) for piece in last_pieces).reshape(-1)
    norm_mine = small[: count * depth].reshape(count, depth)
    bias_sum = small[count * depth : held]
    grad_up, grad_down = final_sums(
        [[(l, l, col) for l in range(LAYERS)] for col in (0, hidden)],
        [shaped((LAYERS, depth, hidden), F32)] * 2,
        late,
    )
    summed = tuple(range(nc))
    qkv_plan = [((1, i), nc, (i + 1) * local) for i in range(3)]
    qkv_plan += [((0, 0), nc + 1, local), ((0, 1), summed, 0), ((0, 2), summed, local)]
    grad_out, grad_qkv = final_sums(
        [[(0, nc + 1, 0), (1, nc, 0)], qkv_plan],
        [shaped((LAYERS, depth, local), F32), shaped((LAYERS, 3, depth, local), F32)],
        [*last_pieces, above, out_q_pieces],
    )
    grad_qkv = grad_qkv.transpose(0, 2, 1, 3)

    norm_mine = (norm_mine + sibling(norm_mine)).reshape(LAYERS, 2, 8, depth)
    grad_gains = norm_mine[:, :, 0].transpose(0, 2, 1)
    grad_shifts = jnp.stack(
        [norm_mine[:, 0, 1], norm_mine[:, 1, 2], norm_mine[:, 1, 1], norm_mine[:, 1, 3]], axis=1
    ).transpose(0, 2, 1)
    queries, values = bias_sum[: LAYERS * local], bias_sum[LAYERS * local : 2 * LAYERS * local]
    grad_bias = jnp.stack([queries.reshape(LAYERS, local), values.reshape(LAYERS, local)], axis=1)
    grad_up_bias = bias_sum[2 * LAYERS * local :].reshape(LAYERS, hidden)

    return (
        block_output,
        grad_tokens,
        grad_qkv,
        grad_out,
        grad_up,
        grad_down,
        grad_bias,
        grad_up_bias,
        grad_gains,
        grad_shifts,
    )


def solution(mesh):
    placed = (
        P(("fsdp", "ctx"), None),
        P(("fsdp", "ctx"), None),
        P("fsdp", None),
        P("fsdp", None),
        P(None, ("fsdp", "ctx"), None, "tp"),
        P(None, ("fsdp", "ctx"), "tp"),
        P(None, ("fsdp", "ctx"), "tp"),
        P(None, ("fsdp", "ctx"), "tp"),
        P(None, None, "tp"),
        P(None, "tp"),
        P(None, ("fsdp", "ctx"), None),
        P(None, ("fsdp", "ctx"), None),
    )
    return jax.shard_map(
        partial(on_device, mesh.shape["fsdp"], mesh.shape["ctx"], mesh.shape["tp"]),
        mesh=mesh,
        in_specs=placed,
        out_specs=(
            P(("fsdp", "ctx"), None),
            P(("fsdp", "ctx"), None),
            P(None, ("fsdp", "ctx"), None, "tp"),
            P(None, ("fsdp", "ctx"), "tp"),
            P(None, ("fsdp", "ctx"), "tp"),
            P(None, ("fsdp", "ctx"), "tp"),
            P(None, None, "tp"),
            P(None, "tp"),
            P(None, ("fsdp", "ctx"), None),
            P(None, ("fsdp", "ctx"), None),
        ),
        check_vma=False,
    )
```

```python
from functools import partial

import jax
import jax.numpy as jnp
from jax import lax
from jax.experimental import pallas as pl
from jax.experimental.pallas import tpu as pltpu
from jax.sharding import PartitionSpec as P

HEADS = 16
HD = 64
BLK = 128
RUN_BLOCKS = 8
LAYERS = 2
NORM_ROWS = 8
NORM_EPS = 1e-05
MASKED = -1000000000.0
QB = 256
GELU_A = 0.7978845608028654
GELU_B = 0.044715
BF = jnp.bfloat16
F32 = jnp.float32
NN = ((1,), (0,))
NT = ((1,), (1,))
VMEM_LIMIT = 40 * 1024 * 1024


def dot(left, right, dims=NN):
    return lax.dot_general(left, right, (dims, ((), ())), preferred_element_type=F32)


def shaped(shape, dtype):
    return jax.ShapeDtypeStruct(shape, dtype)


def whole():
    return pl.BlockSpec(memory_space=pltpu.VMEM)


def params(flops, bytes_accessed, transcendentals=0):
    return dict(
        compiler_params=pltpu.CompilerParams(vmem_limit_bytes=VMEM_LIMIT),
        cost_estimate=pl.CostEstimate(
            flops=int(flops), bytes_accessed=int(bytes_accessed), transcendentals=int(transcendentals)
        ),
    )


def rows_of(order, refs, col, cols, depth, extra=0):
    pieces = []
    if all(ref.shape == refs[0].shape for ref in refs):
        held = refs[0].shape[0] // depth
        for number in range(order.shape[0]):
            start = pl.multiple_of(lax.rem(order[number], held) * depth, depth)
            pieces.append(refs[number // held][pl.ds(start, depth), col : col + cols])
        return jnp.concatenate(pieces, axis=0)
    for ref in refs:
        for start in range(0, ref.shape[0], depth + extra):
            pieces.append(ref[start : start + depth, col : col + cols])
    return jnp.concatenate(pieces, axis=0)


def call(kernel, out_shape, args, flops, scratch=(), transcendentals=0, smem=0):
    outs = out_shape if isinstance(out_shape, (list, tuple)) else [out_shape]
    moved = sum(a.size * a.dtype.itemsize for a in args) + sum(
        o.size * jnp.dtype(o.dtype).itemsize for o in outs
    )
    specs = [pl.BlockSpec(memory_space=pltpu.SMEM)] * smem + [whole()] * (len(args) - smem)
    return pl.pallas_call(
        kernel,
        in_specs=specs,
        out_specs=[whole()] * len(outs) if outs is out_shape else whole(),
        out_shape=out_shape,
        scratch_shapes=list(scratch),
        **params(flops, moved, transcendentals),
    )(*args)


def norm_stats(values):
    average = jnp.mean(values, axis=-1, keepdims=True)
    centred = values - average
    variance = jnp.mean(centred * centred, axis=-1, keepdims=True)
    scale = lax.rsqrt(variance + NORM_EPS)
    return centred * scale, scale


def gelu_parts(u):
    inner = GELU_A * (u + GELU_B * u * u * u)
    t = jnp.tanh(inner)
    return t


def add_norm_kernel(bias_row, gain_row, shift_row, x_ref, a_ref, b_ref, table_ref, y_ref, h_ref):
    branch = a_ref[...].astype(F32) + b_ref[...].astype(F32) + table_ref[bias_row : bias_row + 1, :]
    y = x_ref[...].astype(F32) + branch
    y_ref[...] = y
    n, _ = norm_stats(y)
    h_ref[...] = (
        n * table_ref[gain_row : gain_row + 1, :] + table_ref[shift_row : shift_row + 1, :]
    ).astype(BF)


def add_norm(x, a, b, table, bias_row, gain_row, shift_row):
    rows, width = x.shape
    return call(
        partial(add_norm_kernel, bias_row, gain_row, shift_row),
        [shaped((rows, width), F32), shaped((rows, width), BF)],
        [x, a, b, table],
        rows * width * 12,
    )


def heads_out(out_ref, total, number, row):
    half = total.shape[0]
    turned = total.astype(BF).T
    for j in range(out_ref.shape[0]):
        out_ref[j, row : row + HD, number * half : (number + 1) * half] = turned[j * HD : (j + 1) * HD, :]


def qkv_rows(order, h_refs, bias_ref, w_refs, out_ref, col, depth, extra):
    local = out_ref.shape[0] * HD
    h = jnp.concatenate([h_ref[...] for h_ref in h_refs], axis=0)
    for i in range(3):
        weights = rows_of(order, w_refs, col + i * local, local, depth, extra)
        heads_out(out_ref, dot(h, weights) + bias_ref[i : i + 1, :], 0, i * HD)


def qkv_kernel(col, depth, order, h_own, h_oth, bias_ref, *refs):
    qkv_rows(order, [h_own, h_oth], bias_ref, refs[:-1], refs[-1], col, depth, 0)


def qkv_project(order, h_own, h_oth, bias, pack, col, depth):
    half, width = h_own.shape
    local = bias.shape[1]
    return call(
        partial(qkv_kernel, col, depth),
        shaped((local // HD, 3 * HD, 2 * half), BF),
        [order, h_own, h_oth, bias, *pack],
        12 * half * width * local,
        smem=1,
    )


def first_qkv_kernel(row, depth, extra, order, n_own, n_oth, table_ref, bias_ref, *refs):
    w_refs, (h_own, h_oth, out_ref) = refs[:-3], refs[-3:]
    for n_ref, h_ref in ((n_own, h_own), (n_oth, h_oth)):
        h_ref[...] = (n_ref[...] * table_ref[row : row + 1, :] + table_ref[row + 2 : row + 3, :]).astype(BF)
    qkv_rows(order, [h_own, h_oth], bias_ref, w_refs, out_ref, 0, depth, extra)


def first_qkv(order, n_own, n_oth, table, row, bias, pack, depth, extra):
    half, width = n_own.shape
    local = bias.shape[1]
    return call(
        partial(first_qkv_kernel, row, depth, extra),
        [
            shaped((half, width), BF),
            shaped((half, width), BF),
            shaped((local // HD, 3 * HD, 2 * half), BF),
        ],
        [order, n_own, n_oth, table, bias, *pack],
        12 * half * width * local,
        smem=1,
    )


def out_kernel(col, depth, start, order, o_ref, *refs):
    w_refs, out_ref = refs[:-1], refs[-1]
    half = out_ref.shape[0]
    heads = o_ref.shape[0]
    o = jnp.concatenate([o_ref[j, :, start : start + half] for j in range(heads)], axis=0).T
    weights = rows_of(order, w_refs, col, heads * HD, depth)
    out_ref[...] = dot(o, weights, NT).astype(out_ref.dtype)


def out_project(order, o_rows, pack, col, depth, width, start, dtype):
    heads, _, rows = o_rows.shape
    half = rows // 2
    return call(
        partial(out_kernel, col, depth, start),
        shaped((half, width), dtype),
        [order, o_rows, *pack],
        2 * half * width * heads * HD,
        smem=1,
    )


def mlp_kernel(counts, up_col, down_col, depth, order, h_own, h_oth, bias_ref, *refs):
    ups, downs = refs[: counts[0]], refs[counts[0] : counts[0] + counts[1]]
    u_ref, oth_ref, own_ref = refs[counts[0] + counts[1] :]
    half = h_own.shape[0]
    hidden = u_ref.shape[1]
    h = jnp.concatenate([h_own[...], h_oth[...]], axis=0)
    u = dot(h, rows_of(order, ups, up_col, hidden, depth)) + bias_ref[...]
    u_ref[...] = u
    act = (0.5 * u * (1.0 + gelu_parts(u))).astype(BF)
    total = dot(act, rows_of(order, downs, down_col, hidden, depth), NT)
    own_ref[...] = total[:half, :]
    oth_ref[...] = total[half:, :].astype(BF)


def mlp_forward(order, h_own, h_oth, bias, up, down, depth):
    half, width = h_own.shape
    hidden = bias.shape[1]
    return call(
        partial(mlp_kernel, (len(up[0]), len(down[0])), up[1], down[1], depth),
        [
            shaped((2 * half, hidden), F32),
            shaped((half, width), BF),
            shaped((half, width), F32),
        ],
        [order, h_own, h_oth, bias, *up[0], *down[0]],
        8 * half * width * hidden,
        transcendentals=2 * half * hidden,
        smem=1,
    )


def mlp_back_kernel(counts, up_col, down_col, depth, order, g_own, g_oth, u_ref, *refs):
    ups, downs = refs[: counts[0]], refs[counts[0] : counts[0] + counts[1]]
    act_ref, gu_ref, sum_ref, oth_ref, own_ref = refs[counts[0] + counts[1] :]
    half = g_own.shape[0]
    hidden = u_ref.shape[1]
    g = jnp.concatenate([g_own[...], g_oth[...]], axis=0)
    grad = dot(g, rows_of(order, downs, down_col, hidden, depth))
    u = u_ref[...]
    t = gelu_parts(u)
    act_ref[...] = (0.5 * u * (1.0 + t)).astype(BF)
    slope = 0.5 * (1.0 + t) + 0.5 * u * (1.0 - t * t) * (GELU_A * (1.0 + 3.0 * GELU_B * u * u))
    gu = (grad * slope).astype(BF)
    gu_ref[...] = gu
    sum_ref[...] = jnp.sum(gu.astype(F32), axis=0, keepdims=True)
    total = dot(gu, rows_of(order, ups, up_col, hidden, depth), NT)
    own_ref[...] = total[:half, :]
    oth_ref[...] = total[half:, :].astype(BF)


def mlp_backward(order, g_own, g_oth, u, up, down, depth):
    half, width = g_own.shape
    hidden = u.shape[1]
    return call(
        partial(mlp_back_kernel, (len(up[0]), len(down[0])), up[1], down[1], depth),
        [
            shaped((2 * half, hidden), BF),
            shaped((2 * half, hidden), BF),
            shaped((1, hidden), F32),
            shaped((half, width), BF),
            shaped((half, width), F32),
        ],
        [order, g_own, g_oth, u, *up[0], *down[0]],
        8 * half * width * hidden,
        transcendentals=2 * half * hidden,
        smem=1,
    )


def grads_out(order, out_refs, total, col):
    cols = slice(col, col + total.shape[1])
    if len(out_refs) == 1:
        depth = total.shape[0] // order.shape[0]
        for number in range(order.shape[0]):
            start = pl.multiple_of(order[number] * depth, depth)
            out_refs[0][pl.ds(start, depth), cols] = total[number * depth : (number + 1) * depth].astype(BF)
        return
    span = out_refs[0].shape[0]
    for y, out_ref in enumerate(out_refs):
        out_ref[:, cols] = total[y * span : (y + 1) * span].astype(BF)


def late_grad_kernel(count, order, *refs):
    g_own, g_oth, h_own, h_oth, act_ref, gu_ref = refs[:6]
    out_refs = refs[count:]
    hidden = act_ref.shape[1]
    h = jnp.concatenate([h_own[...], h_oth[...]], axis=0).T
    grads_out(order, out_refs, dot(h, gu_ref[...]), 0)
    g = jnp.concatenate([g_own[...], g_oth[...]], axis=0).T
    grads_out(order, out_refs, dot(g, act_ref[...]), hidden)
    if count > 6:
        attention_grad_body(0, 4, 2 * hidden, order, *refs[6:count], out_refs)


def late_grad(order, mlp, attention):
    half, width = mlp[0].shape
    cols = 2 * mlp[4].shape[1]
    if attention:
        cols += 4 * attention[2].shape[0] * HD
    args = [*mlp, *attention]
    return call(
        partial(late_grad_kernel, len(args)),
        [shaped((width, cols), BF)],
        [order, *args],
        4 * half * width * cols,
        smem=1,
    )[0]


def attention_grad_body(first, last, col, order, g_own, g_oth, o_ref, h_own, h_oth, p_ref, out_refs):
    heads = o_ref.shape[0]
    local = heads * HD
    if first == 0:
        g = jnp.concatenate([g_own[...], g_oth[...]], axis=0).T
        o = jnp.concatenate([o_ref[j] for j in range(heads)], axis=0)
        grads_out(order, out_refs, dot(g, o, NT), col)
        col += local
        first = 1
    h = jnp.concatenate([h_own[...], h_oth[...]], axis=0).T
    grads_out(order, out_refs, dot(h, p_ref[:, (first - 1) * local : (last - 1) * local]), col)


def attention_grad_kernel(first, last, order, *refs):
    attention_grad_body(first, last, 0, order, *refs[:6], refs[6:])


def attention_grad(first, last, order, g_own, g_oth, o_rows, h_own, h_oth, g_proj, nf):
    half, width = g_own.shape
    local = o_rows.shape[0] * HD
    cols = (last - first) * local
    return call(
        partial(attention_grad_kernel, first, last),
        [shaped((width // nf, cols), BF)] * nf,
        [order, g_own, g_oth, o_rows, h_own, h_oth, g_proj],
        4 * half * width * cols,
        smem=1,
    )


def part_sum_kernel(order, own_ref, small_ref, *refs):
    came, out_ref = refs[:-1], refs[-1]
    slots = out_ref.shape[0]
    depth = own_ref.shape[0] // slots
    for number in range(slots):
        rows = slice(number * depth, (number + 1) * depth)
        total = own_ref[rows, :].astype(F32)
        for ref in came:
            total = total + ref[rows, :].astype(F32)
        slot = lax.rem(order[number], slots)
        out_ref[slot, :depth, :] = total.astype(BF)
        out_ref[slot, depth:, :] = small_ref[number].astype(BF)


def part_sum(order, own, small, came):
    rows, cols = own.shape
    slots, extra, _ = small.shape
    return call(
        part_sum_kernel,
        shaped((slots, rows // slots + extra, cols), BF),
        [order, own, small, *came],
        rows * cols * 2,
        smem=1,
    )


def part_pieces_kernel(own_ref, small_ref, *refs):
    slots, extra, _ = small_ref.shape
    came, outs = refs[:-slots], refs[-slots:]
    depth = own_ref.shape[0] // slots
    for number, out_ref in enumerate(outs):
        rows = slice(number * depth, (number + 1) * depth)
        total = own_ref[rows, :].astype(F32)
        for ref in came:
            total = total + ref[rows, :].astype(F32)
        out_ref[:depth, :] = total.astype(BF)
        out_ref[depth:, :] = small_ref[number].astype(BF)


def part_pieces(own, small, came):
    rows, cols = own.shape
    slots, extra, _ = small.shape
    return call(
        part_pieces_kernel,
        [shaped((rows // slots + extra, cols), BF)] * slots,
        [own, small, *came],
        rows * cols * 2,
    )


def final_kernel(plans, *refs):
    outs = refs[-len(plans) :]
    for out_ref, plan in zip(outs, plans):
        cols = out_ref.shape[-1]
        for index, which, col in plan:
            if isinstance(which, tuple):
                rows = slice(0, out_ref.shape[-2])
                total = refs[which[0]][rows, col : col + cols].astype(F32)
                for other in which[1:]:
                    total = total + refs[other][rows, col : col + cols].astype(F32)
                out_ref[index] = total
                continue
            ref = refs[which]
            if len(ref.shape) == 2:
                out_ref[index] = ref[: out_ref.shape[-2], col : col + cols].astype(F32)
                continue
            rows = slice(0, out_ref.shape[-2])
            total = ref[0, rows, col : col + cols].astype(F32)
            for slot in range(1, ref.shape[0]):
                total = total + ref[slot, rows, col : col + cols].astype(F32)
            out_ref[index] = total


def final_sums(plans, shapes, pieces):
    return call(partial(final_kernel, plans), shapes, pieces, sum(p.size for p in pieces))


def norm_back_kernel(gain_row, gx_ref, a_ref, b_ref, y_ref, table_ref, gy_ref, low_ref, sums_ref):
    grad = a_ref[...].astype(F32) + b_ref[...].astype(F32)
    n, scale = norm_stats(y_ref[...].astype(F32))
    e = grad * table_ref[gain_row : gain_row + 1, :]
    mean_e = jnp.mean(e, axis=-1, keepdims=True)
    mean_en = jnp.mean(e * n, axis=-1, keepdims=True)
    gx = gx_ref[...].astype(F32)
    gy = gx + scale * (e - mean_e - n * mean_en)
    gy_ref[...] = gy
    low = gy.astype(BF)
    low_ref[...] = low
    sums_ref[0:1, :] = jnp.sum(grad * n, axis=0, keepdims=True)
    sums_ref[1:2, :] = jnp.sum(grad, axis=0, keepdims=True)
    sums_ref[2:3, :] = jnp.sum(low.astype(F32), axis=0, keepdims=True)
    sums_ref[3:4, :] = jnp.sum(gx.astype(BF).astype(F32), axis=0, keepdims=True)
    sums_ref[4:, :] = jnp.zeros((4, gx.shape[1]), F32)


def norm_backward(gx, a, b, y, table, gain_row):
    rows, width = gx.shape
    return call(
        partial(norm_back_kernel, gain_row),
        [shaped((rows, width), F32), shaped((rows, width), BF), shaped((8, width), F32)],
        [gx, a, b, y, table],
        rows * width * 25,
    )


def out_back_kernel(col, depth, order, g_own, g_oth, *refs):
    w_refs, out_ref = refs[:-1], refs[-1]
    g = jnp.concatenate([g_own[...], g_oth[...]], axis=0)
    heads_out(out_ref, dot(g, rows_of(order, w_refs, col, out_ref.shape[0] * HD, depth)), 0, 0)


def out_backward(order, g_own, g_oth, pack, col, depth, local):
    half, width = g_own.shape
    return call(
        partial(out_back_kernel, col, depth),
        shaped((local // HD, HD, 2 * half), BF),
        [order, g_own, g_oth, *pack],
        4 * half * width * local,
        smem=1,
    )


def qkv_back_kernel(col, depth, extra, order, g_ref, *refs):
    w_refs, (rows_ref, sum_ref, oth_ref, own_ref) = refs[:-4], refs[-4:]
    heads = g_ref.shape[0]
    half = own_ref.shape[0]
    local = heads * HD
    planes = [
        jnp.concatenate([g_ref[j, i * HD : (i + 1) * HD, :] for j in range(heads)], axis=0).T
        for i in range(3)
    ]
    grads = jnp.concatenate(planes, axis=1)
    rows_ref[...] = grads
    total = dot(grads, rows_of(order, w_refs, col, 3 * local, depth, extra), NT)
    oth_ref[...] = total[half:].astype(BF)
    own_ref[...] = total[:half]
    sum_ref[...] = jnp.sum(grads.astype(F32), axis=0, keepdims=True)


def qkv_backward(order, g, pack, col, depth, extra, width):
    heads, _, rows = g.shape
    half = rows // 2
    cols = 3 * heads * HD
    return call(
        partial(qkv_back_kernel, col, depth, extra),
        [
            shaped((rows, cols), BF),
            shaped((1, cols), F32),
            shaped((half, width), BF),
            shaped((half, width), F32),
        ],
        [order, g, *pack],
        2 * rows * width * cols,
        smem=1,
    )


def gather_blocks(source_ref, src_ref, dest_ref, per_device):
    for s in range(dest_ref.shape[1] // BLK):
        src = src_ref[s]
        z = src // per_device
        start = pl.multiple_of((src - z * per_device) * BLK, BLK)
        dest_ref[:, s * BLK : (s + 1) * BLK] = source_ref[z, :, pl.ds(start, BLK)]


def scatter_blocks(dest_ref, src_ref, source, per_device, low, first):
    depth, columns = source.shape
    for s in range(columns // BLK):
        src = src_ref[first + s]
        z = src // per_device
        start = pl.multiple_of((src - z * per_device) * BLK, BLK)
        dest_ref[z, low : low + depth, pl.ds(start, BLK)] = source[:, s * BLK : (s + 1) * BLK]


def segment_columns(seg_ref, column_ref):
    for s in range(seg_ref.shape[1] // BLK):
        row = seg_ref[:, s * BLK : (s + 1) * BLK]
        row = jnp.where(row < 0, -2, row).astype(F32)
        column_ref[s * BLK : (s + 1) * BLK, :] = jnp.broadcast_to(row, (BLK, BLK)).T


def score_tile(keys, queries, column_ref, seg_ref, slope, base, first, last):
    depth = keys.shape[0]
    width = last - first
    scores = dot(keys, queries)
    key_row = lax.broadcasted_iota(jnp.int32, (depth, width), 0)
    query_row = lax.broadcasted_iota(jnp.int32, (depth, width), 1) + (first - base)
    distance = query_row - key_row
    scores = scores - slope * distance.astype(F32)
    columns = column_ref[base : base + depth, :]
    key_seg = jnp.concatenate([columns] * (width // BLK), axis=1)
    query_seg = seg_ref[:, first:last].astype(F32)
    allowed = ((key_seg == query_seg) & (distance >= 0)) | (distance == 0)
    return scores, allowed


def attend_kernel(per_device, src_ref, slope_ref, seg_ref, qkv_ref, o_ref, lse_ref, stream_ref, column_ref):
    gather_blocks(qkv_ref, src_ref, stream_ref, per_device)
    segment_columns(seg_ref, column_ref)
    slope = slope_ref[0]
    run = RUN_BLOCKS * BLK
    for base in range(0, stream_ref.shape[1], run):
        keys = stream_ref[HD : 2 * HD, base : base + run].T
        for first in range(base, base + run, QB):
            last = first + QB
            depth = last - base
            queries = stream_ref[:HD, first:last] * jnp.asarray(HD**-0.5, BF)
            scores, allowed = score_tile(
                keys[:depth], queries, column_ref, seg_ref, slope, base, first, last
            )
            scores = jnp.where(allowed, scores, MASKED)
            top = jnp.max(scores, axis=0, keepdims=True)
            weights = jnp.exp(scores - top)
            total = jnp.sum(weights, axis=0, keepdims=True)
            lse_ref[:, first:last] = top + jnp.log(total)
            values = stream_ref[2 * HD :, base : base + depth]
            out = (dot(values, weights.astype(BF)) / total).astype(BF)
            scatter_blocks(o_ref, src_ref, out, per_device, 0, first // BLK)


def attend(qkv, source, slope, segments):
    nc, depth, rows = qkv.shape
    length = nc * rows
    smem = pl.BlockSpec(memory_space=pltpu.SMEM)
    return pl.pallas_call(
        partial(attend_kernel, rows // BLK),
        in_specs=[smem, smem, whole(), whole()],
        out_specs=[whole(), whole()],
        out_shape=[shaped((nc, HD, rows), BF), shaped((1, length), F32)],
        scratch_shapes=[pltpu.VMEM((3 * HD, length), BF), pltpu.VMEM((length, BLK), F32)],
        **params(length * RUN_BLOCKS * BLK * HD * 3, length * HD * 8, length * RUN_BLOCKS * BLK // 2),
    )(source, slope, segments, qkv)


def attend_back_kernel(
    per_device, src_ref, slope_ref, seg_ref, qkv_ref, g_ref, lse_ref, out_ref, stream_ref, grad_ref, column_ref, k_acc, v_acc
):
    gather_blocks(qkv_ref, src_ref, stream_ref, per_device)
    gather_blocks(g_ref, src_ref, grad_ref, per_device)
    segment_columns(seg_ref, column_ref)
    slope = slope_ref[0]
    run = RUN_BLOCKS * BLK
    scale = HD**-0.5
    for base in range(0, stream_ref.shape[1], run):
        rows = slice(base, base + run)
        keys_turned = stream_ref[HD : 2 * HD, rows]
        keys = keys_turned.T
        values = stream_ref[2 * HD :, rows].T
        queries_rows = stream_ref[:HD, rows].T
        grads_rows = grad_ref[:, rows].T
        for first in range(base + run - QB, base - 1, -QB):
            last = first + QB
            depth = last - base
            inner = slice(first - base, last - base)
            queries = stream_ref[:HD, first:last] * jnp.asarray(scale, BF)
            scores, allowed = score_tile(
                keys[:depth], queries, column_ref, seg_ref, slope, base, first, last
            )
            weights = jnp.where(allowed, jnp.exp(scores - lse_ref[:, first:last]), 0.0)
            back = dot(values[:depth], grad_ref[:, first:last])
            delta = jnp.sum(weights * back, axis=0, keepdims=True)
            low = (weights * (back - delta)).astype(BF)
            v_piece = dot(weights.astype(BF), grads_rows[inner])
            k_piece = dot(low, queries_rows[inner])
            if depth == run:
                v_acc[...] = v_piece
                k_acc[...] = k_piece
            else:
                v_acc[:depth, :] += v_piece
                k_acc[:depth, :] += k_piece
            q_grad = (dot(keys_turned[:, :depth], low) * scale).astype(BF)
            scatter_blocks(out_ref, src_ref, q_grad, per_device, 0, first // BLK)
        scatter_blocks(out_ref, src_ref, (k_acc[...] * scale).T.astype(BF), per_device, HD, base // BLK)
        scatter_blocks(out_ref, src_ref, v_acc[...].T.astype(BF), per_device, 2 * HD, base // BLK)


def attend_backward(qkv, grads, lse, source, slope, segments):
    nc, depth, rows = qkv.shape
    length = nc * rows
    run = RUN_BLOCKS * BLK
    smem = pl.BlockSpec(memory_space=pltpu.SMEM)
    return pl.pallas_call(
        partial(attend_back_kernel, rows // BLK),
        in_specs=[smem, smem, whole(), whole(), whole(), whole()],
        out_specs=whole(),
        out_shape=shaped((nc, depth, rows), BF),
        scratch_shapes=[
            pltpu.VMEM((3 * HD, length), BF),
            pltpu.VMEM((HD, length), BF),
            pltpu.VMEM((length, BLK), F32),
            pltpu.VMEM((run, HD), F32),
            pltpu.VMEM((run, HD), F32),
        ],
        **params(length * run * HD * 7, length * HD * 16, length * run // 2),
    )(source, slope, segments, qkv, grads, lse)


def to_relative_kernel(place_ref, value_ref, own_ref, oth_ref):
    half = own_ref.shape[0]
    for ref, side in ((own_ref, place_ref[0]), (oth_ref, 1 - place_ref[0])):
        rows = pl.ds(pl.multiple_of(side * half, half), half)
        for number in range(place_ref.shape[0] - 1):
            depth = value_ref.shape[1] // (place_ref.shape[0] - 1)
            start = pl.multiple_of(place_ref[number + 1] * depth, depth)
            ref[:, number * depth : (number + 1) * depth] = value_ref[rows, pl.ds(start, depth)]


def from_relative_kernel(place_ref, own_ref, oth_ref, value_ref):
    half = own_ref.shape[0]
    for ref, side in ((own_ref, place_ref[0]), (oth_ref, 1 - place_ref[0])):
        rows = pl.ds(pl.multiple_of(side * half, half), half)
        for number in range(place_ref.shape[0] - 1):
            depth = value_ref.shape[1] // (place_ref.shape[0] - 1)
            start = pl.multiple_of(place_ref[number + 1] * depth, depth)
            value_ref[rows, pl.ds(start, depth)] = ref[:, number * depth : (number + 1) * depth].astype(
                value_ref.dtype
            )


def on_device(
    nf,
    nc,
    nt,
    tokens,
    cotangent,
    block_place,
    segment_ids,
    qkv_weight,
    out_weight,
    up_weight,
    down_weight,
    query_value_bias,
    up_bias,
    norm_gains,
    row_biases,
):
    rows, width = tokens.shape
    half = rows // 2
    depth = qkv_weight.shape[1]
    local = qkv_weight.shape[3]
    heads = local // HD
    hidden = up_weight.shape[2]
    span = nc * depth
    y_index = lax.axis_index("fsdp")
    z_index = lax.axis_index("ctx")
    t_index = lax.axis_index("tp")
    side = t_index % 2

    def swap(value, axis, size, bit):
        return lax.ppermute(value, axis, [(i, i ^ bit) for i in range(size)])

    def sibling(value):
        return swap(value, "tp", nt, 1)

    def across(value):
        return lax.all_to_all(value, "ctx", 0, 0)

    def tie(value, *others):
        return lax.optimization_barrier((value, *others))[0]

    def gather_z(shard, doubling=False):
        if not doubling:
            return [swap(shard, "ctx", nc, bit) for bit in range(1, nc)]
        came, bit = [], 1
        while bit < nc:
            came.append(swap(jnp.concatenate([shard, *came], axis=0) if came else shard, "ctx", nc, bit))
            bit *= 2
        return came

    def gather_y(shard, came, apart=False):
        pack = [shard, *came]
        for bit in range(1, nf):
            if apart:
                own = swap(shard, "fsdp", nf, bit)
                pack.append(own)
                pack.append(swap(tie(jnp.concatenate(came, axis=0), own), "fsdp", nf, bit))
            else:
                pack.append(swap(jnp.concatenate([shard, *came], axis=0), "fsdp", nf, bit))
        return pack

    def whole_gather(shard):
        return lax.all_gather(shard, ("fsdp", "ctx"), axis=0, tiled=True)

    def whole_scatter(total):
        return lax.psum_scatter(total, ("fsdp", "ctx"), scatter_dimension=0, tiled=True)

    def send_y(parts):
        return [swap(parts[bit], "fsdp", nf, bit) for bit in range(1, nf)]

    def tensor_sum(other, own):
        term = (own + sibling(other).astype(F32)).astype(BF)
        bit = 2
        while bit * 2 < nt:
            term = (term.astype(F32) + swap(term, "tp", nt, bit).astype(F32)).astype(BF)
            bit *= 2
        return term, swap(term, "tp", nt, bit)

    order = jnp.stack(
        [(y_index ^ a) * nc + (z_index ^ b) for a in range(nf) for b in range(nc)]
    ).astype(jnp.int32)
    place = jnp.concatenate([side.reshape(1).astype(jnp.int32), order])

    def columns_moved(value):
        return jnp.concatenate(
            [
                lax.dynamic_slice_in_dim(value, order[number] * depth, depth, axis=1)
                for number in range(nf * nc)
            ],
            axis=1,
        )

    def to_relative(value):
        if depth % 128 == 0:
            return call(
                to_relative_kernel,
                [shaped((half, width), value.dtype)] * 2,
                [place, value],
                value.size,
                smem=1,
            )
        moved = columns_moved(value)
        return [lax.dynamic_slice_in_dim(moved, which * half, half) for which in (side, 1 - side)]

    def from_relative(own, oth):
        if depth % 128 == 0:
            return call(
                from_relative_kernel, shaped((rows, width), own.dtype), [place, own, oth], 2 * own.size, smem=1
            )
        return columns_moved(
            jnp.where(side == 0, jnp.concatenate([own, oth], axis=0), jnp.concatenate([oth, own], axis=0))
        )

    per_device = rows // BLK
    count = nc * per_device
    stored_place = block_place[0]
    stored = jnp.arange(count, dtype=jnp.int32)
    relative = (stored // per_device) * per_device + (stored % per_device + side * (per_device // 2)) % per_device
    source = jnp.sum(
        jnp.where(stored_place[None, :] == jnp.arange(count, dtype=jnp.int32)[:, None], relative[None, :], 0), axis=1
    ).astype(jnp.int32)
    head = (t_index * heads + z_index).astype(F32)
    slope = jnp.exp2(-8.0 * (head + 1.0) / HEADS).reshape(1)
    segments = segment_ids

    def qkv_shard(layer):
        return [qkv_weight[layer, :, i, :] for i in range(3)]

    table_rows = []
    for layer in range(LAYERS):
        table_rows += [norm_gains[layer].T, row_biases[layer].T, jnp.zeros((2, depth), BF)]
    table_shard = jnp.concatenate(table_rows, axis=0)
    extra = table_shard.shape[0]
    table_padded = jnp.pad(table_shard, ((0, 0), (0, 3 * local - depth)))
    first_shard = jnp.concatenate([jnp.concatenate(qkv_shard(0), axis=1), table_padded], axis=0)
    first_z = gather_z(first_shard)
    first_pack = gather_y(first_shard, first_z, apart=True)
    table = jnp.concatenate(
        [
            ref[start + depth : start + depth + extra, :depth]
            for ref in first_pack
            for start in range(0, ref.shape[0], depth + extra)
        ],
        axis=1,
    ).astype(F32)

    biases = [
        jnp.stack([query_value_bias[l, 0], jnp.zeros((local,), BF), query_value_bias[l, 1]]).astype(F32)
        for l in range(LAYERS)
    ]
    up_biases = [up_bias[l].astype(F32).reshape(1, hidden) for l in range(LAYERS)]

    x_half, x_oth = to_relative(tokens)
    n_own = norm_stats(x_half.astype(F32))[0]
    n_oth = norm_stats(x_oth.astype(F32))[0]
    h_own, h_oth, qkv_sent = first_qkv(order, n_own, n_oth, table, 0, biases[0], first_pack, depth, extra)

    out_up_shard = tie(jnp.concatenate([out_weight[0], up_weight[0]], axis=1), *first_z)
    out_up_z = gather_z(out_up_shard)
    out_up = gather_y(out_up_shard, out_up_z)
    out_packs, qkv_packs, up_packs = [(out_up, 0)], [(first_pack, 0, extra)], [(out_up, local)]
    next_out_qkv = whole_gather(
        tie(jnp.concatenate([out_weight[1], *qkv_shard(1)], axis=1), *first_z)
    )
    down_shard = tie(down_weight[0], *out_up_z)
    down_z = gather_z(down_shard, True)
    down_packs = [(gather_y(down_shard, down_z), 0)]
    out_packs.append(([next_out_qkv], 0))
    qkv_packs.append(([next_out_qkv], local, 0))

    records = []
    last_other = last_own = None
    for l in range(LAYERS):
        row = l * NORM_ROWS
        qkv = across(qkv_sent)
        if l == 0:
            next_mlp = whole_gather(
                tie(jnp.concatenate([up_weight[1], down_weight[1]], axis=1), next_out_qkv)
            )
            up_packs.append(([next_mlp], 0))
            down_packs.append(([next_mlp], hidden))
        o_stream, lse = attend(qkv, source, slope, segments)
        o_rows = across(o_stream)
        if l == 0:
            o_rows = tie(o_rows, *down_z)
        other = out_project(order, o_rows, *out_packs[l], depth, width, half, BF)
        own = out_project(order, tie(o_rows, other), *out_packs[l], depth, width, 0, F32)
        a, b = tensor_sum(other, own)
        y_half, h2_own = add_norm(x_half, a, b, table, row + 3, row + 1, row + 4)
        h2_oth = sibling(h2_own)
        u, other, own = mlp_forward(order, h2_own, h2_oth, up_biases[l], up_packs[l], down_packs[l], depth)
        records.append((x_half, h_own, h_oth, qkv, lse, o_rows, y_half, h2_own, h2_oth, u))
        if l + 1 < LAYERS:
            a, b = tensor_sum(other, own)
            following = row + NORM_ROWS
            x_half, h_own = add_norm(y_half, a, b, table, row + 5, following, following + 2)
            h_oth = sibling(h_own)
            qkv_sent = qkv_project(order, h_own, h_oth, biases[l + 1], *qkv_packs[l + 1][:2], depth)
        else:
            last_other, last_own = other, own

    gz_own, gz_oth = to_relative(cotangent)
    gx_half = gz_own.astype(F32)
    sums = [None] * LAYERS
    late = [None] * LAYERS
    for l in reversed(range(LAYERS)):
        row = l * NORM_ROWS
        x_half, h_own, h_oth, qkv, lse, o_rows, y_half, h2_own, h2_oth, u = records[l]
        act, gu, up_sum, other, own = mlp_backward(order, gz_own, gz_oth, u, up_packs[l], down_packs[l], depth)
        a, b = tensor_sum(other, own)
        total = late_grad(order, (gz_own, gz_oth, h2_own, h2_oth, tie(act, a), gu), ())
        b = tie(b, total)
        late[l] = whole_scatter(tie(total, *late[l + 1 :]))
        gy_half, ga_own, sums_two = norm_backward(gx_half, a, b, y_half, table, row + 1)
        ga_oth = sibling(ga_own)
        g_stream = across(out_backward(order, ga_own, ga_oth, *out_packs[l], depth, local))
        if l == LAYERS - 1:
            a, b = tensor_sum(tie(last_other, g_stream), last_own)
            final_half = y_half + (a.astype(F32) + b.astype(F32) + table[row + 5])
            final_low = final_half.astype(BF)
            block_output = from_relative(final_low, sibling(final_low))
        if l < LAYERS - 1:
            g_stream = tie(g_stream, *above_came)
        g_sent = attend_backward(qkv, g_stream, lse, source, slope, segments)
        g_rows = across(g_sent)
        if l < LAYERS - 1:
            above_sums = part_sum(
                order, tie(above[0], g_sent), jnp.zeros((nc, 16, 4 * local), F32), above_came
            )
            g_rows = tie(g_rows, above_sums)
        g_proj, qkv_sum, other, own = qkv_backward(
            order, g_rows, qkv_packs[l][0], qkv_packs[l][1], depth, qkv_packs[l][2], width
        )
        a, b = tensor_sum(other, own)
        sources = (order, ga_own, ga_oth, o_rows, h_own, h_oth)
        if l > 0:
            above = attention_grad(0, 4, *sources, tie(g_proj, a), nf)
            above_came = send_y(above)
            b = tie(b, *above)
        else:
            out_q = attention_grad(0, 2, *sources, tie(g_proj, a), nf)
            out_q_came = send_y(out_q)
            last_parts = attention_grad(2, 4, *sources, tie(g_proj, *out_q), nf)
            last_came = send_y(last_parts)
            above = across(tie(above_sums, *last_parts))
            b = tie(b, *last_parts)
        gx_half, gz_own, sums_one = norm_backward(gy_half, a, b, x_half, table, row)
        if l > 0:
            gz_oth = sibling(gz_own)
        sums[l] = (sums_one, sums_two, qkv_sum, up_sum)
    grad_tokens = from_relative(gx_half, sibling(gx_half))

    norm_all = jnp.concatenate([sums[l][which] for l in range(LAYERS) for which in (0, 1)], axis=0)
    bias_all = jnp.concatenate(
        [sums[l][2][:, :local] for l in range(LAYERS)]
        + [sums[l][2][:, 2 * local :] for l in range(LAYERS)]
        + [sums[l][3] for l in range(LAYERS)],
        axis=1,
    ).reshape(-1, depth)
    count = norm_all.shape[0]
    norm_total = norm_all[:, :span]
    bias_total = bias_all
    for bit in range(1, nf):
        sent = jnp.concatenate(
            [norm_all[:, bit * span + b * depth : bit * span + (b + 1) * depth] for b in range(nc)] + [bias_all],
            axis=0,
        )
        came = swap(sent, "fsdp", nf, bit)
        norm_total = norm_total + jnp.concatenate(
            [came[b * count : (b + 1) * count] for b in range(nc)], axis=1
        )
        bias_total = bias_total + came[nc * count :]
    cols = last_parts[0].shape[1]
    held = count * depth + bias_total.size
    extra_rows = -(-held // (16 * cols)) * 16
    small = jnp.concatenate(
        [
            norm_total.reshape(count, nc, depth).transpose(1, 0, 2).reshape(nc, -1),
            jnp.broadcast_to(bias_total.reshape(1, -1), (nc, bias_total.size)),
            jnp.zeros((nc, extra_rows * cols - held), F32),
        ],
        axis=1,
    ).reshape(nc, extra_rows, cols)
    nothing = jnp.zeros((nc, 16, cols), F32)
    out_q_sums = part_sum(order, tie(out_q[0], above), nothing, out_q_came)
    out_q_pieces = across(out_q_sums)
    last_sums = part_pieces(tie(last_parts[0], out_q_sums, late[0]), small, last_came)
    last_pieces = [last_sums[0]] + [swap(last_sums[bit], "ctx", nc, bit) for bit in range(1, nc)]
    small = sum(piece[depth:, :].astype(F32) for piece in last_pieces).reshape(-1)
    norm_mine = small[: count * depth].reshape(count, depth)
    bias_sum = small[count * depth : held]
    grad_up, grad_down = final_sums(
        [[(l, l, col) for l in range(LAYERS)] for col in (0, hidden)],
        [shaped((LAYERS, depth, hidden), F32)] * 2,
        late,
    )
    summed = tuple(range(nc))
    qkv_plan = [((1, i), nc, (i + 1) * local) for i in range(3)]
    qkv_plan += [((0, 0), nc + 1, local), ((0, 1), summed, 0), ((0, 2), summed, local)]
    grad_out, grad_qkv = final_sums(
        [[(0, nc + 1, 0), (1, nc, 0)], qkv_plan],
        [shaped((LAYERS, depth, local), F32), shaped((LAYERS, 3, depth, local), F32)],
        [*last_pieces, above, out_q_pieces],
    )
    grad_qkv = grad_qkv.transpose(0, 2, 1, 3)

    norm_mine = (norm_mine + sibling(norm_mine)).reshape(LAYERS, 2, 8, depth)
    grad_gains = norm_mine[:, :, 0].transpose(0, 2, 1)
    grad_shifts = jnp.stack(
        [norm_mine[:, 0, 1], norm_mine[:, 1, 2], norm_mine[:, 1, 1], norm_mine[:, 1, 3]], axis=1
    ).transpose(0, 2, 1)
    queries, values = bias_sum[: LAYERS * local], bias_sum[LAYERS * local : 2 * LAYERS * local]
    grad_bias = jnp.stack([queries.reshape(LAYERS, local), values.reshape(LAYERS, local)], axis=1)
    grad_up_bias = bias_sum[2 * LAYERS * local :].reshape(LAYERS, hidden)

    return (
        block_output,
        grad_tokens,
        grad_qkv,
        grad_out,
        grad_up,
        grad_down,
        grad_bias,
        grad_up_bias,
        grad_gains,
        grad_shifts,
    )


def solution(mesh):
    placed = (
        P(("fsdp", "ctx"), None),
        P(("fsdp", "ctx"), None),
        P("fsdp", None),
        P("fsdp", None),
        P(None, ("fsdp", "ctx"), None, "tp"),
        P(None, ("fsdp", "ctx"), "tp"),
        P(None, ("fsdp", "ctx"), "tp"),
        P(None, ("fsdp", "ctx"), "tp"),
        P(None, None, "tp"),
        P(None, "tp"),
        P(None, ("fsdp", "ctx"), None),
        P(None, ("fsdp", "ctx"), None),
    )
    return jax.shard_map(
        partial(on_device, mesh.shape["fsdp"], mesh.shape["ctx"], mesh.shape["tp"]),
        mesh=mesh,
        in_specs=placed,
        out_specs=(
            P(("fsdp", "ctx"), None),
            P(("fsdp", "ctx"), None),
            P(None, ("fsdp", "ctx"), None, "tp"),
            P(None, ("fsdp", "ctx"), "tp"),
            P(None, ("fsdp", "ctx"), "tp"),
            P(None, ("fsdp", "ctx"), "tp"),
            P(None, None, "tp"),
            P(None, "tp"),
            P(None, ("fsdp", "ctx"), None),
            P(None, ("fsdp", "ctx"), None),
        ),
        check_vma=False,
    )
```
